512 devices in a mesh: grp: 16 (over x, z_lo), dev: 32 (over y, z_hi, core).
Axes of the slice: x: 4, y: 8, z: 8 (z_hi: 2, z_lo: 4; z = z_hi * 4 + z_lo), core: 2. Of those that a mesh axis runs over, the one named last changes fastest.
Arguments:
- volume: bfloat16 [64, 128, 256], P('grp', 'dev'), may hold values from -6 to 6
- w_first: bfloat16 [3, 3, 3, 32, 32], replicated, may hold values from -0.21875 to 0.21875
- w_second: bfloat16 [3, 3, 3, 32, 32], replicated, may hold values from -0.21875 to 0.21875
- w_lift: bfloat16 [256, 512], replicated, may hold values from -0.375 to 0.375
- w_coarse: bfloat16 [3, 3, 3, 512, 512], P(None, None, None, 'dev'), may hold values from -0.0546875 to 0.0546875
- w_up: bfloat16 [512, 512], replicated, may hold values from -0.25 to 0.25
Outputs:
- mixed: bfloat16 [64, 128, 256], P('grp', 'dev')
The draws below stay inside these ranges and needn't reach their ends.
All inputs are finite; a program needn't handle non-finite values.
Results may differ from the reference program's by a relative error of at most 0.0061.
Values may be sent and summed in bfloat16 or wider, within the bound.
A program may use at most 64 MiB of HBM per device.

```python
import jax
import jax.numpy as jnp
from jax import lax

Z = 8
C = 32
CC = 512
NX = 64
NY = 128
ZC = 256


def steps_of(key, dims, shards, smallest, largest):
    gain, own = 1.0, jax.random.fold_in(key, 6)
    for dim, parts in shards:
        heights = jnp.exp(jax.random.uniform(jax.random.fold_in(own, dim), (parts,), jnp.float32, smallest / len(shards), largest / len(shards)))
        gain = gain * jnp.repeat(heights, dims[dim] // parts).reshape([-1 if axis == dim else 1 for axis in range(len(dims))])
    return gain


def scatter_about(own_key, dims, width, most, pieces=(), held_as=jnp.bfloat16):
    factor_of = steps_of(own_key, dims, pieces, -0.22, 0.18) if pieces else 1.0
    entries = jax.random.normal(own_key, dims, jnp.float32) * width * factor_of
    return jnp.minimum(jnp.maximum(entries, -most), most).astype(held_as)


def setup_inputs(seed: int = 0) -> dict:
    splits = jax.random.split(jax.random.key(seed), 7)
    return {
        "volume": scatter_about(splits[0], (NX, NY, ZC), 1.0, 6.0, ((0, 16), (1, 32))),
        "w_first": scatter_about(splits[1], (3, 3, 3, C, C), (27 * C) ** -0.5, 0.21875),
        "w_second": scatter_about(splits[2], (3, 3, 3, C, C), (27 * C) ** -0.5, 0.21875),
        "w_lift": scatter_about(splits[3], (8 * C, CC), (8 * C) ** -0.5, 0.375),
        "w_coarse": scatter_about(splits[4], (3, 3, 3, CC, CC), (27 * CC) ** -0.5, 0.0546875, ((3, 32),)),
        "w_up": scatter_about(splits[5], (CC, 16 * C), CC ** -0.5, 0.25),
    }


def convolve(field, weight):
    result = lax.conv_general_dilated(field[None], weight, (1, 1, 1), "SAME", dimension_numbers=("NDHWC", "DHWIO", "NDHWC"), precision=lax.Precision.HIGHEST)
    return result[0]


def expand(upper, half):
    grid = upper[:, :, :, half]
    grid = grid.transpose(0, 3, 1, 4, 2, 5, 6)
    return grid.reshape(NX, NY, Z, C)


def reference(volume, w_first, w_second, w_lift, w_coarse, w_up):
    field = volume.astype(jnp.float32).reshape(NX, NY, Z, C)
    first = jax.nn.gelu(convolve(field, w_first.astype(jnp.float32)), approximate=False).astype(jnp.bfloat16)
    skip = jax.nn.gelu(convolve(first.astype(jnp.float32), w_second.astype(jnp.float32)), approximate=False).astype(jnp.bfloat16)
    stacked = skip.reshape(NX // 2, 2, NY // 2, 2, Z // 2, 2, C).transpose(0, 2, 4, 1, 3, 5, 6).reshape(-1, 8 * C)
    lifted = jax.nn.gelu(jnp.dot(stacked, w_lift, preferred_element_type=jnp.float32), approximate=False).astype(jnp.bfloat16)
    lifted = lifted.reshape(NX // 2, NY // 2, Z // 2, CC)
    coarse = jax.nn.gelu(convolve(lifted.astype(jnp.float32), w_coarse.astype(jnp.float32)), approximate=False).astype(jnp.bfloat16)
    upper = jnp.dot(coarse.reshape(-1, CC), w_up, preferred_element_type=jnp.float32)
    upper = upper.reshape(NX // 2, NY // 2, Z // 2, 2, 2, 2, 2, C)
    gate = expand(upper, 0)
    value = expand(upper, 1)
    mixed = skip.astype(jnp.float32) * jax.nn.sigmoid(gate) + value
    return mixed.reshape(NX, NY, Z * C).astype(jnp.bfloat16)
```

```python
import functools

import jax
import jax.numpy as jnp
from jax import lax
from jax.experimental import pallas as pl
from jax.experimental.pallas import tpu as pltpu
from jax.sharding import PartitionSpec as P

F32 = jnp.float32
BF16 = jnp.bfloat16
MESH = pl.DeviceIdType.MESH
BANDS = [(zi, zo) for zo in range(4) for zi in range(4) if abs(zi - zo) <= 1]
GAPS = [(zi, zo) for zo in range(4) for zi in range(4) if abs(zi - zo) > 1]


def gelu(v):
    return 0.5 * v * (1.0 + lax.erf(v * 0.7071067811865476))


def dot(a, b):
    return jnp.dot(a, b, preferred_element_type=F32)


def iota(shape, dim):
    return lax.broadcasted_iota(jnp.int32, shape, dim)


def one_hot(mask):
    return jnp.where(mask, 1.0, 0.0).astype(BF16)


def band_weights(w_ref, t_ref):
    spread = one_hot((iota((32, 256), 1) & 31) == iota((32, 256), 0))
    lane_z = iota((32, 256), 1) >> 5

    def body(tap, carry):
        w0 = dot(w_ref[tap, 0], spread)
        w1 = dot(w_ref[tap, 1], spread)
        w2 = dot(w_ref[tap, 2], spread)
        for zi in range(8):
            rows = jnp.where(
                lane_z == zi,
                w1,
                jnp.where(lane_z == zi - 1, w2, jnp.where(lane_z == zi + 1, w0, 0.0)),
            )
            t_ref[tap, zi * 32 : zi * 32 + 32, :] = rows.astype(BF16)
        return carry

    lax.fori_loop(0, 9, body, 0)


def kernel(
    groups, devices,
    vol, w1, w2, wl, wc, wu,
    out,
    blocks, w1_v, w2_v, wl_v, wu_v, t1, t2, tc, wide, first, skip_p, send, recv, flat, cols, sums, parts, shares,
    load_sem, own_sem, halo_s, halo_r, wc_s, wc_r, a2a_s, a2a_r, rs_s, rs_r,
):
    g = lax.axis_index("grp")
    d = lax.axis_index("dev")
    half = devices // 2
    e = d // 2
    core = d - 2 * e
    lanes = wl.shape[1]

    barrier = pltpu.get_barrier_semaphore()

    def greet(off, carry):
        pl.semaphore_signal(
            barrier, inc=1, device_id=(g, lax.rem(d + off, devices)), device_id_type=MESH
        )
        return carry

    lax.fori_loop(1, devices, greet, 0)
    for dx in (-1, 1):
        for dy in (-1, 0, 1):
            pl.semaphore_signal(
                barrier, inc=1,
                device_id=(lax.rem(g + dx + groups, groups), lax.rem(d + dy + devices, devices)),
                device_id_type=MESH,
            )

    loads = [
        pltpu.make_async_copy(src, dst, load_sem.at[i])
        for i, (src, dst) in enumerate(
            [(w1, w1_v), (w2, w2_v), (wl, wl_v), (wu, wu_v), (vol, blocks.at[4])]
        )
    ]
    for c in loads:
        c.start()
    own = []
    for i, (zi, zo) in enumerate(BANDS):
        own.append(
            pltpu.make_async_copy(
                wc.at[:, zi - zo + 1],
                tc.at[:, zi, core, :, pl.ds(zo * lanes, lanes)],
                own_sem.at[i],
            )
        )
        own[-1].start()

    pl.semaphore_wait(barrier, devices - 1 + 6)

    halo = []
    for dx in (-1, 0, 1):
        for dy in (-1, 0, 1):
            if dx == 0 and dy == 0:
                continue
            slot = (1 - dx) * 3 + 1 - dy
            halo.append(
                pltpu.make_async_remote_copy(
                    src_ref=vol,
                    dst_ref=blocks.at[slot],
                    send_sem=halo_s.at[slot],
                    recv_sem=halo_r.at[slot],
                    device_id=(
                        lax.rem(g + dx + groups, groups),
                        lax.rem(d + dy + devices, devices),
                    ),
                    device_id_type=MESH,
                )
            )
            halo[-1].start()
    twin = []
    for i, (zi, zo) in enumerate(BANDS):
        twin.append(
            pltpu.make_async_remote_copy(
                src_ref=wc.at[:, zi - zo + 1],
                dst_ref=tc.at[:, zi, core, :, pl.ds(zo * lanes, lanes)],
                send_sem=wc_s.at[i],
                recv_sem=wc_r.at[i],
                device_id=(g, d + 1 - 2 * core),
                device_id_type=MESH,
            )
        )
        twin[-1].start()

    for zi, zo in GAPS:
        tc[:, zi, :, :, zo * lanes : zo * lanes + lanes] = jnp.zeros((9, 2, 16, lanes), BF16)
    wide[96:104] = jnp.zeros((8, 256), F32)
    first[80:88] = jnp.zeros((8, 256), F32)
    flat[0:8] = jnp.zeros((8, 128), F32)
    flat[8 + 8 * devices : 16 + 8 * devices] = jnp.zeros((8, 128), F32)
    loads[0].wait()
    band_weights(w1_v, t1)
    loads[1].wait()
    band_weights(w2_v, t2)

    row, col = iota((96, 144), 0), iota((96, 144), 1)
    slot = col >> 4
    sx = (slot >= 3).astype(jnp.int32) + (slot >= 6).astype(jnp.int32)
    sy = slot - 3 * sx
    fits = (sx * 4 + ((col >> 2) & 3) == (row >> 3)) & (sy * 4 + (col & 3) - 2 == (row & 7))
    gx, gy = g - 1 + sx, d - 1 + sy
    fits = fits & (gx >= 0) & (gx < groups) & (gy >= 0) & (gy < devices)
    place = one_hot(fits)

    for c in loads[2:]:
        c.wait()
    for c in halo:
        c.wait_recv()
    wide[0:96] = dot(place, blocks[...].reshape(144, 256))

    total = jnp.zeros((80, 256), F32)
    for tap in range(9):
        off = (tap // 3) * 8 + tap % 3
        total += dot(wide[off : off + 80].astype(BF16), t1[tap])
    rows = iota((80, 256), 0)
    fx, fy = 4 * g - 3 + (rows >> 3), 4 * d - 1 + (rows & 7)
    inside = (fx >= 0) & (fx < 4 * groups) & (fy >= 0) & (fy < 4 * devices)
    act = gelu(total).astype(BF16).astype(F32)
    first[0:80] = jnp.where(inside, act, 0.0)

    total = jnp.zeros((64, 256), F32)
    for tap in range(9):
        off = (tap // 3) * 8 + tap % 3
        total += dot(first[off : off + 64].astype(BF16), t2[tap])
    skip = gelu(total).astype(BF16)

    row, col = iota((32, 64), 0), iota((32, 64), 1)
    ci = (row >> 1) & 3
    fits = (2 * ci + (row >> 4) == (col >> 3)) & (2 * (row & 1) + ((row >> 3) & 1) == (col & 7))
    cx = 2 * g - 1 + ci
    fits = fits & (cx >= 0) & (cx < 2 * groups)
    moved = dot(one_hot(fits), skip)
    skip_p[...] = moved
    stacked = jnp.concatenate(
        [
            jnp.concatenate(
                [moved[ab * 8 : ab * 8 + 8, k * 64 : k * 64 + 64] for ab in range(4)], axis=1
            )
            for k in range(4)
        ],
        axis=0,
    )
    lifted = gelu(dot(stacked.astype(BF16), wl_v[...]))
    for t in range(half):
        send[t] = jnp.concatenate(
            [lifted[k * 8 : k * 8 + 8, t * 32 : t * 32 + 32] for k in range(4)], axis=1
        ).astype(BF16)

    def spread_copy(off):
        to = lax.rem(d + off, devices)
        frm = lax.rem(d + devices - off, devices)
        return to, frm

    def spread_start(off, carry):
        to = lax.rem(d + off, devices)
        pltpu.make_async_remote_copy(
            src_ref=send.at[to // 2],
            dst_ref=recv.at[d],
            send_sem=a2a_s.at[to],
            recv_sem=a2a_r.at[d],
            device_id=(g, to),
            device_id_type=MESH,
        ).start()
        return carry

    lax.fori_loop(1, devices, spread_start, 0)
    recv[d] = send[e]
    for c in own:
        c.wait()
    for c in twin:
        c.wait_recv()

    def spread_wait(off, carry):
        frm = lax.rem(d + off, devices)
        pltpu.make_async_remote_copy(
            src_ref=send.at[frm // 2],
            dst_ref=recv.at[frm],
            send_sem=a2a_s.at[frm],
            recv_sem=a2a_r.at[frm],
            device_id=(g, frm),
            device_id_type=MESH,
        ).wait_recv()
        return carry

    lax.fori_loop(1, devices, spread_wait, 0)

    flat[8 : 8 + 8 * devices] = recv[...].astype(F32).reshape(8 * devices, 128)
    for xx in range(4):
        for yb in range(4):
            ds, y = ((-1, 1), (0, 0), (0, 1), (1, 0))[yb]
            piece = flat[pl.ds(8 + 8 * core + 8 * ds + 2 * xx + y, half, stride=16), :].astype(BF16)
            for a in range(3):
                for b in range(3):
                    x, yy = xx - a, yb - b
                    if 0 <= x < 2 and 0 <= yy < 2:
                        at, tap = (2 * x + yy) * half, 3 * a + b
                        cols[at : at + half, tap * 128 : tap * 128 + 128] = piece

    lhs = cols[...]
    for z in range(4):
        got = dot(lhs, tc[:, :, :, :, z * lanes : z * lanes + lanes].reshape(1152, lanes))
        for q in range(4):
            for lt in range(lanes // 128):
                sums[lt, pl.ds(4 * z + q, half, stride=16), :] = got[
                    q * half : q * half + half, lt * 128 : lt * 128 + 128
                ]
    for lt in range(lanes // 128):
        parts[:, :, lt * 128 : lt * 128 + 128] = sums[lt].reshape(half, 16, 128).astype(BF16)

    def share_start(off, carry):
        to = lax.rem(e + off, half)
        pltpu.make_async_remote_copy(
            src_ref=parts.at[to],
            dst_ref=shares.at[e],
            send_sem=rs_s.at[to],
            recv_sem=rs_r.at[e],
            device_id=(g, 2 * to + core),
            device_id_type=MESH,
        ).start()
        return carry

    lax.fori_loop(1, half, share_start, 0)
    shares[e] = parts[e]

    def share_copy(off):
        frm = lax.rem(e + off, half)
        return pltpu.make_async_remote_copy(
            src_ref=parts.at[frm],
            dst_ref=shares.at[frm],
            send_sem=rs_s.at[frm],
            recv_sem=rs_r.at[frm],
            device_id=(g, 2 * frm + core),
            device_id_type=MESH,
        )

    def share_wait(off, carry):
        share_copy(off).wait_recv()
        return carry

    lax.fori_loop(1, half, share_wait, 0)
    total = shares[0].astype(F32)
    for t in range(1, half):
        total += shares[t].astype(F32)

    coarse = gelu(total).astype(BF16)
    upper = dot(coarse, wu_v[...])

    def expand(base):
        return jnp.concatenate(
            [
                jnp.concatenate(
                    [
                        upper[4 * k : 4 * k + 4, base + ab * 64 : base + ab * 64 + 64]
                        for k in range(4)
                    ],
                    axis=1,
                )
                for ab in range(4)
            ],
            axis=0,
        )

    gate, value = expand(0), expand(256)
    mine = jnp.concatenate([skip_p[ab * 8 + 2 : ab * 8 + 6] for ab in range(4)], axis=0)
    mixed = (mine * jax.nn.sigmoid(gate) + value).astype(BF16)
    row, col = iota((16, 16), 0), iota((16, 16), 1)
    fits = ((row >> 2) == 2 * ((col >> 1) & 1) + (col >> 3)) & (
        (row & 3) == 2 * (col & 1) + ((col >> 2) & 1)
    )
    out[...] = dot(one_hot(fits), mixed).astype(BF16)

    for c in halo:
        c.wait_send()
    for c in twin:
        c.wait_send()

    def spread_sent(off, carry):
        to = lax.rem(d + off, devices)
        pltpu.make_async_remote_copy(
            src_ref=send.at[to // 2],
            dst_ref=recv.at[d],
            send_sem=a2a_s.at[to],
            recv_sem=a2a_r.at[d],
            device_id=(g, to),
            device_id_type=MESH,
        ).wait_send()
        return carry

    lax.fori_loop(1, devices, spread_sent, 0)

    def share_sent(off, carry):
        share_copy(off).wait_send()
        return carry

    lax.fori_loop(1, half, share_sent, 0)


def on_device(groups, devices, volume, w_first, w_second, w_lift, w_coarse, w_up):
    half = devices // 2
    wide = w_up.shape[0]
    anywhere = pl.BlockSpec(memory_space=pl.ANY)
    dma = pltpu.SemaphoreType.DMA
    result = pl.pallas_call(
        functools.partial(kernel, groups, devices),
        out_shape=jax.ShapeDtypeStruct((16, 256), BF16),
        in_specs=[anywhere] * 6,
        out_specs=pl.BlockSpec(memory_space=pltpu.VMEM),
        scratch_shapes=[
            pltpu.VMEM((9, 16, 256), BF16),
            pltpu.VMEM((9, 3, 32, 32), BF16),
            pltpu.VMEM((9, 3, 32, 32), BF16),
            pltpu.VMEM((256, wide), BF16),
            pltpu.VMEM((wide, 512), BF16),
            pltpu.VMEM((9, 256, 256), BF16),
            pltpu.VMEM((9, 256, 256), BF16),
            pltpu.VMEM((9, 4, 2, 16, 4 * wide), BF16),
            pltpu.VMEM((104, 256), F32),
            pltpu.VMEM((88, 256), F32),
            pltpu.VMEM((32, 256), F32),
            pltpu.VMEM((half, 8, 128), BF16),
            pltpu.VMEM((devices, 8, 128), BF16),
            pltpu.VMEM((8 * devices + 16, 128), F32),
            pltpu.VMEM((4 * half, 1152), BF16),
            pltpu.VMEM((wide // 128, 16 * half, 128), F32),
            pltpu.VMEM((half, 16, wide), BF16),
            pltpu.VMEM((half, 16, wide), BF16),
            dma((5,)),
            dma((10,)),
            dma((9,)),
            dma((9,)),
            dma((10,)),
            dma((10,)),
            dma((devices,)),
            dma((devices,)),
            dma((half,)),
            dma((half,)),
        ],
        compiler_params=pltpu.CompilerParams(
            collective_id=0, has_side_effects=True, vmem_limit_bytes=48 * 1024 * 1024
        ),
    )(
        volume.reshape(16, 256),
        w_first.reshape(9, 3, 32, 32),
        w_second.reshape(9, 3, 32, 32),
        w_lift,
        w_coarse.reshape(9, 3, 16, wide),
        w_up,
    )
    return result.reshape(4, 4, 256)


def solution(mesh):
    return jax.shard_map(
        functools.partial(on_device, mesh.shape["grp"], mesh.shape["dev"]),
        mesh=mesh,
        in_specs=(P("grp", "dev", None), P(), P(), P(), P(None, None, None, "dev", None), P()),
        out_specs=P("grp", "dev", None),
        check_vma=False,
    )
```

```python
import functools

import jax
import jax.numpy as jnp
from jax import lax
from jax.experimental import pallas as pl
from jax.experimental.pallas import tpu as pltpu
from jax.sharding import PartitionSpec as P

F32 = jnp.float32
BF16 = jnp.bfloat16
MESH = pl.DeviceIdType.MESH
BANDS = [(zi, zo) for zo in range(4) for zi in range(4) if abs(zi - zo) <= 1]
GAPS = [(zi, zo) for zo in range(4) for zi in range(4) if abs(zi - zo) > 1]


def gelu(v):
    return 0.5 * v * (1.0 + lax.erf(v * 0.7071067811865476))


def dot(a, b):
    return jnp.dot(a, b, preferred_element_type=F32)


def iota(shape, dim):
    return lax.broadcasted_iota(jnp.int32, shape, dim)


def one_hot(mask):
    return jnp.where(mask, 1.0, 0.0).astype(BF16)


def band_weights(w_ref, t_ref):
    spread = one_hot((iota((32, 256), 1) & 31) == iota((32, 256), 0))
    lane_z = iota((32, 256), 1) >> 5

    def body(tap, carry):
        w0 = dot(w_ref[tap, 0], spread)
        w1 = dot(w_ref[tap, 1], spread)
        w2 = dot(w_ref[tap, 2], spread)
        for zi in range(8):
            rows = jnp.where(
                lane_z == zi,
                w1,
                jnp.where(lane_z == zi - 1, w2, jnp.where(lane_z == zi + 1, w0, 0.0)),
            )
            t_ref[tap, zi * 32 : zi * 32 + 32, :] = rows.astype(BF16)
        return carry

    lax.fori_loop(0, 9, body, 0)


def kernel(
    groups, devices,
    vol, w1, w2, wl, wc, wu,
    out,
    blocks, w1_v, w2_v, wl_v, wu_v, t1, t2, tc, wide, first, skip_p, send, recv, flat, cols, sums, parts, shares,
    load_sem, own_sem, halo_s, halo_r, wc_s, wc_r, a2a_s, a2a_r, rs_s, rs_r,
):
    g = lax.axis_index("grp")
    d = lax.axis_index("dev")
    half, ring = devices // 2, devices // 4
    e = d // 2
    core = d - 2 * e
    lanes = wl.shape[1]

    barrier = pltpu.get_barrier_semaphore()

    y, zh = e // 2, e - 2 * (e // 2)

    def member(dy, other_zh, other_core):
        to_y = lax.rem(y + dy + ring, ring)
        to_zh = 1 - zh if other_zh else zh
        to_core = 1 - core if other_core else core
        return (to_y * 2 + to_zh) * 2 + to_core

    steps = [ring // 2]
    for k in range(ring // 2 - 1, 0, -1):
        steps += [k, -k]
    members = [(k, a, b) for k in steps + [0] for a in (1, 0) for b in (0, 1)][:-2] + [(0, 0, 1)]

    def neighbour(dx, dy):
        return lax.rem(g + dx + groups, groups), lax.rem(d + dy + devices, devices)

    beside = [(dx, dy) for dx in (-1, 1) for dy in (-1, 1, 0)]
    for dx, dy in beside:
        pl.semaphore_signal(barrier, inc=1, device_id=neighbour(dx, dy), device_id_type=MESH)
    for m in members:
        pl.semaphore_signal(barrier, inc=1, device_id=(g, member(*m)), device_id_type=MESH)

    loads = [
        pltpu.make_async_copy(src, dst, load_sem.at[i])
        for i, (src, dst) in enumerate(
            [(w1, w1_v), (w2, w2_v), (wl, wl_v), (wu, wu_v), (vol, blocks.at[4])]
        )
    ]
    for c in loads:
        c.start()
    own = []
    for i, (zi, zo) in enumerate(BANDS):
        own.append(
            pltpu.make_async_copy(
                wc.at[:, zi - zo + 1],
                tc.at[:, zi, core, :, pl.ds(zo * lanes, lanes)],
                own_sem.at[i],
            )
        )
        own[-1].start()

    pl.semaphore_wait(barrier, devices - 1 + 6)

    halo = []
    for dx, dy in [(0, -1), (0, 1)] + beside:
        slot = (1 - dx) * 3 + 1 - dy
        halo.append(
            pltpu.make_async_remote_copy(
                src_ref=vol,
                dst_ref=blocks.at[slot],
                send_sem=halo_s.at[slot],
                recv_sem=halo_r.at[slot],
                device_id=neighbour(dx, dy),
                device_id_type=MESH,
            )
        )
        halo[-1].start()
    twin = []
    for i, (zi, zo) in enumerate(BANDS):
        twin.append(
            pltpu.make_async_remote_copy(
                src_ref=wc.at[:, zi - zo + 1],
                dst_ref=tc.at[:, zi, core, :, pl.ds(zo * lanes, lanes)],
                send_sem=wc_s.at[i],
                recv_sem=wc_r.at[i],
                device_id=(g, d + 1 - 2 * core),
                device_id_type=MESH,
            )
        )
        twin[-1].start()

    for zi, zo in GAPS:
        tc[:, zi, :, :, zo * lanes : zo * lanes + lanes] = jnp.zeros((9, 2, 16, lanes), BF16)
    wide[96:104] = jnp.zeros((8, 256), F32)
    first[80:88] = jnp.zeros((8, 256), F32)
    flat[0:8] = jnp.zeros((8, 128), F32)
    flat[8 + 8 * devices : 16 + 8 * devices] = jnp.zeros((8, 128), F32)
    loads[0].wait()
    band_weights(w1_v, t1)
    loads[1].wait()
    band_weights(w2_v, t2)

    row, col = iota((96, 144), 0), iota((96, 144), 1)
    slot = col >> 4
    sx = (slot >= 3).astype(jnp.int32) + (slot >= 6).astype(jnp.int32)
    sy = slot - 3 * sx
    fits = (sx * 4 + ((col >> 2) & 3) == (row >> 3)) & (sy * 4 + (col & 3) - 2 == (row & 7))
    gx, gy = g - 1 + sx, d - 1 + sy
    fits = fits & (gx >= 0) & (gx < groups) & (gy >= 0) & (gy < devices)
    place = one_hot(fits)

    for c in loads[2:]:
        c.wait()
    for c in halo:
        c.wait_recv()
    wide[0:96] = dot(place, blocks[...].reshape(144, 256))

    total = jnp.zeros((80, 256), F32)
    for tap in range(9):
        off = (tap // 3) * 8 + tap % 3
        total += dot(wide[off : off + 80].astype(BF16), t1[tap])
    rows = iota((80, 256), 0)
    fx, fy = 4 * g - 3 + (rows >> 3), 4 * d - 1 + (rows & 7)
    inside = (fx >= 0) & (fx < 4 * groups) & (fy >= 0) & (fy < 4 * devices)
    act = gelu(total).astype(BF16).astype(F32)
    first[0:80] = jnp.where(inside, act, 0.0)

    total = jnp.zeros((64, 256), F32)
    for tap in range(9):
        off = (tap // 3) * 8 + tap % 3
        total += dot(first[off : off + 64].astype(BF16), t2[tap])
    skip = gelu(total).astype(BF16)

    row, col = iota((32, 64), 0), iota((32, 64), 1)
    ci = (row >> 1) & 3
    fits = (2 * ci + (row >> 4) == (col >> 3)) & (2 * (row & 1) + ((row >> 3) & 1) == (col & 7))
    cx = 2 * g - 1 + ci
    fits = fits & (cx >= 0) & (cx < 2 * groups)
    moved = dot(one_hot(fits), skip)
    skip_p[...] = moved
    stacked = jnp.concatenate(
        [
            jnp.concatenate(
                [moved[ab * 8 : ab * 8 + 8, k * 64 : k * 64 + 64] for ab in range(4)], axis=1
            )
            for k in range(4)
        ],
        axis=0,
    )
    lifted = gelu(dot(stacked.astype(BF16), wl_v[...]))
    for t in range(half):
        send[t] = jnp.concatenate(
            [lifted[k * 8 : k * 8 + 8, t * 32 : t * 32 + 32] for k in range(4)], axis=1
        ).astype(BF16)

    def spread(m):
        to = member(*m)
        return pltpu.make_async_remote_copy(
            src_ref=send.at[to // 2],
            dst_ref=recv.at[d],
            send_sem=a2a_s.at[to],
            recv_sem=a2a_r.at[d],
            device_id=(g, to),
            device_id_type=MESH,
        )

    for m in members:
        spread(m).start()
    recv[d] = send[e]
    for c in own:
        c.wait()
    for c in twin:
        c.wait_recv()

    def spread_wait(off, carry):
        frm = lax.rem(d + off, devices)
        pltpu.make_async_remote_copy(
            src_ref=send.at[frm // 2],
            dst_ref=recv.at[frm],
            send_sem=a2a_s.at[frm],
            recv_sem=a2a_r.at[frm],
            device_id=(g, frm),
            device_id_type=MESH,
        ).wait_recv()
        return carry

    lax.fori_loop(1, devices, spread_wait, 0)

    flat[8 : 8 + 8 * devices] = recv[...].astype(F32).reshape(8 * devices, 128)
    for xx in range(4):
        for yb in range(4):
            ds, ly = ((-1, 1), (0, 0), (0, 1), (1, 0))[yb]
            piece = flat[pl.ds(8 + 8 * core + 8 * ds + 2 * xx + ly, half, stride=16), :].astype(BF16)
            for a in range(3):
                for b in range(3):
                    x, yy = xx - a, yb - b
                    if 0 <= x < 2 and 0 <= yy < 2:
                        at, tap = (2 * x + yy) * half, 3 * a + b
                        cols[at : at + half, tap * 128 : tap * 128 + 128] = piece

    lhs = cols[...]
    for z in range(4):
        got = dot(lhs, tc[:, :, :, :, z * lanes : z * lanes + lanes].reshape(1152, lanes))
        for q in range(4):
            for lt in range(lanes // 128):
                sums[lt, pl.ds(4 * z + q, half, stride=16), :] = got[
                    q * half : q * half + half, lt * 128 : lt * 128 + 128
                ]
    for lt in range(lanes // 128):
        parts[:, :, lt * 128 : lt * 128 + 128] = sums[lt].reshape(half, 16, 128).astype(BF16)

    def share(to):
        return pltpu.make_async_remote_copy(
            src_ref=parts.at[to],
            dst_ref=shares.at[e],
            send_sem=rs_s.at[to],
            recv_sem=rs_r.at[e],
            device_id=(g, 2 * to + core),
            device_id_type=MESH,
        )

    owners = [2 * lax.rem(y + k + ring, ring) for k in steps]
    owners = owners + [2 * y + 1 - zh] + [to + 1 for to in owners]
    for to in owners:
        share(to).start()
    shares[e] = parts[e]

    def share_copy(off):
        frm = lax.rem(e + off, half)
        return pltpu.make_async_remote_copy(
            src_ref=parts.at[frm],
            dst_ref=shares.at[frm],
            send_sem=rs_s.at[frm],
            recv_sem=rs_r.at[frm],
            device_id=(g, 2 * frm + core),
            device_id_type=MESH,
        )

    def share_wait(off, carry):
        share_copy(off).wait_recv()
        return carry

    lax.fori_loop(1, half, share_wait, 0)
    total = shares[0].astype(F32)
    for t in range(1, half):
        total += shares[t].astype(F32)

    coarse = gelu(total).astype(BF16)
    upper = dot(coarse, wu_v[...])

    def expand(base):
        return jnp.concatenate(
            [
                jnp.concatenate(
                    [
                        upper[4 * k : 4 * k + 4, base + ab * 64 : base + ab * 64 + 64]
                        for k in range(4)
                    ],
                    axis=1,
                )
                for ab in range(4)
            ],
            axis=0,
        )

    gate, value = expand(0), expand(256)
    mine = jnp.concatenate([skip_p[ab * 8 + 2 : ab * 8 + 6] for ab in range(4)], axis=0)
    mixed = (mine * jax.nn.sigmoid(gate) + value).astype(BF16)
    row, col = iota((16, 16), 0), iota((16, 16), 1)
    fits = ((row >> 2) == 2 * ((col >> 1) & 1) + (col >> 3)) & (
        (row & 3) == 2 * (col & 1) + ((col >> 2) & 1)
    )
    out[...] = dot(one_hot(fits), mixed).astype(BF16)

    for c in halo:
        c.wait_send()
    for c in twin:
        c.wait_send()

    for m in members:
        spread(m).wait_send()
    for to in owners:
        share(to).wait_send()


def on_device(groups, devices, volume, w_first, w_second, w_lift, w_coarse, w_up):
    half = devices // 2
    wide = w_up.shape[0]
    in_hbm = pl.BlockSpec(memory_space=pltpu.HBM)
    dma = pltpu.SemaphoreType.DMA
    result = pl.pallas_call(
        functools.partial(kernel, groups, devices),
        out_shape=jax.ShapeDtypeStruct((16, 256), BF16),
        in_specs=[pl.BlockSpec(memory_space=pl.ANY)] + [in_hbm] * 5,
        out_specs=pl.BlockSpec(memory_space=pltpu.VMEM),
        scratch_shapes=[
            pltpu.VMEM((9, 16, 256), BF16),
            pltpu.VMEM((9, 3, 32, 32), BF16),
            pltpu.VMEM((9, 3, 32, 32), BF16),
            pltpu.VMEM((256, wide), BF16),
            pltpu.VMEM((wide, 512), BF16),
            pltpu.VMEM((9, 256, 256), BF16),
            pltpu.VMEM((9, 256, 256), BF16),
            pltpu.VMEM((9, 4, 2, 16, 4 * wide), BF16),
            pltpu.VMEM((104, 256), F32),
            pltpu.VMEM((88, 256), F32),
            pltpu.VMEM((32, 256), F32),
            pltpu.VMEM((half, 8, 128), BF16),
            pltpu.VMEM((devices, 8, 128), BF16),
            pltpu.VMEM((8 * devices + 16, 128), F32),
            pltpu.VMEM((4 * half, 1152), BF16),
            pltpu.VMEM((wide // 128, 16 * half, 128), F32),
            pltpu.VMEM((half, 16, wide), BF16),
            pltpu.VMEM((half, 16, wide), BF16),
            dma((5,)),
            dma((10,)),
            dma((9,)),
            dma((9,)),
            dma((10,)),
            dma((10,)),
            dma((devices,)),
            dma((devices,)),
            dma((half,)),
            dma((half,)),
        ],
        compiler_params=pltpu.CompilerParams(
            collective_id=0, has_side_effects=True, vmem_limit_bytes=56 * 1024 * 1024
        ),
    )(
        volume.reshape(16, 256),
        w_first.reshape(9, 3, 32, 32),
        w_second.reshape(9, 3, 32, 32),
        w_lift,
        w_coarse.reshape(9, 3, 16, wide),
        w_up,
    )
    return result.reshape(4, 4, 256)


def solution(mesh):
    return jax.shard_map(
        functools.partial(on_device, mesh.shape["grp"], mesh.shape["dev"]),
        mesh=mesh,
        in_specs=(P("grp", "dev", None), P(), P(), P(), P(None, None, None, "dev", None), P()),
        out_specs=P("grp", "dev", None),
        check_vma=False,
    )
```

```python
import functools

import jax
import jax.numpy as jnp
from jax import lax
from jax.experimental import pallas as pl
from jax.experimental.pallas import tpu as pltpu
from jax.sharding import PartitionSpec as P

F32 = jnp.float32
BF16 = jnp.bfloat16
MESH = pl.DeviceIdType.MESH
BANDS = [(zi, zo) for zo in range(4) for zi in range(4) if abs(zi - zo) <= 1]
CHUNKS = [(0, 3), (3, 6), (6, 8), (8, 9)]
GAPS = [(zi, zo) for zo in range(4) for zi in range(4) if abs(zi - zo) > 1]


def gelu(v):
    return 0.5 * v * (1.0 + lax.erf(v * 0.7071067811865476))


def dot(a, b):
    return jnp.dot(a, b, preferred_element_type=F32)


def iota(shape, dim):
    return lax.broadcasted_iota(jnp.int32, shape, dim)


def one_hot(mask):
    return jnp.where(mask, 1.0, 0.0).astype(BF16)


def band_weights(w_ref, t_ref):
    spread = one_hot((iota((32, 256), 1) & 31) == iota((32, 256), 0))
    lane_z = iota((32, 256), 1) >> 5

    def body(tap, carry):
        w0 = dot(w_ref[tap, 0], spread)
        w1 = dot(w_ref[tap, 1], spread)
        w2 = dot(w_ref[tap, 2], spread)
        for zi in range(8):
            rows = jnp.where(
                lane_z == zi,
                w1,
                jnp.where(lane_z == zi - 1, w2, jnp.where(lane_z == zi + 1, w0, 0.0)),
            )
            t_ref[tap, zi * 32 : zi * 32 + 32, :] = rows.astype(BF16)
        return carry

    lax.fori_loop(0, 9, body, 0)


def kernel(
    groups, devices,
    vol, w1, w2, wl, wc, wu,
    out,
    blocks, w1_v, w2_v, wl_v, wu_v, t1, t2, raw, tc, wide, first, skip_p, send, recv, flat, cols, sums, parts, shares,
    load_sem, twin_sem, halo_s, halo_r, raw_s, raw_r, fwd_s, a2a_s, a2a_r, rs_s, rs_r,
):
    g = lax.axis_index("grp")
    d = lax.axis_index("dev")
    ring = devices // 4
    half = devices // 2
    lanes = wl.shape[1]
    width = lanes // 2
    tile = min(128, width)
    core = lax.rem(d, 2)
    zh = lax.rem(lax.div(d, 2), 2)
    ry = lax.div(d, 4)
    zl = lax.rem(g, 4)
    edge = (zl == 0) | (zl == 3)

    def member(dy, other_core):
        to_core = 1 - core if other_core else core
        return (lax.rem(ry + dy + ring, ring) * 2 + zh) * 2 + to_core

    def neighbour(dx, dy):
        return lax.rem(g + dx + groups, groups), lax.rem(d + dy + devices, devices)

    def across(to_core):
        return g + 3 - 2 * zl, (ry * 2 + 1 - zh) * 2 + to_core

    steps = [ring // 2]
    for k in range(ring // 2 - 1, 0, -1):
        steps += [k, -k]
    members = [(k, b) for k in steps for b in (0, 1)] + [(0, 1)]
    beside = [(dx, dy) for dx in (-1, 1) for dy in (-1, 1, 0)]
    outer = (g, lax.rem(d + 2 * core - 1 + devices, devices))

    barrier = pltpu.get_barrier_semaphore()
    partners = [outer] + [neighbour(*b) for b in beside] + [across(0), across(1)]
    partners += [(g, member(*m)) for m in members]
    for p in partners:
        pl.semaphore_signal(barrier, inc=1, device_id=p, device_id_type=MESH)

    mine = 2 * zh + core
    loads = [
        pltpu.make_async_copy(src, dst, load_sem.at[i])
        for i, (src, dst) in enumerate(
            [
                (vol, blocks.at[4]),
                (w1, w1_v),
                (w2, w2_v),
                (wl, wl_v),
                (wc.at[:, :, :, pl.ds(core * width, width)], raw.at[mine]),
                (wu, wu_v),
            ]
        )
    ]
    for c in loads:
        c.start()
    loads[0].wait()
    pl.semaphore_wait(barrier, len(partners))

    halo = []
    for dx, dy in [(0, -1), (0, 1)] + beside:
        slot = (1 - dx) * 3 + 1 - dy
        halo.append(
            pltpu.make_async_remote_copy(
                src_ref=blocks.at[4],
                dst_ref=blocks.at[slot],
                send_sem=halo_s.at[slot],
                recv_sem=halo_r.at[slot],
                device_id=neighbour(dx, dy),
                device_id_type=MESH,
            )
        )
        halo[-1].start()

    twin = pltpu.make_async_remote_copy(
        src_ref=wc.at[:, :, :, pl.ds((1 - core) * width, width)],
        dst_ref=raw.at[mine],
        send_sem=twin_sem.at[0],
        recv_sem=twin_sem.at[1],
        device_id=(g, member(0, 1)),
        device_id_type=MESH,
    )
    twin.start()

    def cross(i, to_core):
        lo, hi = CHUNKS[i]
        return pltpu.make_async_remote_copy(
            src_ref=wc.at[lo:hi, :, :, to_core * width : to_core * width + width],
            dst_ref=raw.at[mine, lo:hi],
            send_sem=raw_s.at[2 * i + to_core],
            recv_sem=raw_r.at[2 * i + core],
            device_id=across(to_core),
            device_id_type=MESH,
        )

    def inward(i, block):
        lo, hi = CHUNKS[i]
        there = 2 * (1 - zh) + block
        return pltpu.make_async_remote_copy(
            src_ref=raw.at[there, lo:hi],
            dst_ref=raw.at[there, lo:hi],
            send_sem=fwd_s.at[2 * i + block],
            recv_sem=raw_r.at[2 * i + block],
            device_id=(jnp.where(zl == 0, g + 1, g - 1), d),
            device_id_type=MESH,
        )

    @pl.when(edge)
    def _():
        for i in range(len(CHUNKS)):
            for to_core in range(2):
                cross(i, to_core).start()

    def pass_on(i):
        @pl.when(edge)
        def _():
            for block in range(2):
                inward(i, block).wait_recv()
                inward(i, block).start()

    def banded(block, lo, hi):
        for zi, zo in BANDS:
            tc[lo:hi, zi, block, :, zo * width : zo * width + width] = raw[block, lo:hi, zi - zo + 1]

    for zi, zo in GAPS:
        tc[:, zi, :, :, zo * width : zo * width + width] = jnp.zeros((9, 4, 16, width), BF16)
    wide[144:152] = jnp.zeros((8, 256), F32)
    first[120:128] = jnp.zeros((8, 256), F32)
    loads[1].wait()
    band_weights(w1_v, t1)
    loads[2].wait()
    band_weights(w2_v, t2)
    for c in loads[3:]:
        c.wait()
    banded(mine, 0, 9)

    row, col = iota((144, 144), 0), iota((144, 144), 1)
    slot = col >> 4
    sx = (slot >= 3).astype(jnp.int32) + (slot >= 6).astype(jnp.int32)
    sy = slot - 3 * sx
    fits = (sx * 4 + ((col >> 2) & 3)) * 12 + sy * 4 + (col & 3) == row
    gx, gy = g - 1 + sx, d - 1 + sy
    fits = fits & (gx >= 0) & (gx < groups) & (gy >= 0) & (gy < devices)
    place = one_hot(fits)

    pass_on(0)
    for c in halo:
        c.wait_recv()
    wide[0:144] = dot(place, blocks[...].reshape(144, 256))

    total = jnp.zeros((120, 256), F32)
    for tap in range(9):
        off = (tap // 3) * 12 + tap % 3
        total += dot(wide[off : off + 120].astype(BF16), t1[tap])
    rows = iota((120, 256), 0)
    rx = (rows * 171) >> 11
    fx, fy = 4 * g - 3 + rx, 4 * d - 3 + rows - 12 * rx
    inside = (fx >= 0) & (fx < 4 * groups) & (fy >= 0) & (fy < 4 * devices)
    act = gelu(total).astype(BF16).astype(F32)
    first[0:120] = jnp.where(inside, act, 0.0)

    total = jnp.zeros((96, 256), F32)
    for tap in range(9):
        off = (tap // 3) * 12 + tap % 3
        total += dot(first[off : off + 96].astype(BF16), t2[tap])
    skip = gelu(total).astype(BF16)

    row, col = iota((64, 96), 0), iota((64, 96), 1)
    ci, cj = (row >> 2) & 3, row & 3
    fits = (2 * ci + (row >> 5)) * 12 + 2 * cj + ((row >> 4) & 1) == col
    cx, cy = 2 * g - 1 + ci, 2 * d - 1 + cj
    fits = fits & (cx >= 0) & (cx < 2 * groups) & (cy >= 0) & (cy < 2 * devices)
    moved = dot(one_hot(fits), skip)
    skip_p[...] = moved
    stacked = jnp.concatenate(
        [
            jnp.concatenate(
                [moved[ab * 16 : ab * 16 + 16, k * 64 : k * 64 + 64] for ab in range(4)], axis=1
            )
            for k in range(4)
        ],
        axis=0,
    )
    lifted = gelu(dot(stacked.astype(BF16), wl_v[...]))
    for t in range(ring):
        send[t] = jnp.concatenate(
            [lifted[k * 16 : k * 16 + 16, t * 64 : t * 64 + 64] for k in range(4)], axis=1
        ).astype(BF16)

    me = 2 * ry + core

    def spread(m):
        to_y = lax.rem(ry + m[0] + ring, ring)
        to = 2 * to_y + (1 - core if m[1] else core)
        return pltpu.make_async_remote_copy(
            src_ref=send.at[to_y],
            dst_ref=recv.at[me],
            send_sem=a2a_s.at[to],
            recv_sem=a2a_r.at[me],
            device_id=(g, member(*m)),
            device_id_type=MESH,
        )

    for m in members:
        spread(m).start()
    recv[me] = send[ry]
    for i in range(1, len(CHUNKS)):
        pass_on(i)
    twin.wait_recv()
    banded(2 * zh + 1 - core, 0, 9)

    def arrive(off, carry):
        frm = lax.rem(me + off, half)
        pltpu.make_async_remote_copy(
            src_ref=send.at[0],
            dst_ref=recv.at[frm],
            send_sem=a2a_s.at[frm],
            recv_sem=a2a_r.at[frm],
            device_id=(g, d),
            device_id_type=MESH,
        ).wait_recv()
        return carry

    lax.fori_loop(1, half, arrive, 0)

    for lt in range(2):
        flat[lt] = recv[:, :, lt * 128 : lt * 128 + 128].astype(F32).reshape(16 * half, 128)
    for xx in range(4):
        for yb in range(4):
            for lt in range(2):
                piece = flat[lt, pl.ds(4 * xx + yb, half, stride=16), :].astype(BF16)
                for a in range(3):
                    for b in range(3):
                        ox, oy = xx - a, yb - b
                        if 0 <= ox < 2 and 0 <= oy < 2:
                            at, to = (2 * ox + oy) * half, (3 * a + b) * 256 + lt * 128
                            cols[at : at + half, to : to + 128] = piece

    @pl.when(jnp.logical_not(edge))
    def _():
        for i in range(len(CHUNKS)):
            for block in range(2):
                inward(i, block).wait_recv()

    for block in range(2):
        banded(2 * (1 - zh) + block, 0, 9)

    lhs = cols[...]
    for z in range(4):
        got = dot(lhs, tc[:, :, :, :, z * width : z * width + width].reshape(2304, width))
        for q in range(4):
            for lt in range(width // tile):
                sums[lt, pl.ds(4 * z + q, half, stride=16), :] = got[
                    q * half : q * half + half, lt * tile : lt * tile + tile
                ]
    for lt in range(width // tile):
        parts[:, :, lt * tile : lt * tile + tile] = sums[lt].reshape(half, 16, tile).astype(BF16)

    def share(m):
        to = 2 * lax.rem(ry + m[0] + ring, ring) + (1 - core if m[1] else core)
        return pltpu.make_async_remote_copy(
            src_ref=parts.at[to],
            dst_ref=shares.at[me],
            send_sem=rs_s.at[to],
            recv_sem=rs_r.at[me],
            device_id=(g, member(*m)),
            device_id_type=MESH,
        )

    for m in members:
        share(m).start()
    shares[me] = parts[me]

    def share_arrive(off, carry):
        frm = lax.rem(me + off, half)
        pltpu.make_async_remote_copy(
            src_ref=parts.at[0],
            dst_ref=shares.at[frm],
            send_sem=rs_s.at[frm],
            recv_sem=rs_r.at[frm],
            device_id=(g, d),
            device_id_type=MESH,
        ).wait_recv()
        return carry

    lax.fori_loop(1, half, share_arrive, 0)

    halves = []
    for h in range(2):
        total = shares[h].astype(F32)
        for t in range(1, ring):
            total += shares[2 * t + h].astype(F32)
        halves.append(total)
    coarse = gelu(jnp.concatenate(halves, axis=1)).astype(BF16)
    upper = dot(coarse, wu_v[...])

    def expand(base):
        return jnp.concatenate(
            [
                jnp.concatenate(
                    [
                        upper[4 * k : 4 * k + 4, base + ab * 64 : base + ab * 64 + 64]
                        for k in range(4)
                    ],
                    axis=1,
                )
                for ab in range(4)
            ],
            axis=0,
        )

    gate, value = expand(0), expand(256)
    own = jnp.concatenate(
        [skip_p[ab * 16 + 4 * i + 1 : ab * 16 + 4 * i + 3] for ab in range(4) for i in (1, 2)], axis=0
    )
    mixed = (own * jax.nn.sigmoid(gate) + value).astype(BF16)
    row, col = iota((16, 16), 0), iota((16, 16), 1)
    fits = ((row >> 2) == 2 * ((col >> 1) & 1) + (col >> 3)) & (
        (row & 3) == 2 * (col & 1) + ((col >> 2) & 1)
    )
    out[...] = dot(one_hot(fits), mixed).astype(BF16)

    for c in halo:
        c.wait_send()
    twin.wait_send()

    @pl.when(edge)
    def _():
        for i in range(len(CHUNKS)):
            for k in range(2):
                cross(i, k).wait_send()
                inward(i, k).wait_send()

    for m in members:
        spread(m).wait_send()
        share(m).wait_send()


def on_device(groups, devices, volume, w_first, w_second, w_lift, w_coarse, w_up):
    half = devices // 2
    wide = w_up.shape[0]
    tile = min(128, wide // 2)
    in_hbm = pl.BlockSpec(memory_space=pltpu.HBM)
    dma = pltpu.SemaphoreType.DMA
    result = pl.pallas_call(
        functools.partial(kernel, groups, devices),
        out_shape=jax.ShapeDtypeStruct((16, 256), BF16),
        in_specs=[pl.BlockSpec(memory_space=pl.ANY)] + [in_hbm] * 5,
        out_specs=pl.BlockSpec(memory_space=pltpu.VMEM),
        scratch_shapes=[
            pltpu.VMEM((9, 16, 256), BF16),
            pltpu.VMEM((9, 3, 32, 32), BF16),
            pltpu.VMEM((9, 3, 32, 32), BF16),
            pltpu.VMEM((256, wide), BF16),
            pltpu.VMEM((wide, 512), BF16),
            pltpu.VMEM((9, 256, 256), BF16),
            pltpu.VMEM((9, 256, 256), BF16),
            pltpu.VMEM((4, 9, 3, 16, wide // 2), BF16),
            pltpu.VMEM((9, 4, 4, 16, 2 * wide), BF16),
            pltpu.VMEM((152, 256), F32),
            pltpu.VMEM((128, 256), F32),
            pltpu.VMEM((64, 256), F32),
            pltpu.VMEM((devices // 4, 16, 256), BF16),
            pltpu.VMEM((half, 16, 256), BF16),
            pltpu.VMEM((2, 16 * half, 128), F32),
            pltpu.VMEM((4 * half, 2304), BF16),
            pltpu.VMEM((wide // 2 // tile, 16 * half, tile), F32),
            pltpu.VMEM((half, 16, wide // 2), BF16),
            pltpu.VMEM((half, 16, wide // 2), BF16),
            dma((6,)),
            dma((2,)),
            dma((9,)),
            dma((9,)),
            dma((2 * len(CHUNKS),)),
            dma((2 * len(CHUNKS),)),
            dma((2 * len(CHUNKS),)),
            dma((half,)),
            dma((half,)),
            dma((half,)),
            dma((half,)),
        ],
        compiler_params=pltpu.CompilerParams(
            collective_id=0, has_side_effects=True, vmem_limit_bytes=56 * 1024 * 1024
        ),
    )(
        volume.reshape(16, 256),
        w_first.reshape(9, 3, 32, 32),
        w_second.reshape(9, 3, 32, 32),
        w_lift,
        w_coarse.reshape(9, 3, 16, wide),
        w_up,
    )
    return result.reshape(4, 4, 256)


def solution(mesh):
    return jax.shard_map(
        functools.partial(on_device, mesh.shape["grp"], mesh.shape["dev"]),
        mesh=mesh,
        in_specs=(P("grp", "dev", None), P(), P(), P(), P(None, None, None, "dev", None), P()),
        out_specs=P("grp", "dev", None),
        check_vma=False,
    )
```

```python
import functools

import jax
import jax.numpy as jnp
from jax import lax
from jax.experimental import pallas as pl
from jax.experimental.pallas import tpu as pltpu
from jax.sharding import PartitionSpec as P

F32 = jnp.float32
BF16 = jnp.bfloat16
MESH = pl.DeviceIdType.MESH
BANDS = [(zi, zo) for zo in range(4) for zi in range(4) if abs(zi - zo) <= 1]
CHUNKS = [(0, 3), (3, 6), (6, 8), (8, 9)]
GAPS = [(zi, zo) for zo in range(4) for zi in range(4) if abs(zi - zo) > 1]


def gelu(v):
    return 0.5 * v * (1.0 + lax.erf(v * 0.7071067811865476))


def dot(a, b):
    return jnp.dot(a, b, preferred_element_type=F32)


def iota(shape, dim):
    return lax.broadcasted_iota(jnp.int32, shape, dim)


def one_hot(mask):
    return jnp.where(mask, 1.0, 0.0).astype(BF16)


def band_weights(w_ref, t_ref):
    spread = one_hot((iota((32, 256), 1) & 31) == iota((32, 256), 0))
    lane_z = iota((32, 256), 1) >> 5

    def body(tap, carry):
        w0 = dot(w_ref[tap, 0], spread)
        w1 = dot(w_ref[tap, 1], spread)
        w2 = dot(w_ref[tap, 2], spread)
        for zi in range(8):
            rows = jnp.where(
                lane_z == zi,
                w1,
                jnp.where(lane_z == zi - 1, w2, jnp.where(lane_z == zi + 1, w0, 0.0)),
            )
            t_ref[tap, zi * 32 : zi * 32 + 32, :] = rows.astype(BF16)
        return carry

    lax.fori_loop(0, 9, body, 0)


def kernel(
    groups, devices,
    vol, w1, w2, wl, wc, wu,
    out,
    block_v, blocks, w1_v, w2_v, wl_v, wu_v, t1, t2, raw, tc, wide, first, skip_p, send, recv, flat, cols, sums, parts, shares,
    load_sem, twin_sem, halo_s, halo_r, raw_s, raw_r, fwd_s, side_s, side_r, a2a_s, a2a_r, rs_s, rs_r,
):
    g = lax.axis_index("grp")
    d = lax.axis_index("dev")
    ring = devices // 4
    half = devices // 2
    lanes = wl.shape[1]
    width = lanes // 2
    tile = min(128, width)
    core = lax.rem(d, 2)
    zh = lax.rem(lax.div(d, 2), 2)
    ry = lax.div(d, 4)
    zl = lax.rem(g, 4)
    edge = (zl == 0) | (zl == 3)

    def member(dy, other_core):
        to_core = 1 - core if other_core else core
        return (lax.rem(ry + dy + ring, ring) * 2 + zh) * 2 + to_core

    def neighbour(dx, dy):
        return lax.rem(g + dx + groups, groups), lax.rem(d + dy + devices, devices)

    def across(to_core):
        return g + 3 - 2 * zl, (ry * 2 + 1 - zh) * 2 + to_core

    xp = lax.rem(lax.div(g, 4), 2)
    aside = (g + 4 - 8 * xp, d)

    steps = [ring // 2]
    for k in range(ring // 2 - 1, 0, -1):
        steps += [k, -k]
    members = [(k, b) for k in steps for b in (0, 1)] + [(0, 1)]
    beside = [(dx, dy) for dx in (-1, 1) for dy in (-1, 1, 0)]
    outer = (g, lax.rem(d + 2 * core - 1 + devices, devices))

    barrier = pltpu.get_barrier_semaphore()
    partners = [outer] + [neighbour(*b) for b in beside] + [across(0), across(1)]
    partners += [aside] + [(g, member(*m)) for m in members]
    for p in partners:
        pl.semaphore_signal(barrier, inc=1, device_id=p, device_id_type=MESH)

    mine = 2 * zh + core
    loads = [
        pltpu.make_async_copy(src, dst, load_sem.at[i])
        for i, (src, dst) in enumerate(
            [
                (vol, block_v),
                (w1, w1_v),
                (w2, w2_v),
                (wl, wl_v),
                (wc.at[:, :, :, pl.ds(core * width, width)], raw.at[mine]),
                (wu, wu_v),
            ]
        )
    ]
    for c in loads:
        c.start()
    loads[0].wait()
    blocks[4] = block_v[...].astype(F32).reshape(16, 256).astype(BF16)
    pl.semaphore_wait(barrier, len(partners))

    halo = []
    for dx, dy in [(0, -1), (0, 1)] + beside:
        slot = (1 - dx) * 3 + 1 - dy
        halo.append(
            pltpu.make_async_remote_copy(
                src_ref=blocks.at[4],
                dst_ref=blocks.at[slot],
                send_sem=halo_s.at[slot],
                recv_sem=halo_r.at[slot],
                device_id=neighbour(dx, dy),
                device_id_type=MESH,
            )
        )
        halo[-1].start()

    twin = pltpu.make_async_remote_copy(
        src_ref=wc.at[:, :, :, pl.ds((1 - core) * width, width)],
        dst_ref=raw.at[mine],
        send_sem=twin_sem.at[0],
        recv_sem=twin_sem.at[1],
        device_id=(g, member(0, 1)),
        device_id_type=MESH,
    )
    twin.start()

    part = width // 2

    def cross(i, to_core):
        lo, hi = CHUNKS[i]
        return pltpu.make_async_remote_copy(
            src_ref=wc.at[lo:hi, :, :, pl.ds(to_core * width + xp * part, part)],
            dst_ref=raw.at[mine, lo:hi, :, :, pl.ds(xp * part, part)],
            send_sem=raw_s.at[2 * i + to_core],
            recv_sem=raw_r.at[2 * i + core],
            device_id=across(to_core),
            device_id_type=MESH,
        )

    def onward(i, block, sideways):
        lo, hi = CHUNKS[i]
        there = 2 * (1 - zh) + block
        here = raw.at[there, lo:hi, :, :, pl.ds(xp * part, part)]
        return pltpu.make_async_remote_copy(
            src_ref=here,
            dst_ref=here,
            send_sem=(side_s if sideways else fwd_s).at[2 * i + block],
            recv_sem=(side_r if sideways else raw_r).at[2 * i + block],
            device_id=aside if sideways else (jnp.where(zl == 0, g + 1, g - 1), d),
            device_id_type=MESH,
        )

    @pl.when(edge)
    def _():
        for i in range(len(CHUNKS)):
            for to_core in range(2):
                cross(i, to_core).start()

    def pass_on(where, chunks):
        @pl.when(edge if where else jnp.logical_not(edge))
        def _():
            for i in chunks:
                for block in range(2):
                    onward(i, block, False).wait_recv()
                    if where:
                        onward(i, block, False).start()
                    onward(i, block, True).start()

    def banded(block, lo, hi):
        for zi, zo in BANDS:
            tc[lo:hi, zi, block, :, zo * width : zo * width + width] = raw[block, lo:hi, zi - zo + 1]

    for zi, zo in GAPS:
        tc[:, zi, :, :, zo * width : zo * width + width] = jnp.zeros((9, 4, 16, width), BF16)
    wide[144:152] = jnp.zeros((8, 256), F32)
    first[120:128] = jnp.zeros((8, 256), F32)
    loads[1].wait()
    band_weights(w1_v, t1)
    loads[2].wait()
    band_weights(w2_v, t2)
    for c in loads[3:]:
        c.wait()
    banded(mine, 0, 9)

    row, col = iota((144, 144), 0), iota((144, 144), 1)
    slot = col >> 4
    sx = (slot >= 3).astype(jnp.int32) + (slot >= 6).astype(jnp.int32)
    sy = slot - 3 * sx
    fits = (sx * 4 + ((col >> 2) & 3)) * 12 + sy * 4 + (col & 3) == row
    gx, gy = g - 1 + sx, d - 1 + sy
    fits = fits & (gx >= 0) & (gx < groups) & (gy >= 0) & (gy < devices)
    place = one_hot(fits)

    pass_on(True, [0])
    for c in halo:
        c.wait_recv()
    wide[0:144] = dot(place, blocks[...].reshape(144, 256))

    total = jnp.zeros((120, 256), F32)
    for tap in range(9):
        off = (tap // 3) * 12 + tap % 3
        total += dot(wide[off : off + 120].astype(BF16), t1[tap])
    rows = iota((120, 256), 0)
    rx = (rows * 171) >> 11
    fx, fy = 4 * g - 3 + rx, 4 * d - 3 + rows - 12 * rx
    inside = (fx >= 0) & (fx < 4 * groups) & (fy >= 0) & (fy < 4 * devices)
    act = gelu(total).astype(BF16).astype(F32)
    first[0:120] = jnp.where(inside, act, 0.0)

    pass_on(True, [1])

    total = jnp.zeros((96, 256), F32)
    for tap in range(9):
        off = (tap // 3) * 12 + tap % 3
        total += dot(first[off : off + 96].astype(BF16), t2[tap])
    skip = gelu(total).astype(BF16)

    row, col = iota((64, 96), 0), iota((64, 96), 1)
    ci, cj = (row >> 2) & 3, row & 3
    fits = (2 * ci + (row >> 5)) * 12 + 2 * cj + ((row >> 4) & 1) == col
    cx, cy = 2 * g - 1 + ci, 2 * d - 1 + cj
    fits = fits & (cx >= 0) & (cx < 2 * groups) & (cy >= 0) & (cy < 2 * devices)
    moved = dot(one_hot(fits), skip)
    skip_p[...] = moved
    stacked = jnp.concatenate(
        [
            jnp.concatenate(
                [moved[ab * 16 : ab * 16 + 16, k * 64 : k * 64 + 64] for ab in range(4)], axis=1
            )
            for k in range(4)
        ],
        axis=0,
    )
    lifted = gelu(dot(stacked.astype(BF16), wl_v[...]))
    for t in range(ring):
        send[t] = jnp.concatenate(
            [lifted[k * 16 : k * 16 + 16, t * 64 : t * 64 + 64] for k in range(4)], axis=1
        ).astype(BF16)

    me = 2 * ry + core

    def spread(m):
        to_y = lax.rem(ry + m[0] + ring, ring)
        to = 2 * to_y + (1 - core if m[1] else core)
        return pltpu.make_async_remote_copy(
            src_ref=send.at[to_y],
            dst_ref=recv.at[me],
            send_sem=a2a_s.at[to],
            recv_sem=a2a_r.at[me],
            device_id=(g, member(*m)),
            device_id_type=MESH,
        )

    for m in members:
        spread(m).start()
    recv[me] = send[ry]
    pass_on(True, range(2, len(CHUNKS)))
    pass_on(False, range(len(CHUNKS)))
    twin.wait_recv()
    banded(2 * zh + 1 - core, 0, 9)

    def arrive(off, carry):
        frm = lax.rem(me + off, half)
        pltpu.make_async_remote_copy(
            src_ref=send.at[0],
            dst_ref=recv.at[frm],
            send_sem=a2a_s.at[frm],
            recv_sem=a2a_r.at[frm],
            device_id=(g, d),
            device_id_type=MESH,
        ).wait_recv()
        return carry

    lax.fori_loop(1, half, arrive, 0)

    for lt in range(2):
        flat[lt] = recv[:, :, lt * 128 : lt * 128 + 128].astype(F32).reshape(16 * half, 128)
    for xx in range(4):
        for yb in range(4):
            for lt in range(2):
                piece = flat[lt, pl.ds(4 * xx + yb, half, stride=16), :].astype(BF16)
                for a in range(3):
                    for b in range(3):
                        ox, oy = xx - a, yb - b
                        if 0 <= ox < 2 and 0 <= oy < 2:
                            at, to = (2 * ox + oy) * half, (3 * a + b) * 256 + lt * 128
                            cols[at : at + half, to : to + 128] = piece

    for i in range(len(CHUNKS)):
        for block in range(2):
            lo, hi = CHUNKS[i]
            there = raw.at[2 * (1 - zh) + block, lo:hi, :, :, pl.ds((1 - xp) * part, part)]
            pltpu.make_async_remote_copy(
                src_ref=there,
                dst_ref=there,
                send_sem=side_s.at[2 * i + block],
                recv_sem=side_r.at[2 * i + block],
                device_id=aside,
                device_id_type=MESH,
            ).wait_recv()
    for block in range(2):
        banded(2 * (1 - zh) + block, 0, 9)

    lhs = cols[...]
    for z in range(4):
        got = dot(lhs, tc[:, :, :, :, z * width : z * width + width].reshape(2304, width))
        for q in range(4):
            for lt in range(width // tile):
                sums[lt, pl.ds(4 * z + q, half, stride=16), :] = got[
                    q * half : q * half + half, lt * tile : lt * tile + tile
                ]
    for lt in range(width // tile):
        parts[:, :, lt * tile : lt * tile + tile] = sums[lt].reshape(half, 16, tile).astype(BF16)

    def share(m):
        to = 2 * lax.rem(ry + m[0] + ring, ring) + (1 - core if m[1] else core)
        return pltpu.make_async_remote_copy(
            src_ref=parts.at[to],
            dst_ref=shares.at[me],
            send_sem=rs_s.at[to],
            recv_sem=rs_r.at[me],
            device_id=(g, member(*m)),
            device_id_type=MESH,
        )

    for m in members:
        share(m).start()
    shares[me] = parts[me]

    def share_arrive(off, carry):
        frm = lax.rem(me + off, half)
        pltpu.make_async_remote_copy(
            src_ref=parts.at[0],
            dst_ref=shares.at[frm],
            send_sem=rs_s.at[frm],
            recv_sem=rs_r.at[frm],
            device_id=(g, d),
            device_id_type=MESH,
        ).wait_recv()
        return carry

    lax.fori_loop(1, half, share_arrive, 0)

    halves = []
    for h in range(2):
        total = shares[h].astype(F32)
        for t in range(1, ring):
            total += shares[2 * t + h].astype(F32)
        halves.append(total)
    coarse = gelu(jnp.concatenate(halves, axis=1)).astype(BF16)
    upper = dot(coarse, wu_v[...])

    def expand(base):
        return jnp.concatenate(
            [
                jnp.concatenate(
                    [
                        upper[4 * k : 4 * k + 4, base + ab * 64 : base + ab * 64 + 64]
                        for k in range(4)
                    ],
                    axis=1,
                )
                for ab in range(4)
            ],
            axis=0,
        )

    gate, value = expand(0), expand(256)
    own = jnp.concatenate(
        [skip_p[ab * 16 + 4 * i + 1 : ab * 16 + 4 * i + 3] for ab in range(4) for i in (1, 2)], axis=0
    )
    mixed = (own * jax.nn.sigmoid(gate) + value).astype(BF16)
    row, col = iota((16, 16), 0), iota((16, 16), 1)
    fits = ((row >> 2) == 2 * ((col >> 1) & 1) + (col >> 3)) & (
        (row & 3) == 2 * (col & 1) + ((col >> 2) & 1)
    )
    out[...] = dot(one_hot(fits), mixed).reshape(4, 4, 256).astype(BF16)

    for c in halo:
        c.wait_send()
    twin.wait_send()

    @pl.when(edge)
    def _():
        for i in range(len(CHUNKS)):
            for k in range(2):
                cross(i, k).wait_send()
                onward(i, k, False).wait_send()

    for i in range(len(CHUNKS)):
        for k in range(2):
            onward(i, k, True).wait_send()

    for m in members:
        spread(m).wait_send()
        share(m).wait_send()


def on_device(groups, devices, volume, w_first, w_second, w_lift, w_coarse, w_up):
    half = devices // 2
    wide = w_up.shape[0]
    tile = min(128, wide // 2)
    in_hbm = pl.BlockSpec(memory_space=pltpu.HBM)
    dma = pltpu.SemaphoreType.DMA
    result = pl.pallas_call(
        functools.partial(kernel, groups, devices),
        out_shape=jax.ShapeDtypeStruct((4, 4, 256), BF16),
        in_specs=[pl.BlockSpec(memory_space=pl.ANY)] + [in_hbm] * 5,
        out_specs=pl.BlockSpec(memory_space=pltpu.VMEM),
        scratch_shapes=[
            pltpu.VMEM((4, 4, 256), BF16),
            pltpu.VMEM((9, 16, 256), BF16),
            pltpu.VMEM((9, 3, 32, 32), BF16),
            pltpu.VMEM((9, 3, 32, 32), BF16),
            pltpu.VMEM((256, wide), BF16),
            pltpu.VMEM((wide, 512), BF16),
            pltpu.VMEM((9, 256, 256), BF16),
            pltpu.VMEM((9, 256, 256), BF16),
            pltpu.VMEM((4, 9, 3, 16, wide // 2), BF16),
            pltpu.VMEM((9, 4, 4, 16, 2 * wide), BF16),
            pltpu.VMEM((152, 256), F32),
            pltpu.VMEM((128, 256), F32),
            pltpu.VMEM((64, 256), F32),
            pltpu.VMEM((devices // 4, 16, 256), BF16),
            pltpu.VMEM((half, 16, 256), BF16),
            pltpu.VMEM((2, 16 * half, 128), F32),
            pltpu.VMEM((4 * half, 2304), BF16),
            pltpu.VMEM((wide // 2 // tile, 16 * half, tile), F32),
            pltpu.VMEM((half, 16, wide // 2), BF16),
            pltpu.VMEM((half, 16, wide // 2), BF16),
            dma((6,)),
            dma((2,)),
            dma((9,)),
            dma((9,)),
            dma((2 * len(CHUNKS),)),
            dma((2 * len(CHUNKS),)),
            dma((2 * len(CHUNKS),)),
            dma((2 * len(CHUNKS),)),
            dma((2 * len(CHUNKS),)),
            dma((half,)),
            dma((half,)),
            dma((half,)),
            dma((half,)),
        ],
        compiler_params=pltpu.CompilerParams(
            collective_id=0, has_side_effects=True, vmem_limit_bytes=56 * 1024 * 1024
        ),
    )(
        volume,
        w_first.reshape(9, 3, 32, 32),
        w_second.reshape(9, 3, 32, 32),
        w_lift,
        w_coarse.reshape(9, 3, 16, wide),
        w_up,
    )
    return result


def solution(mesh):
    return jax.shard_map(
        functools.partial(on_device, mesh.shape["grp"], mesh.shape["dev"]),
        mesh=mesh,
        in_specs=(P("grp", "dev", None), P(), P(), P(), P(None, None, None, "dev", None), P()),
        out_specs=P("grp", "dev", None),
        check_vma=False,
    )
```

```python
import functools

import jax
import jax.numpy as jnp
from jax import lax
from jax.experimental import pallas as pl
from jax.experimental.pallas import tpu as pltpu
from jax.sharding import PartitionSpec as P

F32 = jnp.float32
BF16 = jnp.bfloat16
MESH = pl.DeviceIdType.MESH
BANDS = [(zi, zo) for zo in range(4) for zi in range(4) if abs(zi - zo) <= 1]
CHUNKS = [(0, 4), (4, 7), (7, 9)]
GAPS = [(zi, zo) for zo in range(4) for zi in range(4) if abs(zi - zo) > 1]


def gelu(v):
    return 0.5 * v * (1.0 + lax.erf(v * 0.7071067811865476))


def dot(a, b):
    return jnp.dot(a, b, preferred_element_type=F32)


def iota(shape, dim):
    return lax.broadcasted_iota(jnp.int32, shape, dim)


def one_hot(mask):
    return jnp.where(mask, 1.0, 0.0).astype(BF16)


def band_weights(w_ref, t_ref):
    spread = one_hot((iota((32, 256), 1) & 31) == iota((32, 256), 0))
    lane_z = iota((32, 256), 1) >> 5

    def body(tap, carry):
        w0 = dot(w_ref[tap, 0], spread)
        w1 = dot(w_ref[tap, 1], spread)
        w2 = dot(w_ref[tap, 2], spread)
        for zi in range(8):
            rows = jnp.where(
                lane_z == zi,
                w1,
                jnp.where(lane_z == zi - 1, w2, jnp.where(lane_z == zi + 1, w0, 0.0)),
            )
            t_ref[tap, zi * 32 : zi * 32 + 32, :] = rows.astype(BF16)
        return carry

    lax.fori_loop(0, 9, body, 0)


def kernel(
    groups, devices,
    vol, w1, w2, wl, wc, wu,
    out,
    block_v, blocks, w1_v, w2_v, wl_v, wu_v, t1, t2, raw, tc, wide, first, skip_p, send, recv, flat, cols, sums, parts, shares,
    load_sem, twin_sem, halo_s, halo_r, raw_s, raw_r, fwd_s, fwd_r, side_s, side_r, a2a_s, a2a_r, rs_s, rs_r,
):
    g = lax.axis_index("grp")
    d = lax.axis_index("dev")
    ring = devices // 4
    half = devices // 2
    lanes = wl.shape[1]
    width = lanes // 2
    tile = min(128, width)
    core = lax.rem(d, 2)
    zh = lax.rem(lax.div(d, 2), 2)
    ry = lax.div(d, 4)
    zl = lax.rem(g, 4)
    edge = (zl == 0) | (zl == 3)

    def member(dy, other_core):
        to_core = 1 - core if other_core else core
        return (lax.rem(ry + dy + ring, ring) * 2 + zh) * 2 + to_core

    def neighbour(dx, dy):
        return lax.rem(g + dx + groups, groups), lax.rem(d + dy + devices, devices)

    def across(to_core):
        return g + 3 - 2 * zl, (ry * 2 + 1 - zh) * 2 + to_core

    xp = lax.rem(lax.div(g, 4), 2)
    aside = (g + 4 - 8 * xp, d)

    steps = [ring // 2]
    for k in range(ring // 2 - 1, 0, -1):
        steps += [k, -k]
    members = [(k, b) for k in steps for b in (0, 1)] + [(0, 1)]
    beside = [(dx, dy) for dx in (-1, 1) for dy in (-1, 1, 0)]
    around = [(0, -1), (0, 1)] + beside

    def exists(dx, dy):
        there = (d + dy >= 0) & (d + dy < devices)
        return there & (g + dx >= 0) & (g + dx < groups)

    barrier = pltpu.get_barrier_semaphore()
    first_load = pltpu.make_async_copy(vol, block_v, load_sem.at[0])
    first_load.start()
    sibling = 1 - 2 * core
    greeted = 0
    for dx, dy in around:
        wanted = exists(dx, dy)
        if dx == 0:
            wanted = wanted & (sibling != dy)
        greeted += wanted.astype(jnp.int32)

        @pl.when(wanted)
        def _():
            pl.semaphore_signal(
                barrier, inc=1, device_id=neighbour(dx, dy), device_id_type=MESH
            )

    partners = [across(0), across(1), aside] + [(g, member(*m)) for m in members]
    for p in partners:
        pl.semaphore_signal(barrier, inc=1, device_id=p, device_id_type=MESH)

    mine = 2 * zh + core
    loads = [
        pltpu.make_async_copy(src, dst, load_sem.at[i + 1])
        for i, (src, dst) in enumerate(
            [
                (w1, w1_v),
                (w2, w2_v),
                (wl, wl_v),
                (wc.at[:, :, :, pl.ds(core * width, width)], raw.at[mine]),
                (wu, wu_v),
            ]
        )
    ]
    for c in loads:
        c.start()
    first_load.wait()
    blocks[4] = block_v[...].astype(F32).reshape(16, 256).astype(BF16)
    pl.semaphore_wait(barrier, greeted + len(partners))

    def block_copy(dx, dy, slot):
        return pltpu.make_async_remote_copy(
            src_ref=blocks.at[4],
            dst_ref=blocks.at[slot],
            send_sem=halo_s.at[slot],
            recv_sem=halo_r.at[slot],
            device_id=neighbour(dx, dy),
            device_id_type=MESH,
        )

    for dx, dy in around:

        @pl.when(exists(dx, dy))
        def _():
            block_copy(dx, dy, (1 - dx) * 3 + 1 - dy).start()

    twin = pltpu.make_async_remote_copy(
        src_ref=wc.at[:, :, :, pl.ds((1 - core) * width, width)],
        dst_ref=raw.at[mine],
        send_sem=twin_sem.at[0],
        recv_sem=twin_sem.at[1],
        device_id=(g, member(0, 1)),
        device_id_type=MESH,
    )
    twin.start()

    part = width // 2

    def cross(i, to_core):
        lo, hi = CHUNKS[i]
        return pltpu.make_async_remote_copy(
            src_ref=wc.at[lo:hi, :, :, pl.ds(to_core * width + xp * part, part)],
            dst_ref=raw.at[mine, lo:hi, :, :, pl.ds(xp * part, part)],
            send_sem=raw_s.at[2 * i + to_core],
            recv_sem=raw_r.at[2 * i + core],
            device_id=across(to_core),
            device_id_type=MESH,
        )

    foreign = 2 * (1 - zh)

    def onward(i, sideways):
        lo, hi = CHUNKS[i]
        here = raw.at[pl.ds(foreign, 2), lo:hi, :, :, pl.ds(xp * part, part)]
        return pltpu.make_async_remote_copy(
            src_ref=here,
            dst_ref=here,
            send_sem=(side_s if sideways else fwd_s).at[i],
            recv_sem=(side_r if sideways else fwd_r).at[i],
            device_id=aside if sideways else (jnp.where(zl == 0, g + 1, g - 1), d),
            device_id_type=MESH,
        )

    @pl.when(edge)
    def _():
        for i in range(len(CHUNKS)):
            for to_core in range(2):
                cross(i, to_core).start()

    def crossed(i, block):
        lo, hi = CHUNKS[i]
        there = raw.at[foreign + block, lo:hi, :, :, pl.ds(xp * part, part)]
        return pltpu.make_async_remote_copy(
            src_ref=there,
            dst_ref=there,
            send_sem=raw_s.at[2 * i + block],
            recv_sem=raw_r.at[2 * i + block],
            device_id=across(block),
            device_id_type=MESH,
        )

    def pass_on(where, chunks):
        @pl.when(edge if where else jnp.logical_not(edge))
        def _():
            for i in chunks:
                if where:
                    crossed(i, 0).wait_recv()
                    crossed(i, 1).wait_recv()
                    onward(i, False).start()
                else:
                    onward(i, False).wait_recv()
                onward(i, True).start()

    def banded(block, lo, hi):
        for zi, zo in BANDS:
            tc[lo:hi, zi, block, :, zo * width : zo * width + width] = raw[block, lo:hi, zi - zo + 1]

    for zi, zo in GAPS:
        tc[:, zi, :, :, zo * width : zo * width + width] = jnp.zeros((9, 4, 16, width), BF16)
    wide[144:152] = jnp.zeros((8, 256), F32)
    first[120:128] = jnp.zeros((8, 256), F32)
    loads[0].wait()
    band_weights(w1_v, t1)
    loads[1].wait()
    band_weights(w2_v, t2)
    for c in loads[2:]:
        c.wait()
    banded(mine, 0, 9)

    row, col = iota((144, 144), 0), iota((144, 144), 1)
    slot = col >> 4
    sx = (slot >= 3).astype(jnp.int32) + (slot >= 6).astype(jnp.int32)
    sy = slot - 3 * sx
    fits = (sx * 4 + ((col >> 2) & 3)) * 12 + sy * 4 + (col & 3) == row
    gx, gy = g - 1 + sx, d - 1 + sy
    fits = fits & (gx >= 0) & (gx < groups) & (gy >= 0) & (gy < devices)
    place = one_hot(fits)

    pass_on(True, [0])
    for dx, dy in around:
        slot = (1 + dx) * 3 + 1 + dy

        @pl.when(exists(dx, dy))
        def _():
            block_copy(dx, dy, slot).wait_recv()

        @pl.when(jnp.logical_not(exists(dx, dy)))
        def _():
            blocks[slot] = jnp.zeros((16, 256), BF16)

    wide[0:144] = dot(place, blocks[...].reshape(144, 256))

    total = jnp.zeros((120, 256), F32)
    for tap in range(9):
        off = (tap // 3) * 12 + tap % 3
        total += dot(wide[off : off + 120].astype(BF16), t1[tap])
    rows = iota((120, 256), 0)
    rx = (rows * 171) >> 11
    fx, fy = 4 * g - 3 + rx, 4 * d - 3 + rows - 12 * rx
    inside = (fx >= 0) & (fx < 4 * groups) & (fy >= 0) & (fy < 4 * devices)
    act = gelu(total).astype(BF16).astype(F32)
    first[0:120] = jnp.where(inside, act, 0.0)

    pass_on(True, [1])

    total = jnp.zeros((96, 256), F32)
    for tap in range(9):
        off = (tap // 3) * 12 + tap % 3
        total += dot(first[off : off + 96].astype(BF16), t2[tap])
    skip = gelu(total).astype(BF16)

    row, col = iota((64, 96), 0), iota((64, 96), 1)
    ci, cj = (row >> 2) & 3, row & 3
    fits = (2 * ci + (row >> 5)) * 12 + 2 * cj + ((row >> 4) & 1) == col
    cx, cy = 2 * g - 1 + ci, 2 * d - 1 + cj
    fits = fits & (cx >= 0) & (cx < 2 * groups) & (cy >= 0) & (cy < 2 * devices)
    moved = dot(one_hot(fits), skip)
    skip_p[...] = moved
    stacked = jnp.concatenate(
        [
            jnp.concatenate(
                [moved[ab * 16 : ab * 16 + 16, k * 64 : k * 64 + 64] for ab in range(4)], axis=1
            )
            for k in range(4)
        ],
        axis=0,
    )
    lifted = gelu(dot(stacked.astype(BF16), wl_v[...]))
    for t in range(ring):
        send[t] = jnp.concatenate(
            [lifted[k * 16 : k * 16 + 16, t * 64 : t * 64 + 64] for k in range(4)], axis=1
        ).astype(BF16)

    me = 2 * ry + core

    def spread(m):
        to_y = lax.rem(ry + m[0] + ring, ring)
        to = 2 * to_y + (1 - core if m[1] else core)
        return pltpu.make_async_remote_copy(
            src_ref=send.at[to_y],
            dst_ref=recv.at[me],
            send_sem=a2a_s.at[to],
            recv_sem=a2a_r.at[me],
            device_id=(g, member(*m)),
            device_id_type=MESH,
        )

    for m in members:
        spread(m).start()
    recv[me] = send[ry]
    pass_on(True, range(2, len(CHUNKS)))
    pass_on(False, range(len(CHUNKS)))
    twin.wait_recv()
    banded(2 * zh + 1 - core, 0, 9)

    def arrive(off, carry):
        frm = lax.rem(me + off, half)
        pltpu.make_async_remote_copy(
            src_ref=send.at[0],
            dst_ref=recv.at[frm],
            send_sem=a2a_s.at[frm],
            recv_sem=a2a_r.at[frm],
            device_id=(g, d),
            device_id_type=MESH,
        ).wait_recv()
        return carry

    lax.fori_loop(1, half, arrive, 0)

    for lt in range(2):
        flat[lt] = recv[:, :, lt * 128 : lt * 128 + 128].astype(F32).reshape(16 * half, 128)
    for xx in range(4):
        for yb in range(4):
            for lt in range(2):
                piece = flat[lt, pl.ds(4 * xx + yb, half, stride=16), :].astype(BF16)
                for a in range(3):
                    for b in range(3):
                        ox, oy = xx - a, yb - b
                        if 0 <= ox < 2 and 0 <= oy < 2:
                            at, to = (2 * ox + oy) * half, (3 * a + b) * 256 + lt * 128
                            cols[at : at + half, to : to + 128] = piece

    for i in range(len(CHUNKS)):
        lo, hi = CHUNKS[i]
        there = raw.at[pl.ds(foreign, 2), lo:hi, :, :, pl.ds((1 - xp) * part, part)]
        pltpu.make_async_remote_copy(
            src_ref=there,
            dst_ref=there,
            send_sem=side_s.at[i],
            recv_sem=side_r.at[i],
            device_id=aside,
            device_id_type=MESH,
        ).wait_recv()
    for block in range(2):
        banded(foreign + block, 0, 9)

    lhs = cols[...]
    for z in range(4):
        got = dot(lhs, tc[:, :, :, :, z * width : z * width + width].reshape(2304, width))
        for q in range(4):
            for lt in range(width // tile):
                sums[lt, pl.ds(4 * z + q, half, stride=16), :] = got[
                    q * half : q * half + half, lt * tile : lt * tile + tile
                ]
    for lt in range(width // tile):
        parts[:, :, lt * tile : lt * tile + tile] = sums[lt].reshape(half, 16, tile).astype(BF16)

    def share(m):
        to = 2 * lax.rem(ry + m[0] + ring, ring) + (1 - core if m[1] else core)
        return pltpu.make_async_remote_copy(
            src_ref=parts.at[to],
            dst_ref=shares.at[me],
            send_sem=rs_s.at[to],
            recv_sem=rs_r.at[me],
            device_id=(g, member(*m)),
            device_id_type=MESH,
        )

    for m in members:
        share(m).start()
    shares[me] = parts[me]

    def share_arrive(off, carry):
        frm = lax.rem(me + off, half)
        pltpu.make_async_remote_copy(
            src_ref=parts.at[0],
            dst_ref=shares.at[frm],
            send_sem=rs_s.at[frm],
            recv_sem=rs_r.at[frm],
            device_id=(g, d),
            device_id_type=MESH,
        ).wait_recv()
        return carry

    lax.fori_loop(1, half, share_arrive, 0)

    halves = []
    for h in range(2):
        total = shares[h].astype(F32)
        for t in range(1, ring):
            total += shares[2 * t + h].astype(F32)
        halves.append(total)
    coarse = gelu(jnp.concatenate(halves, axis=1)).astype(BF16)
    upper = dot(coarse, wu_v[...])

    def expand(base):
        return jnp.concatenate(
            [
                jnp.concatenate(
                    [
                        upper[4 * k : 4 * k + 4, base + ab * 64 : base + ab * 64 + 64]
                        for k in range(4)
                    ],
                    axis=1,
                )
                for ab in range(4)
            ],
            axis=0,
        )

    gate, value = expand(0), expand(256)
    own = jnp.concatenate(
        [skip_p[ab * 16 + 4 * i + 1 : ab * 16 + 4 * i + 3] for ab in range(4) for i in (1, 2)], axis=0
    )
    mixed = (own * jax.nn.sigmoid(gate) + value).astype(BF16)
    row, col = iota((16, 16), 0), iota((16, 16), 1)
    fits = ((row >> 2) == 2 * ((col >> 1) & 1) + (col >> 3)) & (
        (row & 3) == 2 * (col & 1) + ((col >> 2) & 1)
    )
    out[...] = dot(one_hot(fits), mixed).reshape(4, 4, 256).astype(BF16)

    for dx, dy in around:

        @pl.when(exists(dx, dy))
        def _():
            block_copy(dx, dy, (1 - dx) * 3 + 1 - dy).wait_send()

    twin.wait_send()

    @pl.when(edge)
    def _():
        for i in range(len(CHUNKS)):
            for k in range(2):
                cross(i, k).wait_send()
            onward(i, False).wait_send()

    for i in range(len(CHUNKS)):
        onward(i, True).wait_send()

    for m in members:
        spread(m).wait_send()
        share(m).wait_send()


def on_device(groups, devices, volume, w_first, w_second, w_lift, w_coarse, w_up):
    half = devices // 2
    wide = w_up.shape[0]
    tile = min(128, wide // 2)
    in_hbm = pl.BlockSpec(memory_space=pltpu.HBM)
    dma = pltpu.SemaphoreType.DMA
    result = pl.pallas_call(
        functools.partial(kernel, groups, devices),
        out_shape=jax.ShapeDtypeStruct((4, 4, 256), BF16),
        in_specs=[pl.BlockSpec(memory_space=pl.ANY)] + [in_hbm] * 5,
        out_specs=pl.BlockSpec(memory_space=pltpu.VMEM),
        scratch_shapes=[
            pltpu.VMEM((4, 4, 256), BF16),
            pltpu.VMEM((9, 16, 256), BF16),
            pltpu.VMEM((9, 3, 32, 32), BF16),
            pltpu.VMEM((9, 3, 32, 32), BF16),
            pltpu.VMEM((256, wide), BF16),
            pltpu.VMEM((wide, 512), BF16),
            pltpu.VMEM((9, 256, 256), BF16),
            pltpu.VMEM((9, 256, 256), BF16),
            pltpu.VMEM((4, 9, 3, 16, wide // 2), BF16),
            pltpu.VMEM((9, 4, 4, 16, 2 * wide), BF16),
            pltpu.VMEM((152, 256), F32),
            pltpu.VMEM((128, 256), F32),
            pltpu.VMEM((64, 256), F32),
            pltpu.VMEM((devices // 4, 16, 256), BF16),
            pltpu.VMEM((half, 16, 256), BF16),
            pltpu.VMEM((2, 16 * half, 128), F32),
            pltpu.VMEM((4 * half, 2304), BF16),
            pltpu.VMEM((wide // 2 // tile, 16 * half, tile), F32),
            pltpu.VMEM((half, 16, wide // 2), BF16),
            pltpu.VMEM((half, 16, wide // 2), BF16),
            dma((6,)),
            dma((2,)),
            dma((9,)),
            dma((9,)),
            dma((2 * len(CHUNKS),)),
            dma((2 * len(CHUNKS),)),
            dma((len(CHUNKS),)),
            dma((len(CHUNKS),)),
            dma((len(CHUNKS),)),
            dma((len(CHUNKS),)),
            dma((half,)),
            dma((half,)),
            dma((half,)),
            dma((half,)),
        ],
        compiler_params=pltpu.CompilerParams(
            collective_id=0, has_side_effects=True, vmem_limit_bytes=56 * 1024 * 1024
        ),
    )(
        volume,
        w_first.reshape(9, 3, 32, 32),
        w_second.reshape(9, 3, 32, 32),
        w_lift,
        w_coarse.reshape(9, 3, 16, wide),
        w_up,
    )
    return result


def solution(mesh):
    return jax.shard_map(
        functools.partial(on_device, mesh.shape["grp"], mesh.shape["dev"]),
        mesh=mesh,
        in_specs=(P("grp", "dev", None), P(), P(), P(), P(None, None, None, "dev", None), P()),
        out_specs=P("grp", "dev", None),
        check_vma=False,
    )
```

```python
import functools

import jax
import jax.numpy as jnp
from jax import lax
from jax.experimental import pallas as pl
from jax.experimental.pallas import tpu as pltpu
from jax.sharding import PartitionSpec as P

F32 = jnp.float32
BF16 = jnp.bfloat16
MESH = pl.DeviceIdType.MESH
BANDS = [(zi, zo) for zo in range(4) for zi in range(4) if abs(zi - zo) <= 1]
CHUNKS = [(0, 4), (4, 7), (7, 9)]
GAPS = [(zi, zo) for zo in range(4) for zi in range(4) if abs(zi - zo) > 1]


def gelu(v):
    return 0.5 * v * (1.0 + lax.erf(v * 0.7071067811865476))


def dot(a, b):
    return jnp.dot(a, b, preferred_element_type=F32)


def iota(shape, dim):
    return lax.broadcasted_iota(jnp.int32, shape, dim)


def one_hot(mask):
    return jnp.where(mask, 1.0, 0.0).astype(BF16)


def band_weights(w_ref, t_ref):
    spread = one_hot((iota((32, 256), 1) & 31) == iota((32, 256), 0))
    lane_z = iota((32, 256), 1) >> 5

    def body(tap, carry):
        w0 = dot(w_ref[tap, 0], spread)
        w1 = dot(w_ref[tap, 1], spread)
        w2 = dot(w_ref[tap, 2], spread)
        for zi in range(8):
            rows = jnp.where(
                lane_z == zi,
                w1,
                jnp.where(lane_z == zi - 1, w2, jnp.where(lane_z == zi + 1, w0, 0.0)),
            )
            t_ref[tap, zi * 32 : zi * 32 + 32, :] = rows.astype(BF16)
        return carry

    lax.fori_loop(0, 9, body, 0)


def kernel(
    groups, devices,
    vol, w1, w2, wl, wc, wu,
    out,
    block_v, blocks, w1_v, w2_v, wl_v, wu_v, t1, t2, wq, raw, tc, wide, first, skip_p, send, recv, flat, cols, sums, parts, shares,
    load_sem, twin_sem, halo_s, halo_r, raw_s, raw_r, fwd_s, fwd_r, side_s, side_r, a2a_s, a2a_r, rs_s, rs_r,
):
    g = lax.axis_index("grp")
    d = lax.axis_index("dev")
    ring = devices // 4
    half = devices // 2
    lanes = wl.shape[1]
    width = lanes // 2
    part = width // 2
    tile = min(128, width)
    core = lax.rem(d, 2)
    zh = lax.rem(lax.div(d, 2), 2)
    ry = lax.div(d, 4)
    zl = lax.rem(g, 4)
    edge = (zl == 0) | (zl == 3)

    def member(dy, other_core):
        to_core = 1 - core if other_core else core
        return (lax.rem(ry + dy + ring, ring) * 2 + zh) * 2 + to_core

    def neighbour(dx, dy):
        return lax.rem(g + dx + groups, groups), lax.rem(d + dy + devices, devices)

    def across(to_core):
        return g + 3 - 2 * zl, (ry * 2 + 1 - zh) * 2 + to_core

    xp = lax.rem(lax.div(g, 4), 2)
    aside = (g + 4 - 8 * xp, d)

    steps = [ring // 2]
    for k in range(ring // 2 - 1, 0, -1):
        steps += [k, -k]
    members = [(k, b) for k in steps for b in (0, 1)] + [(0, 1)]
    beside = [(dx, dy) for dx in (-1, 1) for dy in (-1, 1, 0)]
    around = [(0, -1), (0, 1)] + beside

    def exists(dx, dy):
        there = (d + dy >= 0) & (d + dy < devices)
        return there & (g + dx >= 0) & (g + dx < groups)

    barrier = pltpu.get_barrier_semaphore()
    first_load = pltpu.make_async_copy(vol, block_v, load_sem.at[0])
    first_load.start()
    sibling = 1 - 2 * core
    greeted = 0
    for dx, dy in around:
        wanted = exists(dx, dy)
        if dx == 0:
            wanted = wanted & (sibling != dy)
        greeted += wanted.astype(jnp.int32)

        @pl.when(wanted)
        def _():
            pl.semaphore_signal(
                barrier, inc=1, device_id=neighbour(dx, dy), device_id_type=MESH
            )

    partners = [across(0), across(1), aside] + [(g, member(*m)) for m in members]
    for p in partners:
        pl.semaphore_signal(barrier, inc=1, device_id=p, device_id_type=MESH)

    mine = 2 * zh + core
    loads = [
        pltpu.make_async_copy(src, dst, load_sem.at[i + 1])
        for i, (src, dst) in enumerate(
            [
                (w1, w1_v),
                (w2, w2_v),
                (wl, wl_v),
                (wu, wu_v),
            ]
        )
    ]
    quarters = [
        pltpu.make_async_copy(
            wc.at[:, :, :, q * part : q * part + part], wq.at[q], load_sem.at[5 + q]
        )
        for q in range(4)
    ]
    for c in quarters + loads:
        c.start()
    first_load.wait()
    blocks[4] = block_v[...].astype(F32).reshape(16, 256).astype(BF16)
    pl.semaphore_wait(barrier, greeted + len(partners))

    def block_copy(dx, dy, slot):
        return pltpu.make_async_remote_copy(
            src_ref=blocks.at[4],
            dst_ref=blocks.at[slot],
            send_sem=halo_s.at[slot],
            recv_sem=halo_r.at[slot],
            device_id=neighbour(dx, dy),
            device_id_type=MESH,
        )

    for dx, dy in around:

        @pl.when(exists(dx, dy))
        def _():
            block_copy(dx, dy, (1 - dx) * 3 + 1 - dy).start()

    for c in quarters:
        c.wait()
    twin = pltpu.make_async_remote_copy(
        src_ref=wq.at[pl.ds(2 - 2 * core, 2)],
        dst_ref=raw.at[mine],
        send_sem=twin_sem.at[0],
        recv_sem=twin_sem.at[1],
        device_id=(g, member(0, 1)),
        device_id_type=MESH,
    )
    twin.start()

    def cross(i, to_core):
        lo, hi = CHUNKS[i]
        return pltpu.make_async_remote_copy(
            src_ref=wq.at[2 * to_core + xp, lo:hi],
            dst_ref=raw.at[mine, xp, lo:hi],
            send_sem=raw_s.at[2 * i + to_core],
            recv_sem=raw_r.at[2 * i + core],
            device_id=across(to_core),
            device_id_type=MESH,
        )

    foreign = 2 * (1 - zh)

    def onward(i, sideways):
        lo, hi = CHUNKS[i]
        here = raw.at[pl.ds(foreign, 2), xp, lo:hi]
        return pltpu.make_async_remote_copy(
            src_ref=here,
            dst_ref=here,
            send_sem=(side_s if sideways else fwd_s).at[i],
            recv_sem=(side_r if sideways else fwd_r).at[i],
            device_id=aside if sideways else (jnp.where(zl == 0, g + 1, g - 1), d),
            device_id_type=MESH,
        )

    @pl.when(edge)
    def _():
        for i in range(len(CHUNKS)):
            for to_core in range(2):
                cross(i, to_core).start()

    def crossed(i, block):
        lo, hi = CHUNKS[i]
        there = raw.at[foreign + block, xp, lo:hi]
        return pltpu.make_async_remote_copy(
            src_ref=there,
            dst_ref=there,
            send_sem=raw_s.at[2 * i + block],
            recv_sem=raw_r.at[2 * i + block],
            device_id=across(block),
            device_id_type=MESH,
        )

    def pass_on(where, chunks):
        @pl.when(edge if where else jnp.logical_not(edge))
        def _():
            for i in chunks:
                if where:
                    crossed(i, 0).wait_recv()
                    crossed(i, 1).wait_recv()
                    onward(i, False).start()
                else:
                    onward(i, False).wait_recv()
                onward(i, True).start()

    def banded(block, source):
        for h in range(2):
            for zi, zo in BANDS:
                at = zo * width + h * part
                tc[:, zi, block, :, at : at + part] = source[h][:, zi - zo + 1]

    for zi, zo in GAPS:
        tc[:, zi, :, :, zo * width : zo * width + width] = jnp.zeros((9, 4, 16, width), BF16)
    wide[144:152] = jnp.zeros((8, 256), F32)
    first[120:128] = jnp.zeros((8, 256), F32)
    loads[0].wait()
    band_weights(w1_v, t1)
    loads[1].wait()
    band_weights(w2_v, t2)
    for c in loads[2:]:
        c.wait()
    banded(mine, [wq.at[2 * core + h] for h in range(2)])

    row, col = iota((144, 144), 0), iota((144, 144), 1)
    slot = col >> 4
    sx = (slot >= 3).astype(jnp.int32) + (slot >= 6).astype(jnp.int32)
    sy = slot - 3 * sx
    fits = (sx * 4 + ((col >> 2) & 3)) * 12 + sy * 4 + (col & 3) == row
    gx, gy = g - 1 + sx, d - 1 + sy
    fits = fits & (gx >= 0) & (gx < groups) & (gy >= 0) & (gy < devices)
    place = one_hot(fits)

    pass_on(True, [0])
    for dx, dy in around:
        slot = (1 + dx) * 3 + 1 + dy

        @pl.when(exists(dx, dy))
        def _():
            block_copy(dx, dy, slot).wait_recv()

        @pl.when(jnp.logical_not(exists(dx, dy)))
        def _():
            blocks[slot] = jnp.zeros((16, 256), BF16)

    wide[0:144] = dot(place, blocks[...].reshape(144, 256))

    total = jnp.zeros((120, 256), F32)
    for tap in range(9):
        off = (tap // 3) * 12 + tap % 3
        total += dot(wide[off : off + 120].astype(BF16), t1[tap])
    rows = iota((120, 256), 0)
    rx = (rows * 171) >> 11
    fx, fy = 4 * g - 3 + rx, 4 * d - 3 + rows - 12 * rx
    inside = (fx >= 0) & (fx < 4 * groups) & (fy >= 0) & (fy < 4 * devices)
    act = gelu(total).astype(BF16).astype(F32)
    first[0:120] = jnp.where(inside, act, 0.0)

    pass_on(True, [1])

    total = jnp.zeros((96, 256), F32)
    for tap in range(9):
        off = (tap // 3) * 12 + tap % 3
        total += dot(first[off : off + 96].astype(BF16), t2[tap])
    skip = gelu(total).astype(BF16)

    row, col = iota((64, 96), 0), iota((64, 96), 1)
    ci, cj = (row >> 2) & 3, row & 3
    fits = (2 * ci + (row >> 5)) * 12 + 2 * cj + ((row >> 4) & 1) == col
    cx, cy = 2 * g - 1 + ci, 2 * d - 1 + cj
    fits = fits & (cx >= 0) & (cx < 2 * groups) & (cy >= 0) & (cy < 2 * devices)
    moved = dot(one_hot(fits), skip)
    skip_p[...] = moved
    stacked = jnp.concatenate(
        [
            jnp.concatenate(
                [moved[ab * 16 : ab * 16 + 16, k * 64 : k * 64 + 64] for ab in range(4)], axis=1
            )
            for k in range(4)
        ],
        axis=0,
    )
    lifted = gelu(dot(stacked.astype(BF16), wl_v[...]))
    for t in range(ring):
        send[t] = jnp.concatenate(
            [lifted[k * 16 : k * 16 + 16, t * 64 : t * 64 + 64] for k in range(4)], axis=1
        ).astype(BF16)

    me = 2 * ry + core

    def spread(m):
        to_y = lax.rem(ry + m[0] + ring, ring)
        to = 2 * to_y + (1 - core if m[1] else core)
        return pltpu.make_async_remote_copy(
            src_ref=send.at[to_y],
            dst_ref=recv.at[me],
            send_sem=a2a_s.at[to],
            recv_sem=a2a_r.at[me],
            device_id=(g, member(*m)),
            device_id_type=MESH,
        )

    for m in members:
        spread(m).start()
    recv[me] = send[ry]
    pass_on(True, range(2, len(CHUNKS)))
    pass_on(False, range(len(CHUNKS)))
    twin.wait_recv()
    banded(2 * zh + 1 - core, [raw.at[2 * zh + 1 - core, h] for h in range(2)])

    def arrive(off, carry):
        frm = lax.rem(me + off, half)
        pltpu.make_async_remote_copy(
            src_ref=send.at[0],
            dst_ref=recv.at[frm],
            send_sem=a2a_s.at[frm],
            recv_sem=a2a_r.at[frm],
            device_id=(g, d),
            device_id_type=MESH,
        ).wait_recv()
        return carry

    lax.fori_loop(1, half, arrive, 0)

    for lt in range(2):
        flat[lt] = recv[:, :, lt * 128 : lt * 128 + 128].astype(F32).reshape(16 * half, 128)
    for xx in range(4):
        for yb in range(4):
            for lt in range(2):
                piece = flat[lt, pl.ds(4 * xx + yb, half, stride=16), :].astype(BF16)
                for a in range(3):
                    for b in range(3):
                        ox, oy = xx - a, yb - b
                        if 0 <= ox < 2 and 0 <= oy < 2:
                            at, to = (2 * ox + oy) * half, (3 * a + b) * 256 + lt * 128
                            cols[at : at + half, to : to + 128] = piece

    for i in range(len(CHUNKS)):
        lo, hi = CHUNKS[i]
        there = raw.at[pl.ds(foreign, 2), 1 - xp, lo:hi]
        pltpu.make_async_remote_copy(
            src_ref=there,
            dst_ref=there,
            send_sem=side_s.at[i],
            recv_sem=side_r.at[i],
            device_id=aside,
            device_id_type=MESH,
        ).wait_recv()
    for block in range(2):
        banded(foreign + block, [raw.at[foreign + block, h] for h in range(2)])

    lhs = cols[...]
    for z in range(4):
        got = dot(lhs, tc[:, :, :, :, z * width : z * width + width].reshape(2304, width))
        for q in range(4):
            for lt in range(width // tile):
                sums[lt, pl.ds(4 * z + q, half, stride=16), :] = got[
                    q * half : q * half + half, lt * tile : lt * tile + tile
                ]
    for lt in range(width // tile):
        parts[:, :, lt * tile : lt * tile + tile] = sums[lt].reshape(half, 16, tile).astype(BF16)

    def share(m):
        to = 2 * lax.rem(ry + m[0] + ring, ring) + (1 - core if m[1] else core)
        return pltpu.make_async_remote_copy(
            src_ref=parts.at[to],
            dst_ref=shares.at[me],
            send_sem=rs_s.at[to],
            recv_sem=rs_r.at[me],
            device_id=(g, member(*m)),
            device_id_type=MESH,
        )

    for m in members:
        share(m).start()
    shares[me] = parts[me]

    def share_arrive(off, carry):
        frm = lax.rem(me + off, half)
        pltpu.make_async_remote_copy(
            src_ref=parts.at[0],
            dst_ref=shares.at[frm],
            send_sem=rs_s.at[frm],
            recv_sem=rs_r.at[frm],
            device_id=(g, d),
            device_id_type=MESH,
        ).wait_recv()
        return carry

    lax.fori_loop(1, half, share_arrive, 0)

    halves = []
    for h in range(2):
        total = shares[h].astype(F32)
        for t in range(1, ring):
            total += shares[2 * t + h].astype(F32)
        halves.append(total)
    coarse = gelu(jnp.concatenate(halves, axis=1)).astype(BF16)
    upper = dot(coarse, wu_v[...])

    def expand(base):
        return jnp.concatenate(
            [
                jnp.concatenate(
                    [
                        upper[4 * k : 4 * k + 4, base + ab * 64 : base + ab * 64 + 64]
                        for k in range(4)
                    ],
                    axis=1,
                )
                for ab in range(4)
            ],
            axis=0,
        )

    gate, value = expand(0), expand(256)
    own = jnp.concatenate(
        [skip_p[ab * 16 + 4 * i + 1 : ab * 16 + 4 * i + 3] for ab in range(4) for i in (1, 2)], axis=0
    )
    mixed = (own * jax.nn.sigmoid(gate) + value).astype(BF16)
    row, col = iota((16, 16), 0), iota((16, 16), 1)
    fits = ((row >> 2) == 2 * ((col >> 1) & 1) + (col >> 3)) & (
        (row & 3) == 2 * (col & 1) + ((col >> 2) & 1)
    )
    out[...] = dot(one_hot(fits), mixed).reshape(4, 4, 256).astype(BF16)

    for dx, dy in around:

        @pl.when(exists(dx, dy))
        def _():
            block_copy(dx, dy, (1 - dx) * 3 + 1 - dy).wait_send()

    twin.wait_send()

    @pl.when(edge)
    def _():
        for i in range(len(CHUNKS)):
            for k in range(2):
                cross(i, k).wait_send()
            onward(i, False).wait_send()

    for i in range(len(CHUNKS)):
        onward(i, True).wait_send()

    for m in members:
        spread(m).wait_send()
        share(m).wait_send()


def on_device(groups, devices, volume, w_first, w_second, w_lift, w_coarse, w_up):
    half = devices // 2
    wide = w_up.shape[0]
    tile = min(128, wide // 2)
    in_hbm = pl.BlockSpec(memory_space=pltpu.HBM)
    dma = pltpu.SemaphoreType.DMA
    result = pl.pallas_call(
        functools.partial(kernel, groups, devices),
        out_shape=jax.ShapeDtypeStruct((4, 4, 256), BF16),
        in_specs=[pl.BlockSpec(memory_space=pl.ANY)] + [in_hbm] * 5,
        out_specs=pl.BlockSpec(memory_space=pltpu.VMEM),
        scratch_shapes=[
            pltpu.VMEM((4, 4, 256), BF16),
            pltpu.VMEM((9, 16, 256), BF16),
            pltpu.VMEM((9, 3, 32, 32), BF16),
            pltpu.VMEM((9, 3, 32, 32), BF16),
            pltpu.VMEM((256, wide), BF16),
            pltpu.VMEM((wide, 512), BF16),
            pltpu.VMEM((9, 256, 256), BF16),
            pltpu.VMEM((9, 256, 256), BF16),
            pltpu.VMEM((4, 9, 3, 16, wide // 4), BF16),
            pltpu.VMEM((4, 2, 9, 3, 16, wide // 4), BF16),
            pltpu.VMEM((9, 4, 4, 16, 2 * wide), BF16),
            pltpu.VMEM((152, 256), F32),
            pltpu.VMEM((128, 256), F32),
            pltpu.VMEM((64, 256), F32),
            pltpu.VMEM((devices // 4, 16, 256), BF16),
            pltpu.VMEM((half, 16, 256), BF16),
            pltpu.VMEM((2, 16 * half, 128), F32),
            pltpu.VMEM((4 * half, 2304), BF16),
            pltpu.VMEM((wide // 2 // tile, 16 * half, tile), F32),
            pltpu.VMEM((half, 16, wide // 2), BF16),
            pltpu.VMEM((half, 16, wide // 2), BF16),
            dma((9,)),
            dma((2,)),
            dma((9,)),
            dma((9,)),
            dma((2 * len(CHUNKS),)),
            dma((2 * len(CHUNKS),)),
            dma((len(CHUNKS),)),
            dma((len(CHUNKS),)),
            dma((len(CHUNKS),)),
            dma((len(CHUNKS),)),
            dma((half,)),
            dma((half,)),
            dma((half,)),
            dma((half,)),
        ],
        compiler_params=pltpu.CompilerParams(
            collective_id=0, has_side_effects=True, vmem_limit_bytes=56 * 1024 * 1024
        ),
    )(
        volume,
        w_first.reshape(9, 3, 32, 32),
        w_second.reshape(9, 3, 32, 32),
        w_lift,
        w_coarse.reshape(9, 3, 16, wide),
        w_up,
    )
    return result


def solution(mesh):
    return jax.shard_map(
        functools.partial(on_device, mesh.shape["grp"], mesh.shape["dev"]),
        mesh=mesh,
        in_specs=(P("grp", "dev", None), P(), P(), P(), P(None, None, None, "dev", None), P()),
        out_specs=P("grp", "dev", None),
        check_vma=False,
    )
```

```python
import functools

import jax
import jax.numpy as jnp
from jax import lax
from jax.experimental import pallas as pl
from jax.experimental.pallas import tpu as pltpu
from jax.sharding import PartitionSpec as P

F32 = jnp.float32
BF16 = jnp.bfloat16
MESH = pl.DeviceIdType.MESH
BANDS = [(zi, zo) for zo in range(4) for zi in range(4) if abs(zi - zo) <= 1]
CHUNKS = [(0, 4), (4, 7), (7, 9)]
GAPS = [(zi, zo) for zo in range(4) for zi in range(4) if abs(zi - zo) > 1]


def gelu(v):
    return 0.5 * v * (1.0 + lax.erf(v * 0.7071067811865476))


def dot(a, b):
    return jnp.dot(a, b, preferred_element_type=F32)


def iota(shape, dim):
    return lax.broadcasted_iota(jnp.int32, shape, dim)


def one_hot(mask):
    return jnp.where(mask, 1.0, 0.0).astype(BF16)


def band_weights(w_ref, t_ref):
    spread = one_hot((iota((32, 256), 1) & 31) == iota((32, 256), 0))
    lane_z = iota((32, 256), 1) >> 5

    def body(tap, carry):
        w0 = dot(w_ref[tap, 0], spread)
        w1 = dot(w_ref[tap, 1], spread)
        w2 = dot(w_ref[tap, 2], spread)
        for zi in range(8):
            rows = jnp.where(
                lane_z == zi,
                w1,
                jnp.where(lane_z == zi - 1, w2, jnp.where(lane_z == zi + 1, w0, 0.0)),
            )
            t_ref[tap, zi * 32 : zi * 32 + 32, :] = rows.astype(BF16)
        return carry

    lax.fori_loop(0, 9, body, 0)


def kernel(
    groups, devices,
    vol, w1, w2, wl, wc, wu,
    out,
    block_v, blocks, w1_v, w2_v, wl_v, wu_v, t1, t2, wq, raw, tc, wide, first, skip_p, send, recv, flat, cols, sums, parts, shares,
    load_sem, twin_sem, halo_s, halo_r, raw_s, raw_r, fwd_s, fwd_r, side_s, side_r, a2a_s, a2a_r, rs_s, rs_r,
):
    g = lax.axis_index("grp")
    d = lax.axis_index("dev")
    ring = devices // 4
    half = devices // 2
    lanes = wl.shape[1]
    width = lanes // 2
    part = width // 2
    tile = min(128, width)
    core = lax.rem(d, 2)
    zh = lax.rem(lax.div(d, 2), 2)
    ry = lax.div(d, 4)
    zl = lax.rem(g, 4)
    edge = (zl == 0) | (zl == 3)

    def member(dy, other_core):
        to_core = 1 - core if other_core else core
        return (lax.rem(ry + dy + ring, ring) * 2 + zh) * 2 + to_core

    def neighbour(dx, dy):
        return lax.rem(g + dx + groups, groups), lax.rem(d + dy + devices, devices)

    def across(to_core):
        return g + 3 - 2 * zl, (ry * 2 + 1 - zh) * 2 + to_core

    xp = lax.rem(lax.div(g, 4), 2)
    aside = (g + 4 - 8 * xp, d)

    steps = [ring // 2]
    for k in range(ring // 2 - 1, 0, -1):
        steps += [k, -k]
    members = [(k, b) for k in steps for b in (0, 1)] + [(0, 1)]
    beside = [(dx, dy) for dx in (-1, 1) for dy in (-1, 1, 0)]
    around = [(0, -1), (0, 1)] + beside

    def exists(dx, dy):
        there = (d + dy >= 0) & (d + dy < devices)
        return there & (g + dx >= 0) & (g + dx < groups)

    barrier = pltpu.get_barrier_semaphore()
    first_load = pltpu.make_async_copy(vol, block_v, load_sem.at[0])
    first_load.start()
    sibling = 1 - 2 * core
    greeted = 0
    for dx, dy in around:
        wanted = exists(dx, dy)
        if dx == 0:
            wanted = wanted & (sibling != dy)
        greeted += wanted.astype(jnp.int32)

        @pl.when(wanted)
        def _():
            pl.semaphore_signal(
                barrier, inc=1, device_id=neighbour(dx, dy), device_id_type=MESH
            )

    partners = [across(0), across(1), aside] + [(g, member(*m)) for m in members]
    for p in partners:
        pl.semaphore_signal(barrier, inc=1, device_id=p, device_id_type=MESH)

    mine = 2 * zh + core
    loads = [
        pltpu.make_async_copy(src, dst, load_sem.at[i + 1])
        for i, (src, dst) in enumerate(
            [
                (w1, w1_v),
                (w2, w2_v),
                (wl, wl_v),
                (wu, wu_v),
            ]
        )
    ]
    quarters = [
        pltpu.make_async_copy(
            wc.at[:, :, :, q * part : q * part + part], wq.at[q], load_sem.at[5 + q]
        )
        for q in range(4)
    ]
    for c in quarters + loads:
        c.start()
    first_load.wait()
    blocks[4] = block_v[...].astype(F32).reshape(16, 256).astype(BF16)
    pl.semaphore_wait(barrier, greeted + len(partners))

    def block_copy(dx, dy, slot):
        return pltpu.make_async_remote_copy(
            src_ref=blocks.at[4],
            dst_ref=blocks.at[slot],
            send_sem=halo_s.at[slot],
            recv_sem=halo_r.at[slot],
            device_id=neighbour(dx, dy),
            device_id_type=MESH,
        )

    for dx, dy in around:

        @pl.when(exists(dx, dy))
        def _():
            block_copy(dx, dy, (1 - dx) * 3 + 1 - dy).start()

    for c in quarters:
        c.wait()
    twin = pltpu.make_async_remote_copy(
        src_ref=wq.at[pl.ds(2 - 2 * core, 2)],
        dst_ref=raw.at[mine],
        send_sem=twin_sem.at[0],
        recv_sem=twin_sem.at[1],
        device_id=(g, member(0, 1)),
        device_id_type=MESH,
    )
    twin.start()

    def cross(i, to_core):
        lo, hi = CHUNKS[i]
        return pltpu.make_async_remote_copy(
            src_ref=wq.at[2 * to_core + xp, lo:hi],
            dst_ref=raw.at[mine, xp, lo:hi],
            send_sem=raw_s.at[2 * i + to_core],
            recv_sem=raw_r.at[2 * i + core],
            device_id=across(to_core),
            device_id_type=MESH,
        )

    foreign = 2 * (1 - zh)

    def onward(i, sideways):
        lo, hi = CHUNKS[i]
        here = raw.at[pl.ds(foreign, 2), xp, lo:hi]
        return pltpu.make_async_remote_copy(
            src_ref=here,
            dst_ref=here,
            send_sem=(side_s if sideways else fwd_s).at[i],
            recv_sem=(side_r if sideways else fwd_r).at[i],
            device_id=aside if sideways else (jnp.where(zl == 0, g + 1, g - 1), d),
            device_id_type=MESH,
        )

    @pl.when(edge)
    def _():
        for i in range(len(CHUNKS)):
            for to_core in range(2):
                cross(i, to_core).start()

    def crossed(i, block):
        lo, hi = CHUNKS[i]
        there = raw.at[foreign + block, xp, lo:hi]
        return pltpu.make_async_remote_copy(
            src_ref=there,
            dst_ref=there,
            send_sem=raw_s.at[2 * i + block],
            recv_sem=raw_r.at[2 * i + block],
            device_id=across(block),
            device_id_type=MESH,
        )

    def pass_on(where):
        @pl.when(edge if where else jnp.logical_not(edge))
        def _():
            for i in range(len(CHUNKS)):
                if where:
                    crossed(i, 0).wait_recv()
                    crossed(i, 1).wait_recv()
                    onward(i, False).start()
                else:
                    onward(i, False).wait_recv()
                onward(i, True).start()

    def banded(block, source):
        for h in range(2):
            for zi, zo in BANDS:
                at = zo * width + h * part
                tc[:, zi, block, :, at : at + part] = source[h][:, zi - zo + 1]

    for zi, zo in GAPS:
        tc[:, zi, :, :, zo * width : zo * width + width] = jnp.zeros((9, 4, 16, width), BF16)
    wide[144:152] = jnp.zeros((8, 256), F32)
    first[120:128] = jnp.zeros((8, 256), F32)
    loads[0].wait()
    band_weights(w1_v, t1)
    loads[1].wait()
    band_weights(w2_v, t2)
    for c in loads[2:]:
        c.wait()
    banded(mine, [wq.at[2 * core + h] for h in range(2)])

    row, col = iota((144, 144), 0), iota((144, 144), 1)
    slot = col >> 4
    sx = (slot >= 3).astype(jnp.int32) + (slot >= 6).astype(jnp.int32)
    sy = slot - 3 * sx
    fits = (sx * 4 + ((col >> 2) & 3)) * 12 + sy * 4 + (col & 3) == row
    gx, gy = g - 1 + sx, d - 1 + sy
    fits = fits & (gx >= 0) & (gx < groups) & (gy >= 0) & (gy < devices)
    place = one_hot(fits)

    for dx, dy in around:
        slot = (1 + dx) * 3 + 1 + dy

        @pl.when(exists(dx, dy))
        def _():
            block_copy(dx, dy, slot).wait_recv()

        @pl.when(jnp.logical_not(exists(dx, dy)))
        def _():
            blocks[slot] = jnp.zeros((16, 256), BF16)

    wide[0:144] = dot(place, blocks[...].reshape(144, 256))

    total = jnp.zeros((120, 256), F32)
    for tap in range(9):
        off = (tap // 3) * 12 + tap % 3
        total += dot(wide[off : off + 120].astype(BF16), t1[tap])
    rows = iota((120, 256), 0)
    rx = (rows * 171) >> 11
    fx, fy = 4 * g - 3 + rx, 4 * d - 3 + rows - 12 * rx
    inside = (fx >= 0) & (fx < 4 * groups) & (fy >= 0) & (fy < 4 * devices)
    act = gelu(total).astype(BF16).astype(F32)
    first[0:120] = jnp.where(inside, act, 0.0)

    total = jnp.zeros((96, 256), F32)
    for tap in range(9):
        off = (tap // 3) * 12 + tap % 3
        total += dot(first[off : off + 96].astype(BF16), t2[tap])
    skip = gelu(total).astype(BF16)

    row, col = iota((64, 96), 0), iota((64, 96), 1)
    ci, cj = (row >> 2) & 3, row & 3
    fits = (2 * ci + (row >> 5)) * 12 + 2 * cj + ((row >> 4) & 1) == col
    cx, cy = 2 * g - 1 + ci, 2 * d - 1 + cj
    fits = fits & (cx >= 0) & (cx < 2 * groups) & (cy >= 0) & (cy < 2 * devices)
    moved = dot(one_hot(fits), skip)
    skip_p[...] = moved
    stacked = jnp.concatenate(
        [
            jnp.concatenate(
                [moved[ab * 16 : ab * 16 + 16, k * 64 : k * 64 + 64] for ab in range(4)], axis=1
            )
            for k in range(4)
        ],
        axis=0,
    )
    lifted = gelu(dot(stacked.astype(BF16), wl_v[...]))
    for t in range(ring):
        send[t] = jnp.concatenate(
            [lifted[k * 16 : k * 16 + 16, t * 64 : t * 64 + 64] for k in range(4)], axis=1
        ).astype(BF16)

    me = 2 * ry + core

    def spread(m):
        to_y = lax.rem(ry + m[0] + ring, ring)
        to = 2 * to_y + (1 - core if m[1] else core)
        return pltpu.make_async_remote_copy(
            src_ref=send.at[to_y],
            dst_ref=recv.at[me],
            send_sem=a2a_s.at[to],
            recv_sem=a2a_r.at[me],
            device_id=(g, member(*m)),
            device_id_type=MESH,
        )

    for m in members:
        spread(m).start()
    recv[me] = send[ry]
    twin.wait_recv()
    banded(2 * zh + 1 - core, [raw.at[2 * zh + 1 - core, h] for h in range(2)])
    pass_on(True)
    pass_on(False)

    def arrive(off, carry):
        frm = lax.rem(me + off, half)
        pltpu.make_async_remote_copy(
            src_ref=send.at[0],
            dst_ref=recv.at[frm],
            send_sem=a2a_s.at[frm],
            recv_sem=a2a_r.at[frm],
            device_id=(g, d),
            device_id_type=MESH,
        ).wait_recv()
        return carry

    lax.fori_loop(1, half, arrive, 0)

    for lt in range(2):
        flat[lt] = recv[:, :, lt * 128 : lt * 128 + 128].astype(F32).reshape(16 * half, 128)
    for xx in range(4):
        for yb in range(4):
            for lt in range(2):
                piece = flat[lt, pl.ds(4 * xx + yb, half, stride=16), :].astype(BF16)
                for a in range(3):
                    for b in range(3):
                        ox, oy = xx - a, yb - b
                        if 0 <= ox < 2 and 0 <= oy < 2:
                            at, to = (2 * ox + oy) * half, (3 * a + b) * 256 + lt * 128
                            cols[at : at + half, to : to + 128] = piece

    for i in range(len(CHUNKS)):
        lo, hi = CHUNKS[i]
        there = raw.at[pl.ds(foreign, 2), 1 - xp, lo:hi]
        pltpu.make_async_remote_copy(
            src_ref=there,
            dst_ref=there,
            send_sem=side_s.at[i],
            recv_sem=side_r.at[i],
            device_id=aside,
            device_id_type=MESH,
        ).wait_recv()
    for block in range(2):
        banded(foreign + block, [raw.at[foreign + block, h] for h in range(2)])

    lhs = cols[...]
    for z in range(4):
        got = dot(lhs, tc[:, :, :, :, z * width : z * width + width].reshape(2304, width))
        for q in range(4):
            for lt in range(width // tile):
                sums[lt, pl.ds(4 * z + q, half, stride=16), :] = got[
                    q * half : q * half + half, lt * tile : lt * tile + tile
                ]
    for lt in range(width // tile):
        parts[:, :, lt * tile : lt * tile + tile] = sums[lt].reshape(half, 16, tile).astype(BF16)

    def share(m):
        to = 2 * lax.rem(ry + m[0] + ring, ring) + (1 - core if m[1] else core)
        return pltpu.make_async_remote_copy(
            src_ref=parts.at[to],
            dst_ref=shares.at[me],
            send_sem=rs_s.at[to],
            recv_sem=rs_r.at[me],
            device_id=(g, member(*m)),
            device_id_type=MESH,
        )

    for m in members:
        share(m).start()
    shares[me] = parts[me]

    def share_arrive(off, carry):
        frm = lax.rem(me + off, half)
        pltpu.make_async_remote_copy(
            src_ref=parts.at[0],
            dst_ref=shares.at[frm],
            send_sem=rs_s.at[frm],
            recv_sem=rs_r.at[frm],
            device_id=(g, d),
            device_id_type=MESH,
        ).wait_recv()
        return carry

    lax.fori_loop(1, half, share_arrive, 0)

    halves = []
    for h in range(2):
        total = shares[h].astype(F32)
        for t in range(1, ring):
            total += shares[2 * t + h].astype(F32)
        halves.append(total)
    coarse = gelu(jnp.concatenate(halves, axis=1)).astype(BF16)
    upper = dot(coarse, wu_v[...])

    def expand(base):
        return jnp.concatenate(
            [
                jnp.concatenate(
                    [
                        upper[4 * k : 4 * k + 4, base + ab * 64 : base + ab * 64 + 64]
                        for k in range(4)
                    ],
                    axis=1,
                )
                for ab in range(4)
            ],
            axis=0,
        )

    gate, value = expand(0), expand(256)
    own = jnp.concatenate(
        [skip_p[ab * 16 + 4 * i + 1 : ab * 16 + 4 * i + 3] for ab in range(4) for i in (1, 2)], axis=0
    )
    mixed = (own * jax.nn.sigmoid(gate) + value).astype(BF16)
    row, col = iota((16, 16), 0), iota((16, 16), 1)
    fits = ((row >> 2) == 2 * ((col >> 1) & 1) + (col >> 3)) & (
        (row & 3) == 2 * (col & 1) + ((col >> 2) & 1)
    )
    out[...] = dot(one_hot(fits), mixed).reshape(4, 4, 256).astype(BF16)

    for dx, dy in around:

        @pl.when(exists(dx, dy))
        def _():
            block_copy(dx, dy, (1 - dx) * 3 + 1 - dy).wait_send()

    twin.wait_send()

    @pl.when(edge)
    def _():
        for i in range(len(CHUNKS)):
            for k in range(2):
                cross(i, k).wait_send()
            onward(i, False).wait_send()

    for i in range(len(CHUNKS)):
        onward(i, True).wait_send()

    for m in members:
        spread(m).wait_send()
        share(m).wait_send()


def on_device(groups, devices, volume, w_first, w_second, w_lift, w_coarse, w_up):
    half = devices // 2
    wide = w_up.shape[0]
    tile = min(128, wide // 2)
    in_hbm = pl.BlockSpec(memory_space=pltpu.HBM)
    dma = pltpu.SemaphoreType.DMA
    result = pl.pallas_call(
        functools.partial(kernel, groups, devices),
        out_shape=jax.ShapeDtypeStruct((4, 4, 256), BF16),
        in_specs=[pl.BlockSpec(memory_space=pl.ANY)] + [in_hbm] * 5,
        out_specs=pl.BlockSpec(memory_space=pltpu.VMEM),
        scratch_shapes=[
            pltpu.VMEM((4, 4, 256), BF16),
            pltpu.VMEM((9, 16, 256), BF16),
            pltpu.VMEM((9, 3, 32, 32), BF16),
            pltpu.VMEM((9, 3, 32, 32), BF16),
            pltpu.VMEM((256, wide), BF16),
            pltpu.VMEM((wide, 512), BF16),
            pltpu.VMEM((9, 256, 256), BF16),
            pltpu.VMEM((9, 256, 256), BF16),
            pltpu.VMEM((4, 9, 3, 16, wide // 4), BF16),
            pltpu.VMEM((4, 2, 9, 3, 16, wide // 4), BF16),
            pltpu.VMEM((9, 4, 4, 16, 2 * wide), BF16),
            pltpu.VMEM((152, 256), F32),
            pltpu.VMEM((128, 256), F32),
            pltpu.VMEM((64, 256), F32),
            pltpu.VMEM((devices // 4, 16, 256), BF16),
            pltpu.VMEM((half, 16, 256), BF16),
            pltpu.VMEM((2, 16 * half, 128), F32),
            pltpu.VMEM((4 * half, 2304), BF16),
            pltpu.VMEM((wide // 2 // tile, 16 * half, tile), F32),
            pltpu.VMEM((half, 16, wide // 2), BF16),
            pltpu.VMEM((half, 16, wide // 2), BF16),
            dma((9,)),
            dma((2,)),
            dma((9,)),
            dma((9,)),
            dma((2 * len(CHUNKS),)),
            dma((2 * len(CHUNKS),)),
            dma((len(CHUNKS),)),
            dma((len(CHUNKS),)),
            dma((len(CHUNKS),)),
            dma((len(CHUNKS),)),
            dma((half,)),
            dma((half,)),
            dma((half,)),
            dma((half,)),
        ],
        compiler_params=pltpu.CompilerParams(
            collective_id=0, has_side_effects=True, vmem_limit_bytes=56 * 1024 * 1024
        ),
    )(
        volume,
        w_first.reshape(9, 3, 32, 32),
        w_second.reshape(9, 3, 32, 32),
        w_lift,
        w_coarse.reshape(9, 3, 16, wide),
        w_up,
    )
    return result


def solution(mesh):
    return jax.shard_map(
        functools.partial(on_device, mesh.shape["grp"], mesh.shape["dev"]),
        mesh=mesh,
        in_specs=(P("grp", "dev", None), P(), P(), P(), P(None, None, None, "dev", None), P()),
        out_specs=P("grp", "dev", None),
        check_vma=False,
    )
```

```python
import functools

import jax
import jax.numpy as jnp
from jax import lax
from jax.experimental import pallas as pl
from jax.experimental.pallas import tpu as pltpu
from jax.sharding import PartitionSpec as P

F32 = jnp.float32
BF16 = jnp.bfloat16
MESH = pl.DeviceIdType.MESH
BANDS = [(zi, zo) for zo in range(4) for zi in range(4) if abs(zi - zo) <= 1]
CHUNKS = [(0, 3), (3, 5), (5, 7), (7, 8), (8, 9)]
GAPS = [(zi, zo) for zo in range(4) for zi in range(4) if abs(zi - zo) > 1]


def gelu(v):
    return 0.5 * v * (1.0 + lax.erf(v * 0.7071067811865476))


def dot(a, b):
    return jnp.dot(a, b, preferred_element_type=F32)


def iota(shape, dim):
    return lax.broadcasted_iota(jnp.int32, shape, dim)


def one_hot(mask):
    return jnp.where(mask, 1.0, 0.0).astype(BF16)


def band_weights(w_ref, t_ref):
    spread = one_hot((iota((32, 256), 1) & 31) == iota((32, 256), 0))
    lane_z = iota((32, 256), 1) >> 5

    def body(tap, carry):
        w0 = dot(w_ref[tap, 0], spread)
        w1 = dot(w_ref[tap, 1], spread)
        w2 = dot(w_ref[tap, 2], spread)
        for zi in range(8):
            rows = jnp.where(
                lane_z == zi,
                w1,
                jnp.where(lane_z == zi - 1, w2, jnp.where(lane_z == zi + 1, w0, 0.0)),
            )
            t_ref[tap, zi * 32 : zi * 32 + 32, :] = rows.astype(BF16)
        return carry

    lax.fori_loop(0, 9, body, 0)


def kernel(
    groups, devices,
    vol, w1, w2, wl, wc, wu,
    out,
    block_v, blocks, w1_v, w2_v, wl_v, wu_v, t1, t2, wq, raw, tc, wide, first, skip_p, send, recv, flat, cols, own_sums, sums, parts, shares,
    load_sem, twin_sem, halo_s, halo_r, raw_s, raw_r, fwd_s, fwd_r, side_s, side_r, a2a_s, a2a_r, rs_s, rs_r,
):
    g = lax.axis_index("grp")
    d = lax.axis_index("dev")
    ring = devices // 4
    half = devices // 2
    lanes = wl.shape[1]
    width = lanes // 2
    part = width // 2
    tile = min(128, width)
    core = lax.rem(d, 2)
    zh = lax.rem(lax.div(d, 2), 2)
    ry = lax.div(d, 4)
    zl = lax.rem(g, 4)
    edge = (zl == 0) | (zl == 3)

    def member(dy, other_core):
        to_core = 1 - core if other_core else core
        return (lax.rem(ry + dy + ring, ring) * 2 + zh) * 2 + to_core

    def neighbour(dx, dy):
        return lax.rem(g + dx + groups, groups), lax.rem(d + dy + devices, devices)

    def across(to_core):
        return g + 3 - 2 * zl, (ry * 2 + 1 - zh) * 2 + to_core

    xp = lax.rem(lax.div(g, 4), 2)
    aside = (g + 4 - 8 * xp, d)

    steps = [ring // 2]
    for k in range(ring // 2 - 1, 0, -1):
        steps += [k, -k]
    members = [(k, b) for k in steps for b in (0, 1)] + [(0, 1)]
    beside = [(dx, dy) for dx in (-1, 1) for dy in (-1, 1, 0)]
    around = [(0, -1), (0, 1)] + beside

    def exists(dx, dy):
        there = (d + dy >= 0) & (d + dy < devices)
        return there & (g + dx >= 0) & (g + dx < groups)

    barrier = pltpu.get_barrier_semaphore()
    first_load = pltpu.make_async_copy(vol, block_v, load_sem.at[0])
    first_load.start()
    sibling = 1 - 2 * core
    greeted = 0
    for dx, dy in around:
        wanted = exists(dx, dy)
        if dx == 0:
            wanted = wanted & (sibling != dy)
        greeted += wanted.astype(jnp.int32)

        @pl.when(wanted)
        def _():
            pl.semaphore_signal(
                barrier, inc=1, device_id=neighbour(dx, dy), device_id_type=MESH
            )

    partners = [across(0), across(1), aside] + [(g, member(*m)) for m in members]
    for p in partners:
        pl.semaphore_signal(barrier, inc=1, device_id=p, device_id_type=MESH)

    mine = 2 * zh + core
    loads = [
        pltpu.make_async_copy(src, dst, load_sem.at[i + 1])
        for i, (src, dst) in enumerate(
            [
                (w1, w1_v),
                (w2, w2_v),
                (wl, wl_v),
                (wu, wu_v),
            ]
        )
    ]
    quarters = [
        pltpu.make_async_copy(
            wc.at[:, :, :, q * part : q * part + part], wq.at[q], load_sem.at[5 + q]
        )
        for q in range(4)
    ]
    for c in quarters + loads:
        c.start()
    first_load.wait()
    blocks[4] = block_v[...].astype(F32).reshape(16, 256).astype(BF16)
    pl.semaphore_wait(barrier, greeted + len(partners))

    def cross(i, to_core):
        lo, hi = CHUNKS[i]
        return pltpu.make_async_remote_copy(
            src_ref=wq.at[2 * to_core + xp, lo:hi],
            dst_ref=raw.at[mine, xp, lo:hi],
            send_sem=raw_s.at[2 * i + to_core],
            recv_sem=raw_r.at[2 * i + core],
            device_id=across(to_core),
            device_id_type=MESH,
        )

    for c in quarters:
        c.wait()

    @pl.when(edge)
    def _():
        for i in range(len(CHUNKS)):
            for to_core in range(2):
                cross(i, to_core).start()

    def block_copy(dx, dy, slot):
        return pltpu.make_async_remote_copy(
            src_ref=blocks.at[4],
            dst_ref=blocks.at[slot],
            send_sem=halo_s.at[slot],
            recv_sem=halo_r.at[slot],
            device_id=neighbour(dx, dy),
            device_id_type=MESH,
        )

    for dx, dy in around:

        @pl.when(exists(dx, dy))
        def _():
            block_copy(dx, dy, (1 - dx) * 3 + 1 - dy).start()

    twin = pltpu.make_async_remote_copy(
        src_ref=wq.at[pl.ds(2 - 2 * core, 2)],
        dst_ref=raw.at[mine],
        send_sem=twin_sem.at[0],
        recv_sem=twin_sem.at[1],
        device_id=(g, member(0, 1)),
        device_id_type=MESH,
    )
    twin.start()

    foreign = 2 * (1 - zh)

    def onward(i, sideways):
        lo, hi = CHUNKS[i]
        here = raw.at[pl.ds(foreign, 2), xp, lo:hi]
        return pltpu.make_async_remote_copy(
            src_ref=here,
            dst_ref=here,
            send_sem=(side_s if sideways else fwd_s).at[i],
            recv_sem=(side_r if sideways else fwd_r).at[i],
            device_id=aside if sideways else (jnp.where(zl == 0, g + 1, g - 1), d),
            device_id_type=MESH,
        )

    def crossed(i, block):
        lo, hi = CHUNKS[i]
        there = raw.at[foreign + block, xp, lo:hi]
        return pltpu.make_async_remote_copy(
            src_ref=there,
            dst_ref=there,
            send_sem=raw_s.at[2 * i + block],
            recv_sem=raw_r.at[2 * i + block],
            device_id=across(block),
            device_id_type=MESH,
        )

    def pass_on(where):
        @pl.when(edge if where else jnp.logical_not(edge))
        def _():
            for i in range(len(CHUNKS)):
                if where:
                    crossed(i, 0).wait_recv()
                    crossed(i, 1).wait_recv()
                    onward(i, False).start()
                else:
                    onward(i, False).wait_recv()
                onward(i, True).start()

    def banded(z_half, block, h, source):
        for zi, zo in BANDS:
            at = pl.multiple_of(zo * width + h * part, part)
            tc[z_half, :, zi, block, :, pl.ds(at, part)] = source[:, zi - zo + 1]

    for zi, zo in GAPS:
        tc[:, :, zi, :, :, zo * width : zo * width + width] = jnp.zeros((2, 9, 2, 16, width), BF16)
    wide[144:152] = jnp.zeros((8, 256), F32)
    first[120:128] = jnp.zeros((8, 256), F32)
    loads[0].wait()
    band_weights(w1_v, t1)
    loads[1].wait()
    band_weights(w2_v, t2)
    for c in loads[2:]:
        c.wait()
    for h in range(2):
        banded(zh, core, h, wq.at[2 * core + h])

    row, col = iota((144, 144), 0), iota((144, 144), 1)
    slot = col >> 4
    sx = (slot >= 3).astype(jnp.int32) + (slot >= 6).astype(jnp.int32)
    sy = slot - 3 * sx
    fits = (sx * 4 + ((col >> 2) & 3)) * 12 + sy * 4 + (col & 3) == row
    gx, gy = g - 1 + sx, d - 1 + sy
    fits = fits & (gx >= 0) & (gx < groups) & (gy >= 0) & (gy < devices)
    place = one_hot(fits)

    for dx, dy in around:
        slot = (1 + dx) * 3 + 1 + dy

        @pl.when(exists(dx, dy))
        def _():
            block_copy(dx, dy, slot).wait_recv()

        @pl.when(jnp.logical_not(exists(dx, dy)))
        def _():
            blocks[slot] = jnp.zeros((16, 256), BF16)

    wide[0:144] = dot(place, blocks[...].reshape(144, 256))

    total = jnp.zeros((120, 256), F32)
    for tap in range(9):
        off = (tap // 3) * 12 + tap % 3
        total += dot(wide[off : off + 120].astype(BF16), t1[tap])
    rows = iota((120, 256), 0)
    rx = (rows * 171) >> 11
    fx, fy = 4 * g - 3 + rx, 4 * d - 3 + rows - 12 * rx
    inside = (fx >= 0) & (fx < 4 * groups) & (fy >= 0) & (fy < 4 * devices)
    act = gelu(total).astype(BF16).astype(F32)
    first[0:120] = jnp.where(inside, act, 0.0)

    total = jnp.zeros((96, 256), F32)
    for tap in range(9):
        off = (tap // 3) * 12 + tap % 3
        total += dot(first[off : off + 96].astype(BF16), t2[tap])
    skip = gelu(total).astype(BF16)

    row, col = iota((64, 96), 0), iota((64, 96), 1)
    ci, cj = (row >> 2) & 3, row & 3
    fits = (2 * ci + (row >> 5)) * 12 + 2 * cj + ((row >> 4) & 1) == col
    cx, cy = 2 * g - 1 + ci, 2 * d - 1 + cj
    fits = fits & (cx >= 0) & (cx < 2 * groups) & (cy >= 0) & (cy < 2 * devices)
    moved = dot(one_hot(fits), skip)
    skip_p[...] = moved
    stacked = jnp.concatenate(
        [
            jnp.concatenate(
                [moved[ab * 16 : ab * 16 + 16, k * 64 : k * 64 + 64] for ab in range(4)], axis=1
            )
            for k in range(4)
        ],
        axis=0,
    )
    lifted = gelu(dot(stacked.astype(BF16), wl_v[...]))
    for t in range(ring):
        send[t] = jnp.concatenate(
            [
                lifted[k * 16 : k * 16 + 16, t * 64 + h * 32 : t * 64 + h * 32 + 32]
                for h in range(2)
                for k in range(4)
            ],
            axis=1,
        ).astype(BF16)

    me = 2 * ry + core

    def spread(m):
        to_y = lax.rem(ry + m[0] + ring, ring)
        to = 2 * to_y + (1 - core if m[1] else core)
        return pltpu.make_async_remote_copy(
            src_ref=send.at[to_y],
            dst_ref=recv.at[me],
            send_sem=a2a_s.at[to],
            recv_sem=a2a_r.at[me],
            device_id=(g, member(*m)),
            device_id_type=MESH,
        )

    for m in members:
        spread(m).start()
    recv[me] = send[ry]
    twin.wait_recv()
    for h in range(2):
        banded(zh, 1 - core, h, raw.at[2 * zh + 1 - core, h])
    pass_on(True)
    pass_on(False)

    def arrive(off, carry):
        frm = lax.rem(me + off, half)
        pltpu.make_async_remote_copy(
            src_ref=send.at[0],
            dst_ref=recv.at[frm],
            send_sem=a2a_s.at[frm],
            recv_sem=a2a_r.at[frm],
            device_id=(g, d),
            device_id_type=MESH,
        ).wait_recv()
        return carry

    lax.fori_loop(1, half, arrive, 0)

    for lt in range(2):
        flat[lt] = recv[:, :, lt * 128 : lt * 128 + 128].astype(F32).reshape(16 * half, 128)
    for xx in range(4):
        for yb in range(4):
            for lt in range(2):
                piece = flat[lt, pl.ds(4 * xx + yb, half, stride=16), :].astype(BF16)
                for a in range(3):
                    for b in range(3):
                        ox, oy = xx - a, yb - b
                        if 0 <= ox < 2 and 0 <= oy < 2:
                            at, to = (2 * ox + oy) * half, (3 * a + b) * 128
                            cols[lt, at : at + half, to : to + 128] = piece

    def product(z_half, z):
        return dot(
            cols[z_half],
            tc[z_half, :, :, :, :, z * width : z * width + width].reshape(1152, width),
        )

    for z in range(4):
        own_sums[z] = product(zh, z)
    for block in range(2):
        banded(1 - zh, block, xp, raw.at[foreign + block, xp])

    for i in range(len(CHUNKS)):
        lo, hi = CHUNKS[i]
        there = raw.at[pl.ds(foreign, 2), 1 - xp, lo:hi]
        pltpu.make_async_remote_copy(
            src_ref=there,
            dst_ref=there,
            send_sem=side_s.at[i],
            recv_sem=side_r.at[i],
            device_id=aside,
            device_id_type=MESH,
        ).wait_recv()
    for block in range(2):
        banded(1 - zh, block, 1 - xp, raw.at[foreign + block, 1 - xp])

    for z in range(4):
        got = own_sums[z] + product(1 - zh, z)
        for q in range(4):
            for lt in range(width // tile):
                sums[lt, pl.ds(4 * z + q, half, stride=16), :] = got[
                    q * half : q * half + half, lt * tile : lt * tile + tile
                ]
    for lt in range(width // tile):
        parts[:, :, lt * tile : lt * tile + tile] = sums[lt].reshape(half, 16, tile).astype(BF16)

    def share(m):
        to = 2 * lax.rem(ry + m[0] + ring, ring) + (1 - core if m[1] else core)
        return pltpu.make_async_remote_copy(
            src_ref=parts.at[to],
            dst_ref=shares.at[me],
            send_sem=rs_s.at[to],
            recv_sem=rs_r.at[me],
            device_id=(g, member(*m)),
            device_id_type=MESH,
        )

    for m in members:
        share(m).start()
    shares[me] = parts[me]

    def share_arrive(off, carry):
        frm = lax.rem(me + off, half)
        pltpu.make_async_remote_copy(
            src_ref=parts.at[0],
            dst_ref=shares.at[frm],
            send_sem=rs_s.at[frm],
            recv_sem=rs_r.at[frm],
            device_id=(g, d),
            device_id_type=MESH,
        ).wait_recv()
        return carry

    lax.fori_loop(1, half, share_arrive, 0)

    halves = []
    for h in range(2):
        total = shares[h].astype(F32)
        for t in range(1, ring):
            total += shares[2 * t + h].astype(F32)
        halves.append(total)
    coarse = gelu(jnp.concatenate(halves, axis=1)).astype(BF16)
    upper = dot(coarse, wu_v[...])

    def expand(base):
        return jnp.concatenate(
            [
                jnp.concatenate(
                    [
                        upper[4 * k : 4 * k + 4, base + ab * 64 : base + ab * 64 + 64]
                        for k in range(4)
                    ],
                    axis=1,
                )
                for ab in range(4)
            ],
            axis=0,
        )

    gate, value = expand(0), expand(256)
    own = jnp.concatenate(
        [skip_p[ab * 16 + 4 * i + 1 : ab * 16 + 4 * i + 3] for ab in range(4) for i in (1, 2)], axis=0
    )
    mixed = (own * jax.nn.sigmoid(gate) + value).astype(BF16)
    row, col = iota((16, 16), 0), iota((16, 16), 1)
    fits = ((row >> 2) == 2 * ((col >> 1) & 1) + (col >> 3)) & (
        (row & 3) == 2 * (col & 1) + ((col >> 2) & 1)
    )
    out[...] = dot(one_hot(fits), mixed).reshape(4, 4, 256).astype(BF16)

    for dx, dy in around:

        @pl.when(exists(dx, dy))
        def _():
            block_copy(dx, dy, (1 - dx) * 3 + 1 - dy).wait_send()

    twin.wait_send()

    @pl.when(edge)
    def _():
        for i in range(len(CHUNKS)):
            for k in range(2):
                cross(i, k).wait_send()
            onward(i, False).wait_send()

    for i in range(len(CHUNKS)):
        onward(i, True).wait_send()

    for m in members:
        spread(m).wait_send()
        share(m).wait_send()


def on_device(groups, devices, volume, w_first, w_second, w_lift, w_coarse, w_up):
    half = devices // 2
    wide = w_up.shape[0]
    tile = min(128, wide // 2)
    in_hbm = pl.BlockSpec(memory_space=pltpu.HBM)
    dma = pltpu.SemaphoreType.DMA
    result = pl.pallas_call(
        functools.partial(kernel, groups, devices),
        out_shape=jax.ShapeDtypeStruct((4, 4, 256), BF16),
        in_specs=[pl.BlockSpec(memory_space=pl.ANY)] + [in_hbm] * 5,
        out_specs=pl.BlockSpec(memory_space=pltpu.VMEM),
        scratch_shapes=[
            pltpu.VMEM((4, 4, 256), BF16),
            pltpu.VMEM((9, 16, 256), BF16),
            pltpu.VMEM((9, 3, 32, 32), BF16),
            pltpu.VMEM((9, 3, 32, 32), BF16),
            pltpu.VMEM((256, wide), BF16),
            pltpu.VMEM((wide, 512), BF16),
            pltpu.VMEM((9, 256, 256), BF16),
            pltpu.VMEM((9, 256, 256), BF16),
            pltpu.VMEM((4, 9, 3, 16, wide // 4), BF16),
            pltpu.VMEM((4, 2, 9, 3, 16, wide // 4), BF16),
            pltpu.VMEM((2, 9, 4, 2, 16, 2 * wide), BF16),
            pltpu.VMEM((152, 256), F32),
            pltpu.VMEM((128, 256), F32),
            pltpu.VMEM((64, 256), F32),
            pltpu.VMEM((devices // 4, 16, 256), BF16),
            pltpu.VMEM((half, 16, 256), BF16),
            pltpu.VMEM((2, 16 * half, 128), F32),
            pltpu.VMEM((2, 4 * half, 1152), BF16),
            pltpu.VMEM((4, 4 * half, wide // 2), F32),
            pltpu.VMEM((wide // 2 // tile, 16 * half, tile), F32),
            pltpu.VMEM((half, 16, wide // 2), BF16),
            pltpu.VMEM((half, 16, wide // 2), BF16),
            dma((9,)),
            dma((2,)),
            dma((9,)),
            dma((9,)),
            dma((2 * len(CHUNKS),)),
            dma((2 * len(CHUNKS),)),
            dma((len(CHUNKS),)),
            dma((len(CHUNKS),)),
            dma((len(CHUNKS),)),
            dma((len(CHUNKS),)),
            dma((half,)),
            dma((half,)),
            dma((half,)),
            dma((half,)),
        ],
        compiler_params=pltpu.CompilerParams(
            collective_id=0, has_side_effects=True, vmem_limit_bytes=56 * 1024 * 1024
        ),
    )(
        volume,
        w_first.reshape(9, 3, 32, 32),
        w_second.reshape(9, 3, 32, 32),
        w_lift,
        w_coarse.reshape(9, 3, 16, wide),
        w_up,
    )
    return result


def solution(mesh):
    return jax.shard_map(
        functools.partial(on_device, mesh.shape["grp"], mesh.shape["dev"]),
        mesh=mesh,
        in_specs=(P("grp", "dev", None), P(), P(), P(), P(None, None, None, "dev", None), P()),
        out_specs=P("grp", "dev", None),
        check_vma=False,
    )
```

```python
import functools

import jax
import jax.numpy as jnp
from jax import lax
from jax.experimental import pallas as pl
from jax.experimental.pallas import tpu as pltpu
from jax.sharding import PartitionSpec as P

F32 = jnp.float32
BF16 = jnp.bfloat16
MESH = pl.DeviceIdType.MESH
BANDS = [(zi, zo) for zo in range(4) for zi in range(4) if abs(zi - zo) <= 1]
CHUNKS = [(0, 4), (4, 7), (7, 9)]
GAPS = [(zi, zo) for zo in range(4) for zi in range(4) if abs(zi - zo) > 1]


def gelu(v):
    return 0.5 * v * (1.0 + lax.erf(v * 0.7071067811865476))


def dot(a, b):
    return jnp.dot(a, b, preferred_element_type=F32)


def iota(shape, dim):
    return lax.broadcasted_iota(jnp.int32, shape, dim)


def one_hot(mask):
    return jnp.where(mask, 1.0, 0.0).astype(BF16)


def band_weights(w_ref, t_ref):
    spread = one_hot((iota((32, 256), 1) & 31) == iota((32, 256), 0))
    lane_z = iota((32, 256), 1) >> 5

    def body(tap, carry):
        w0 = dot(w_ref[tap, 0], spread)
        w1 = dot(w_ref[tap, 1], spread)
        w2 = dot(w_ref[tap, 2], spread)
        for zi in range(8):
            rows = jnp.where(
                lane_z == zi,
                w1,
                jnp.where(lane_z == zi - 1, w2, jnp.where(lane_z == zi + 1, w0, 0.0)),
            )
            t_ref[tap, zi * 32 : zi * 32 + 32, :] = rows.astype(BF16)
        return carry

    lax.fori_loop(0, 9, body, 0)


def kernel(
    groups, devices,
    vol, w1, w2, wl, wc, wu,
    out,
    block_v, blocks, w1_v, w2_v, wl_v, wu_v, t1, t2, wq, raw, tc, wide, first, skip_p, send, recv, flat, cols, own_sums, sums, parts, shares,
    load_sem, twin_sem, halo_s, halo_r, raw_s, raw_r, fwd_s, fwd_r, side_s, side_r, a2a_s, a2a_r, rs_s, rs_r,
):
    g = lax.axis_index("grp")
    d = lax.axis_index("dev")
    ring = devices // 4
    half = devices // 2
    lanes = wl.shape[1]
    width = lanes // 2
    part = width // 2
    tile = min(128, width)
    core = lax.rem(d, 2)
    zh = lax.rem(lax.div(d, 2), 2)
    ry = lax.div(d, 4)
    zl = lax.rem(g, 4)
    edge = (zl == 0) | (zl == 3)

    def member(dy, other_core):
        to_core = 1 - core if other_core else core
        return (lax.rem(ry + dy + ring, ring) * 2 + zh) * 2 + to_core

    def neighbour(dx, dy):
        return lax.rem(g + dx + groups, groups), lax.rem(d + dy + devices, devices)

    def across(to_core):
        return g + 3 - 2 * zl, (ry * 2 + 1 - zh) * 2 + to_core

    xp = lax.rem(lax.div(g, 4), 2)
    aside = (g + 4 - 8 * xp, d)

    steps = [ring // 2]
    for k in range(ring // 2 - 1, 0, -1):
        steps += [k, -k]
    members = [(k, b) for k in steps for b in (0, 1)] + [(0, 1)]
    beside = [(dx, dy) for dx in (-1, 1) for dy in (-1, 1, 0)]
    around = [(0, -1), (0, 1)] + beside

    def exists(dx, dy):
        there = (d + dy >= 0) & (d + dy < devices)
        return there & (g + dx >= 0) & (g + dx < groups)

    barrier = pltpu.get_barrier_semaphore()
    first_load = pltpu.make_async_copy(vol, block_v, load_sem.at[0])
    first_load.start()
    sibling = 1 - 2 * core
    greeted = 0
    for dx, dy in around:
        wanted = exists(dx, dy)
        if dx == 0:
            wanted = wanted & (sibling != dy)
        greeted += wanted.astype(jnp.int32)

        @pl.when(wanted)
        def _():
            pl.semaphore_signal(
                barrier, inc=1, device_id=neighbour(dx, dy), device_id_type=MESH
            )

    partners = [across(0), across(1), aside] + [(g, member(*m)) for m in members]
    for p in partners:
        pl.semaphore_signal(barrier, inc=1, device_id=p, device_id_type=MESH)

    mine = 2 * zh + core
    loads = [
        pltpu.make_async_copy(src, dst, load_sem.at[i + 1])
        for i, (src, dst) in enumerate(
            [
                (w1, w1_v),
                (w2, w2_v),
                (wl, wl_v),
                (wu, wu_v),
            ]
        )
    ]
    quarters = [
        pltpu.make_async_copy(
            wc.at[:, :, :, q * part : q * part + part], wq.at[q], load_sem.at[5 + q]
        )
        for q in range(4)
    ]
    for c in quarters + loads:
        c.start()
    first_load.wait()
    blocks[4] = block_v[...].astype(F32).reshape(16, 256).astype(BF16)
    pl.semaphore_wait(barrier, greeted + len(partners))

    def cross(i, to_core):
        lo, hi = CHUNKS[i]
        return pltpu.make_async_remote_copy(
            src_ref=wq.at[2 * to_core + xp, lo:hi],
            dst_ref=raw.at[mine, xp, lo:hi],
            send_sem=raw_s.at[2 * i + to_core],
            recv_sem=raw_r.at[2 * i + core],
            device_id=across(to_core),
            device_id_type=MESH,
        )

    def block_copy(dx, dy, slot):
        return pltpu.make_async_remote_copy(
            src_ref=blocks.at[4],
            dst_ref=blocks.at[slot],
            send_sem=halo_s.at[slot],
            recv_sem=halo_r.at[slot],
            device_id=neighbour(dx, dy),
            device_id_type=MESH,
        )

    for dx, dy in around:

        @pl.when(exists(dx, dy))
        def _():
            block_copy(dx, dy, (1 - dx) * 3 + 1 - dy).start()

    for c in quarters:
        c.wait()

    @pl.when(edge)
    def _():
        for i in range(len(CHUNKS)):
            for to_core in range(2):
                cross(i, to_core).start()

    twin = pltpu.make_async_remote_copy(
        src_ref=wq.at[pl.ds(2 - 2 * core, 2)],
        dst_ref=raw.at[mine],
        send_sem=twin_sem.at[0],
        recv_sem=twin_sem.at[1],
        device_id=(g, member(0, 1)),
        device_id_type=MESH,
    )
    twin.start()

    foreign = 2 * (1 - zh)

    def onward(i, sideways):
        lo, hi = CHUNKS[i]
        here = raw.at[pl.ds(foreign, 2), xp, lo:hi]
        return pltpu.make_async_remote_copy(
            src_ref=here,
            dst_ref=here,
            send_sem=(side_s if sideways else fwd_s).at[i],
            recv_sem=(side_r if sideways else fwd_r).at[i],
            device_id=aside if sideways else (jnp.where(zl == 0, g + 1, g - 1), d),
            device_id_type=MESH,
        )

    def crossed(i, block):
        lo, hi = CHUNKS[i]
        there = raw.at[foreign + block, xp, lo:hi]
        return pltpu.make_async_remote_copy(
            src_ref=there,
            dst_ref=there,
            send_sem=raw_s.at[2 * i + block],
            recv_sem=raw_r.at[2 * i + block],
            device_id=across(block),
            device_id_type=MESH,
        )

    def pass_on(where):
        @pl.when(edge if where else jnp.logical_not(edge))
        def _():
            for i in range(len(CHUNKS)):
                if where:
                    crossed(i, 0).wait_recv()
                    crossed(i, 1).wait_recv()
                    onward(i, False).start()
                else:
                    onward(i, False).wait_recv()
                onward(i, True).start()

    def banded(z_half, block, h, source):
        for zi, zo in BANDS:
            at = pl.multiple_of(zo * width + h * part, part)
            tc[z_half, :, zi, block, :, pl.ds(at, part)] = source[:, zi - zo + 1]

    for zi, zo in GAPS:
        tc[:, :, zi, :, :, zo * width : zo * width + width] = jnp.zeros((2, 9, 2, 16, width), BF16)
    wide[144:152] = jnp.zeros((8, 256), F32)
    first[120:128] = jnp.zeros((8, 256), F32)
    loads[0].wait()
    band_weights(w1_v, t1)
    loads[1].wait()
    band_weights(w2_v, t2)
    for c in loads[2:]:
        c.wait()
    for h in range(2):
        banded(zh, core, h, wq.at[2 * core + h])

    row, col = iota((144, 144), 0), iota((144, 144), 1)
    slot = col >> 4
    sx = (slot >= 3).astype(jnp.int32) + (slot >= 6).astype(jnp.int32)
    sy = slot - 3 * sx
    fits = (sx * 4 + ((col >> 2) & 3)) * 12 + sy * 4 + (col & 3) == row
    gx, gy = g - 1 + sx, d - 1 + sy
    fits = fits & (gx >= 0) & (gx < groups) & (gy >= 0) & (gy < devices)
    place = one_hot(fits)

    for dx, dy in around:
        slot = (1 + dx) * 3 + 1 + dy

        @pl.when(exists(dx, dy))
        def _():
            block_copy(dx, dy, slot).wait_recv()

        @pl.when(jnp.logical_not(exists(dx, dy)))
        def _():
            blocks[slot] = jnp.zeros((16, 256), BF16)

    wide[0:144] = dot(place, blocks[...].reshape(144, 256))

    total = jnp.zeros((120, 256), F32)
    for tap in range(9):
        off = (tap // 3) * 12 + tap % 3
        total += dot(wide[off : off + 120].astype(BF16), t1[tap])
    rows = iota((120, 256), 0)
    rx = (rows * 171) >> 11
    fx, fy = 4 * g - 3 + rx, 4 * d - 3 + rows - 12 * rx
    inside = (fx >= 0) & (fx < 4 * groups) & (fy >= 0) & (fy < 4 * devices)
    act = gelu(total).astype(BF16).astype(F32)
    first[0:120] = jnp.where(inside, act, 0.0)

    total = jnp.zeros((96, 256), F32)
    for tap in range(9):
        off = (tap // 3) * 12 + tap % 3
        total += dot(first[off : off + 96].astype(BF16), t2[tap])
    skip = gelu(total).astype(BF16)

    row, col = iota((64, 96), 0), iota((64, 96), 1)
    ci, cj = (row >> 2) & 3, row & 3
    fits = (2 * ci + (row >> 5)) * 12 + 2 * cj + ((row >> 4) & 1) == col
    cx, cy = 2 * g - 1 + ci, 2 * d - 1 + cj
    fits = fits & (cx >= 0) & (cx < 2 * groups) & (cy >= 0) & (cy < 2 * devices)
    moved = dot(one_hot(fits), skip)
    skip_p[...] = moved
    stacked = jnp.concatenate(
        [
            jnp.concatenate(
                [moved[ab * 16 : ab * 16 + 16, k * 64 : k * 64 + 64] for ab in range(4)], axis=1
            )
            for k in range(4)
        ],
        axis=0,
    )
    lifted = gelu(dot(stacked.astype(BF16), wl_v[...]))
    for t in range(ring):
        send[t] = jnp.concatenate(
            [
                lifted[k * 16 : k * 16 + 16, t * 64 + h * 32 : t * 64 + h * 32 + 32]
                for h in range(2)
                for k in range(4)
            ],
            axis=1,
        ).astype(BF16)

    me = 2 * ry + core

    def spread(m):
        to_y = lax.rem(ry + m[0] + ring, ring)
        to = 2 * to_y + (1 - core if m[1] else core)
        return pltpu.make_async_remote_copy(
            src_ref=send.at[to_y],
            dst_ref=recv.at[me],
            send_sem=a2a_s.at[to],
            recv_sem=a2a_r.at[me],
            device_id=(g, member(*m)),
            device_id_type=MESH,
        )

    for m in members:
        spread(m).start()
    recv[me] = send[ry]
    twin.wait_recv()
    for h in range(2):
        banded(zh, 1 - core, h, raw.at[2 * zh + 1 - core, h])
    pass_on(True)
    pass_on(False)

    def arrive(off, carry):
        frm = lax.rem(me + off, half)
        pltpu.make_async_remote_copy(
            src_ref=send.at[0],
            dst_ref=recv.at[frm],
            send_sem=a2a_s.at[frm],
            recv_sem=a2a_r.at[frm],
            device_id=(g, d),
            device_id_type=MESH,
        ).wait_recv()
        return carry

    lax.fori_loop(1, half, arrive, 0)

    for lt in range(2):
        flat[lt] = recv[:, :, lt * 128 : lt * 128 + 128].astype(F32).reshape(16 * half, 128)
    for xx in range(4):
        for yb in range(4):
            for lt in range(2):
                piece = flat[lt, pl.ds(4 * xx + yb, half, stride=16), :].astype(BF16)
                for a in range(3):
                    for b in range(3):
                        ox, oy = xx - a, yb - b
                        if 0 <= ox < 2 and 0 <= oy < 2:
                            at, to = (2 * ox + oy) * half, (3 * a + b) * 128
                            cols[lt, at : at + half, to : to + 128] = piece

    def product(z_half, z):
        return dot(
            cols[z_half],
            tc[z_half, :, :, :, :, z * width : z * width + width].reshape(1152, width),
        )

    for z in range(4):
        own_sums[z] = product(zh, z)
    for block in range(2):
        banded(1 - zh, block, xp, raw.at[foreign + block, xp])

    for i in range(len(CHUNKS)):
        lo, hi = CHUNKS[i]
        there = raw.at[pl.ds(foreign, 2), 1 - xp, lo:hi]
        pltpu.make_async_remote_copy(
            src_ref=there,
            dst_ref=there,
            send_sem=side_s.at[i],
            recv_sem=side_r.at[i],
            device_id=aside,
            device_id_type=MESH,
        ).wait_recv()
    for block in range(2):
        banded(1 - zh, block, 1 - xp, raw.at[foreign + block, 1 - xp])

    for z in range(4):
        got = own_sums[z] + product(1 - zh, z)
        for q in range(4):
            for lt in range(width // tile):
                sums[lt, pl.ds(4 * z + q, half, stride=16), :] = got[
                    q * half : q * half + half, lt * tile : lt * tile + tile
                ]
    for lt in range(width // tile):
        parts[:, :, lt * tile : lt * tile + tile] = sums[lt].reshape(half, 16, tile).astype(BF16)

    def share(m):
        to = 2 * lax.rem(ry + m[0] + ring, ring) + (1 - core if m[1] else core)
        return pltpu.make_async_remote_copy(
            src_ref=parts.at[to],
            dst_ref=shares.at[me],
            send_sem=rs_s.at[to],
            recv_sem=rs_r.at[me],
            device_id=(g, member(*m)),
            device_id_type=MESH,
        )

    for m in members:
        share(m).start()
    shares[me] = parts[me]

    def share_arrive(off, carry):
        frm = lax.rem(me + off, half)
        pltpu.make_async_remote_copy(
            src_ref=parts.at[0],
            dst_ref=shares.at[frm],
            send_sem=rs_s.at[frm],
            recv_sem=rs_r.at[frm],
            device_id=(g, d),
            device_id_type=MESH,
        ).wait_recv()
        return carry

    lax.fori_loop(1, half, share_arrive, 0)

    halves = []
    for h in range(2):
        total = shares[h].astype(F32)
        for t in range(1, ring):
            total += shares[2 * t + h].astype(F32)
        halves.append(total)
    coarse = gelu(jnp.concatenate(halves, axis=1)).astype(BF16)
    upper = dot(coarse, wu_v[...])

    def expand(base):
        return jnp.concatenate(
            [
                jnp.concatenate(
                    [
                        upper[4 * k : 4 * k + 4, base + ab * 64 : base + ab * 64 + 64]
                        for k in range(4)
                    ],
                    axis=1,
                )
                for ab in range(4)
            ],
            axis=0,
        )

    gate, value = expand(0), expand(256)
    own = jnp.concatenate(
        [skip_p[ab * 16 + 4 * i + 1 : ab * 16 + 4 * i + 3] for ab in range(4) for i in (1, 2)], axis=0
    )
    mixed = (own * jax.nn.sigmoid(gate) + value).astype(BF16)
    row, col = iota((16, 16), 0), iota((16, 16), 1)
    fits = ((row >> 2) == 2 * ((col >> 1) & 1) + (col >> 3)) & (
        (row & 3) == 2 * (col & 1) + ((col >> 2) & 1)
    )
    out[...] = dot(one_hot(fits), mixed).reshape(4, 4, 256).astype(BF16)

    for dx, dy in around:

        @pl.when(exists(dx, dy))
        def _():
            block_copy(dx, dy, (1 - dx) * 3 + 1 - dy).wait_send()

    twin.wait_send()

    @pl.when(edge)
    def _():
        for i in range(len(CHUNKS)):
            for k in range(2):
                cross(i, k).wait_send()
            onward(i, False).wait_send()

    for i in range(len(CHUNKS)):
        onward(i, True).wait_send()

    for m in members:
        spread(m).wait_send()
        share(m).wait_send()


def on_device(groups, devices, volume, w_first, w_second, w_lift, w_coarse, w_up):
    half = devices // 2
    wide = w_up.shape[0]
    tile = min(128, wide // 2)
    in_hbm = pl.BlockSpec(memory_space=pltpu.HBM)
    dma = pltpu.SemaphoreType.DMA
    result = pl.pallas_call(
        functools.partial(kernel, groups, devices),
        out_shape=jax.ShapeDtypeStruct((4, 4, 256), BF16),
        in_specs=[pl.BlockSpec(memory_space=pl.ANY)] + [in_hbm] * 5,
        out_specs=pl.BlockSpec(memory_space=pltpu.VMEM),
        scratch_shapes=[
            pltpu.VMEM((4, 4, 256), BF16),
            pltpu.VMEM((9, 16, 256), BF16),
            pltpu.VMEM((9, 3, 32, 32), BF16),
            pltpu.VMEM((9, 3, 32, 32), BF16),
            pltpu.VMEM((256, wide), BF16),
            pltpu.VMEM((wide, 512), BF16),
            pltpu.VMEM((9, 256, 256), BF16),
            pltpu.VMEM((9, 256, 256), BF16),
            pltpu.VMEM((4, 9, 3, 16, wide // 4), BF16),
            pltpu.VMEM((4, 2, 9, 3, 16, wide // 4), BF16),
            pltpu.VMEM((2, 9, 4, 2, 16, 2 * wide), BF16),
            pltpu.VMEM((152, 256), F32),
            pltpu.VMEM((128, 256), F32),
            pltpu.VMEM((64, 256), F32),
            pltpu.VMEM((devices // 4, 16, 256), BF16),
            pltpu.VMEM((half, 16, 256), BF16),
            pltpu.VMEM((2, 16 * half, 128), F32),
            pltpu.VMEM((2, 4 * half, 1152), BF16),
            pltpu.VMEM((4, 4 * half, wide // 2), F32),
            pltpu.VMEM((wide // 2 // tile, 16 * half, tile), F32),
            pltpu.VMEM((half, 16, wide // 2), BF16),
            pltpu.VMEM((half, 16, wide // 2), BF16),
            dma((9,)),
            dma((2,)),
            dma((9,)),
            dma((9,)),
            dma((2 * len(CHUNKS),)),
            dma((2 * len(CHUNKS),)),
            dma((len(CHUNKS),)),
            dma((len(CHUNKS),)),
            dma((len(CHUNKS),)),
            dma((len(CHUNKS),)),
            dma((half,)),
            dma((half,)),
            dma((half,)),
            dma((half,)),
        ],
        compiler_params=pltpu.CompilerParams(
            collective_id=0, has_side_effects=True, vmem_limit_bytes=56 * 1024 * 1024
        ),
    )(
        volume,
        w_first.reshape(9, 3, 32, 32),
        w_second.reshape(9, 3, 32, 32),
        w_lift,
        w_coarse.reshape(9, 3, 16, wide),
        w_up,
    )
    return result


def solution(mesh):
    return jax.shard_map(
        functools.partial(on_device, mesh.shape["grp"], mesh.shape["dev"]),
        mesh=mesh,
        in_specs=(P("grp", "dev", None), P(), P(), P(), P(None, None, None, "dev", None), P()),
        out_specs=P("grp", "dev", None),
        check_vma=False,
    )
```

```python
import functools

import jax
import jax.numpy as jnp
from jax import lax
from jax.experimental import pallas as pl
from jax.experimental.pallas import tpu as pltpu
from jax.sharding import PartitionSpec as P

F32 = jnp.float32
BF16 = jnp.bfloat16
MESH = pl.DeviceIdType.MESH
BANDS = [(zi, zo) for zo in range(4) for zi in range(4) if abs(zi - zo) <= 1]
CHUNKS = [(0, 3), (3, 5), (5, 7), (7, 8), (8, 9)]
GAPS = [(zi, zo) for zo in range(4) for zi in range(4) if abs(zi - zo) > 1]


def gelu(v):
    return 0.5 * v * (1.0 + lax.erf(v * 0.7071067811865476))


def dot(a, b):
    return jnp.dot(a, b, preferred_element_type=F32)


def iota(shape, dim):
    return lax.broadcasted_iota(jnp.int32, shape, dim)


def one_hot(mask):
    return jnp.where(mask, 1.0, 0.0).astype(BF16)


def band_weights(w_ref, t_ref):
    spread = one_hot((iota((32, 256), 1) & 31) == iota((32, 256), 0))
    lane_z = iota((32, 256), 1) >> 5

    def body(tap, carry):
        w0 = dot(w_ref[tap, 0], spread)
        w1 = dot(w_ref[tap, 1], spread)
        w2 = dot(w_ref[tap, 2], spread)
        for zi in range(8):
            rows = jnp.where(
                lane_z == zi,
                w1,
                jnp.where(lane_z == zi - 1, w2, jnp.where(lane_z == zi + 1, w0, 0.0)),
            )
            t_ref[tap, zi * 32 : zi * 32 + 32, :] = rows.astype(BF16)
        return carry

    lax.fori_loop(0, 9, body, 0)


def kernel(
    groups, devices,
    vol, w1, w2, wl, wc, wu,
    out,
    block_v, blocks, w1_v, w2_v, wl_v, wu_v, t1, t2, wq, raw, tc, wide, first, skip_p, send, recv, flat, cols, own_sums, sums, parts, shares,
    load_sem, twin_sem, halo_s, halo_r, raw_s, raw_r, fwd_s, fwd_r, side_s, side_r, a2a_s, a2a_r, rs_s, rs_r,
):
    g = lax.axis_index("grp")
    d = lax.axis_index("dev")
    ring = devices // 4
    half = devices // 2
    lanes = wl.shape[1]
    width = lanes // 2
    part = width // 2
    tile = min(128, width)
    core = lax.rem(d, 2)
    zh = lax.rem(lax.div(d, 2), 2)
    ry = lax.div(d, 4)
    zl = lax.rem(g, 4)
    edge = (zl == 0) | (zl == 3)

    def member(dy, other_core):
        to_core = 1 - core if other_core else core
        return (lax.rem(ry + dy + ring, ring) * 2 + zh) * 2 + to_core

    def neighbour(dx, dy):
        return lax.rem(g + dx + groups, groups), lax.rem(d + dy + devices, devices)

    def across(to_core):
        return g + 3 - 2 * zl, (ry * 2 + 1 - zh) * 2 + to_core

    xp = lax.rem(lax.div(g, 4), 2)
    aside = (g + 4 - 8 * xp, d)

    steps = [ring // 2]
    for k in range(ring // 2 - 1, 0, -1):
        steps += [k, -k]
    members = [(k, b) for k in steps for b in (0, 1)] + [(0, 1)]
    beside = [(dx, dy) for dx in (-1, 1) for dy in (-1, 1, 0)]
    around = [(0, -1), (0, 1)] + beside

    def exists(dx, dy):
        there = (d + dy >= 0) & (d + dy < devices)
        return there & (g + dx >= 0) & (g + dx < groups)

    barrier = pltpu.get_barrier_semaphore()
    first_load = pltpu.make_async_copy(vol, block_v, load_sem.at[0])
    first_load.start()
    sibling = 1 - 2 * core
    greeted = 0
    for dx, dy in around:
        wanted = exists(dx, dy)
        if dx == 0:
            wanted = wanted & (sibling != dy)
        greeted += wanted.astype(jnp.int32)

        @pl.when(wanted)
        def _():
            pl.semaphore_signal(
                barrier, inc=1, device_id=neighbour(dx, dy), device_id_type=MESH
            )

    partners = [across(0), across(1), aside] + [(g, member(*m)) for m in members]
    for p in partners:
        pl.semaphore_signal(barrier, inc=1, device_id=p, device_id_type=MESH)

    mine = 2 * zh + core
    loads = [
        pltpu.make_async_copy(src, dst, load_sem.at[i + 1])
        for i, (src, dst) in enumerate(
            [
                (w1, w1_v),
                (w2, w2_v),
                (wl, wl_v),
                (wu, wu_v),
            ]
        )
    ]
    quarters = [
        pltpu.make_async_copy(
            wc.at[:, :, :, q * part : q * part + part], wq.at[q], load_sem.at[5 + q]
        )
        for q in range(4)
    ]
    for c in quarters + loads:
        c.start()
    first_load.wait()
    blocks[4] = block_v[...].astype(F32).reshape(16, 256).astype(BF16)
    pl.semaphore_wait(barrier, greeted + len(partners))

    def cross(i, to_core):
        lo, hi = CHUNKS[i]
        return pltpu.make_async_remote_copy(
            src_ref=wq.at[2 * to_core + xp, lo:hi],
            dst_ref=raw.at[mine, xp, lo:hi],
            send_sem=raw_s.at[2 * i + to_core],
            recv_sem=raw_r.at[2 * i + core],
            device_id=across(to_core),
            device_id_type=MESH,
        )

    def block_copy(dx, dy, slot):
        return pltpu.make_async_remote_copy(
            src_ref=blocks.at[4],
            dst_ref=blocks.at[slot],
            send_sem=halo_s.at[slot],
            recv_sem=halo_r.at[slot],
            device_id=neighbour(dx, dy),
            device_id_type=MESH,
        )

    for dx, dy in around:

        @pl.when(exists(dx, dy))
        def _():
            block_copy(dx, dy, (1 - dx) * 3 + 1 - dy).start()

    for c in quarters:
        c.wait()

    @pl.when(edge)
    def _():
        for i in range(len(CHUNKS)):
            for to_core in range(2):
                cross(i, to_core).start()

    twin = pltpu.make_async_remote_copy(
        src_ref=wq.at[pl.ds(2 - 2 * core, 2)],
        dst_ref=raw.at[mine],
        send_sem=twin_sem.at[0],
        recv_sem=twin_sem.at[1],
        device_id=(g, member(0, 1)),
        device_id_type=MESH,
    )
    twin.start()

    foreign = 2 * (1 - zh)

    def onward(i, sideways):
        lo, hi = CHUNKS[i]
        here = raw.at[pl.ds(foreign, 2), xp, lo:hi]
        return pltpu.make_async_remote_copy(
            src_ref=here,
            dst_ref=here,
            send_sem=(side_s if sideways else fwd_s).at[i],
            recv_sem=(side_r if sideways else fwd_r).at[i],
            device_id=aside if sideways else (jnp.where(zl == 0, g + 1, g - 1), d),
            device_id_type=MESH,
        )

    def crossed(i, block):
        lo, hi = CHUNKS[i]
        there = raw.at[foreign + block, xp, lo:hi]
        return pltpu.make_async_remote_copy(
            src_ref=there,
            dst_ref=there,
            send_sem=raw_s.at[2 * i + block],
            recv_sem=raw_r.at[2 * i + block],
            device_id=across(block),
            device_id_type=MESH,
        )

    def pass_on(where):
        @pl.when(edge if where else jnp.logical_not(edge))
        def _():
            for i in range(len(CHUNKS)):
                if where:
                    crossed(i, 0).wait_recv()
                    crossed(i, 1).wait_recv()
                    onward(i, False).start()
                else:
                    onward(i, False).wait_recv()
                onward(i, True).start()

    def banded(z_half, block, h, source):
        for zi, zo in BANDS:
            at = pl.multiple_of(zo * width + h * part, part)
            tc[z_half, :, zi, block, :, pl.ds(at, part)] = source[:, zi - zo + 1]

    for zi, zo in GAPS:
        tc[:, :, zi, :, :, zo * width : zo * width + width] = jnp.zeros((2, 9, 2, 16, width), BF16)
    wide[144:152] = jnp.zeros((8, 256), F32)
    first[120:128] = jnp.zeros((8, 256), F32)
    loads[0].wait()
    band_weights(w1_v, t1)
    loads[1].wait()
    band_weights(w2_v, t2)
    for c in loads[2:]:
        c.wait()
    for h in range(2):
        banded(zh, core, h, wq.at[2 * core + h])

    row, col = iota((144, 144), 0), iota((144, 144), 1)
    slot = col >> 4
    sx = (slot >= 3).astype(jnp.int32) + (slot >= 6).astype(jnp.int32)
    sy = slot - 3 * sx
    fits = (sx * 4 + ((col >> 2) & 3)) * 12 + sy * 4 + (col & 3) == row
    gx, gy = g - 1 + sx, d - 1 + sy
    fits = fits & (gx >= 0) & (gx < groups) & (gy >= 0) & (gy < devices)
    place = one_hot(fits)

    for dx, dy in around:
        slot = (1 + dx) * 3 + 1 + dy

        @pl.when(exists(dx, dy))
        def _():
            block_copy(dx, dy, slot).wait_recv()

        @pl.when(jnp.logical_not(exists(dx, dy)))
        def _():
            blocks[slot] = jnp.zeros((16, 256), BF16)

    wide[0:144] = dot(place, blocks[...].reshape(144, 256))

    total = jnp.zeros((120, 256), F32)
    for tap in range(9):
        off = (tap // 3) * 12 + tap % 3
        total += dot(wide[off : off + 120].astype(BF16), t1[tap])
    rows = iota((120, 256), 0)
    rx = (rows * 171) >> 11
    fx, fy = 4 * g - 3 + rx, 4 * d - 3 + rows - 12 * rx
    inside = (fx >= 0) & (fx < 4 * groups) & (fy >= 0) & (fy < 4 * devices)
    act = gelu(total).astype(BF16).astype(F32)
    first[0:120] = jnp.where(inside, act, 0.0)

    total = jnp.zeros((96, 256), F32)
    for tap in range(9):
        off = (tap // 3) * 12 + tap % 3
        total += dot(first[off : off + 96].astype(BF16), t2[tap])
    skip = gelu(total).astype(BF16)

    row, col = iota((64, 96), 0), iota((64, 96), 1)
    ci, cj = (row >> 2) & 3, row & 3
    fits = (2 * ci + (row >> 5)) * 12 + 2 * cj + ((row >> 4) & 1) == col
    cx, cy = 2 * g - 1 + ci, 2 * d - 1 + cj
    fits = fits & (cx >= 0) & (cx < 2 * groups) & (cy >= 0) & (cy < 2 * devices)
    moved = dot(one_hot(fits), skip)
    skip_p[...] = moved
    stacked = jnp.concatenate(
        [
            jnp.concatenate(
                [moved[ab * 16 : ab * 16 + 16, k * 64 : k * 64 + 64] for ab in range(4)], axis=1
            )
            for k in range(4)
        ],
        axis=0,
    )
    lifted = gelu(dot(stacked.astype(BF16), wl_v[...]))
    for t in range(ring):
        send[t] = jnp.concatenate(
            [
                lifted[k * 16 : k * 16 + 16, t * 64 + h * 32 : t * 64 + h * 32 + 32]
                for h in range(2)
                for k in range(4)
            ],
            axis=1,
        ).astype(BF16)

    me = 2 * ry + core

    def spread(m):
        to_y = lax.rem(ry + m[0] + ring, ring)
        to = 2 * to_y + (1 - core if m[1] else core)
        return pltpu.make_async_remote_copy(
            src_ref=send.at[to_y],
            dst_ref=recv.at[me],
            send_sem=a2a_s.at[to],
            recv_sem=a2a_r.at[me],
            device_id=(g, member(*m)),
            device_id_type=MESH,
        )

    for m in members:
        spread(m).start()
    recv[me] = send[ry]
    twin.wait_recv()
    for h in range(2):
        banded(zh, 1 - core, h, raw.at[2 * zh + 1 - core, h])
    pass_on(True)
    pass_on(False)

    def arrive(off, carry):
        frm = lax.rem(me + off, half)
        pltpu.make_async_remote_copy(
            src_ref=send.at[0],
            dst_ref=recv.at[frm],
            send_sem=a2a_s.at[frm],
            recv_sem=a2a_r.at[frm],
            device_id=(g, d),
            device_id_type=MESH,
        ).wait_recv()
        return carry

    lax.fori_loop(1, half, arrive, 0)

    for lt in range(2):
        flat[lt] = recv[:, :, lt * 128 : lt * 128 + 128].astype(F32).reshape(16 * half, 128)
    for xx in range(4):
        for yb in range(4):
            for lt in range(2):
                piece = flat[lt, pl.ds(4 * xx + yb, half, stride=16), :].astype(BF16)
                for a in range(3):
                    for b in range(3):
                        ox, oy = xx - a, yb - b
                        if 0 <= ox < 2 and 0 <= oy < 2:
                            at, to = (2 * ox + oy) * half, (3 * a + b) * 128
                            cols[lt, at : at + half, to : to + 128] = piece

    def product(z_half, z):
        return dot(
            cols[z_half],
            tc[z_half, :, :, :, :, z * width : z * width + width].reshape(1152, width),
        )

    for z in range(4):
        own_sums[z] = product(zh, z)
    for block in range(2):
        banded(1 - zh, block, xp, raw.at[foreign + block, xp])

    for i in range(len(CHUNKS)):
        lo, hi = CHUNKS[i]
        there = raw.at[pl.ds(foreign, 2), 1 - xp, lo:hi]
        pltpu.make_async_remote_copy(
            src_ref=there,
            dst_ref=there,
            send_sem=side_s.at[i],
            recv_sem=side_r.at[i],
            device_id=aside,
            device_id_type=MESH,
        ).wait_recv()
    for block in range(2):
        banded(1 - zh, block, 1 - xp, raw.at[foreign + block, 1 - xp])

    for z in range(4):
        got = own_sums[z] + product(1 - zh, z)
        for q in range(4):
            for lt in range(width // tile):
                sums[lt, pl.ds(4 * z + q, half, stride=16), :] = got[
                    q * half : q * half + half, lt * tile : lt * tile + tile
                ]
    for lt in range(width // tile):
        parts[:, :, lt * tile : lt * tile + tile] = sums[lt].reshape(half, 16, tile).astype(BF16)

    def share(m):
        to = 2 * lax.rem(ry + m[0] + ring, ring) + (1 - core if m[1] else core)
        return pltpu.make_async_remote_copy(
            src_ref=parts.at[to],
            dst_ref=shares.at[me],
            send_sem=rs_s.at[to],
            recv_sem=rs_r.at[me],
            device_id=(g, member(*m)),
            device_id_type=MESH,
        )

    for m in members:
        share(m).start()
    shares[me] = parts[me]

    def share_arrive(off, carry):
        frm = lax.rem(me + off, half)
        pltpu.make_async_remote_copy(
            src_ref=parts.at[0],
            dst_ref=shares.at[frm],
            send_sem=rs_s.at[frm],
            recv_sem=rs_r.at[frm],
            device_id=(g, d),
            device_id_type=MESH,
        ).wait_recv()
        return carry

    lax.fori_loop(1, half, share_arrive, 0)

    halves = []
    for h in range(2):
        total = shares[h].astype(F32)
        for t in range(1, ring):
            total += shares[2 * t + h].astype(F32)
        halves.append(total)
    coarse = gelu(jnp.concatenate(halves, axis=1)).astype(BF16)
    upper = dot(coarse, wu_v[...])

    def expand(base):
        return jnp.concatenate(
            [
                jnp.concatenate(
                    [
                        upper[4 * k : 4 * k + 4, base + ab * 64 : base + ab * 64 + 64]
                        for k in range(4)
                    ],
                    axis=1,
                )
                for ab in range(4)
            ],
            axis=0,
        )

    gate, value = expand(0), expand(256)
    own = jnp.concatenate(
        [skip_p[ab * 16 + 4 * i + 1 : ab * 16 + 4 * i + 3] for ab in range(4) for i in (1, 2)], axis=0
    )
    mixed = (own * jax.nn.sigmoid(gate) + value).astype(BF16)
    row, col = iota((16, 16), 0), iota((16, 16), 1)
    fits = ((row >> 2) == 2 * ((col >> 1) & 1) + (col >> 3)) & (
        (row & 3) == 2 * (col & 1) + ((col >> 2) & 1)
    )
    out[...] = dot(one_hot(fits), mixed).reshape(4, 4, 256).astype(BF16)

    for dx, dy in around:

        @pl.when(exists(dx, dy))
        def _():
            block_copy(dx, dy, (1 - dx) * 3 + 1 - dy).wait_send()

    twin.wait_send()

    @pl.when(edge)
    def _():
        for i in range(len(CHUNKS)):
            for k in range(2):
                cross(i, k).wait_send()
            onward(i, False).wait_send()

    for i in range(len(CHUNKS)):
        onward(i, True).wait_send()

    for m in members:
        spread(m).wait_send()
        share(m).wait_send()


def on_device(groups, devices, volume, w_first, w_second, w_lift, w_coarse, w_up):
    half = devices // 2
    wide = w_up.shape[0]
    tile = min(128, wide // 2)
    in_hbm = pl.BlockSpec(memory_space=pltpu.HBM)
    dma = pltpu.SemaphoreType.DMA
    result = pl.pallas_call(
        functools.partial(kernel, groups, devices),
        out_shape=jax.ShapeDtypeStruct((4, 4, 256), BF16),
        in_specs=[pl.BlockSpec(memory_space=pl.ANY)] + [in_hbm] * 5,
        out_specs=pl.BlockSpec(memory_space=pltpu.VMEM),
        scratch_shapes=[
            pltpu.VMEM((4, 4, 256), BF16),
            pltpu.VMEM((9, 16, 256), BF16),
            pltpu.VMEM((9, 3, 32, 32), BF16),
            pltpu.VMEM((9, 3, 32, 32), BF16),
            pltpu.VMEM((256, wide), BF16),
            pltpu.VMEM((wide, 512), BF16),
            pltpu.VMEM((9, 256, 256), BF16),
            pltpu.VMEM((9, 256, 256), BF16),
            pltpu.VMEM((4, 9, 3, 16, wide // 4), BF16),
            pltpu.VMEM((4, 2, 9, 3, 16, wide // 4), BF16),
            pltpu.VMEM((2, 9, 4, 2, 16, 2 * wide), BF16),
            pltpu.VMEM((152, 256), F32),
            pltpu.VMEM((128, 256), F32),
            pltpu.VMEM((64, 256), F32),
            pltpu.VMEM((devices // 4, 16, 256), BF16),
            pltpu.VMEM((half, 16, 256), BF16),
            pltpu.VMEM((2, 16 * half, 128), F32),
            pltpu.VMEM((2, 4 * half, 1152), BF16),
            pltpu.VMEM((4, 4 * half, wide // 2), F32),
            pltpu.VMEM((wide // 2 // tile, 16 * half, tile), F32),
            pltpu.VMEM((half, 16, wide // 2), BF16),
            pltpu.VMEM((half, 16, wide // 2), BF16),
            dma((9,)),
            dma((2,)),
            dma((9,)),
            dma((9,)),
            dma((2 * len(CHUNKS),)),
            dma((2 * len(CHUNKS),)),
            dma((len(CHUNKS),)),
            dma((len(CHUNKS),)),
            dma((len(CHUNKS),)),
            dma((len(CHUNKS),)),
            dma((half,)),
            dma((half,)),
            dma((half,)),
            dma((half,)),
        ],
        compiler_params=pltpu.CompilerParams(
            collective_id=0, has_side_effects=True, vmem_limit_bytes=56 * 1024 * 1024
        ),
    )(
        volume,
        w_first.reshape(9, 3, 32, 32),
        w_second.reshape(9, 3, 32, 32),
        w_lift,
        w_coarse.reshape(9, 3, 16, wide),
        w_up,
    )
    return result


def solution(mesh):
    return jax.shard_map(
        functools.partial(on_device, mesh.shape["grp"], mesh.shape["dev"]),
        mesh=mesh,
        in_specs=(P("grp", "dev", None), P(), P(), P(), P(None, None, None, "dev", None), P()),
        out_specs=P("grp", "dev", None),
        check_vma=False,
    )
```

```python
import functools

import jax
import jax.numpy as jnp
from jax import lax
from jax.experimental import pallas as pl
from jax.experimental.pallas import tpu as pltpu
from jax.sharding import PartitionSpec as P

F32 = jnp.float32
BF16 = jnp.bfloat16
MESH = pl.DeviceIdType.MESH
BANDS = [(zi, zo) for zo in range(4) for zi in range(4) if abs(zi - zo) <= 1]
CHUNKS = [(0, 3), (3, 5), (5, 7), (7, 8), (8, 9)]
GAPS = [(zi, zo) for zo in range(4) for zi in range(4) if abs(zi - zo) > 1]


def gelu(v):
    return 0.5 * v * (1.0 + lax.erf(v * 0.7071067811865476))


def dot(a, b):
    return jnp.dot(a, b, preferred_element_type=F32)


def iota(shape, dim):
    return lax.broadcasted_iota(jnp.int32, shape, dim)


def one_hot(mask):
    return jnp.where(mask, 1.0, 0.0).astype(BF16)


def band_weights(w_ref, t_ref):
    spread = one_hot((iota((32, 256), 1) & 31) == iota((32, 256), 0))
    lane_z = iota((32, 256), 1) >> 5

    def body(tap, carry):
        w0 = dot(w_ref[tap, 0], spread)
        w1 = dot(w_ref[tap, 1], spread)
        w2 = dot(w_ref[tap, 2], spread)
        for zi in range(8):
            rows = jnp.where(
                lane_z == zi,
                w1,
                jnp.where(lane_z == zi - 1, w2, jnp.where(lane_z == zi + 1, w0, 0.0)),
            )
            t_ref[tap, zi * 32 : zi * 32 + 32, :] = rows.astype(BF16)
        return carry

    lax.fori_loop(0, 9, body, 0)


def kernel(
    groups, devices,
    vol, w1, w2, wl, wc, wu,
    out,
    block_v, blocks, w1_v, w2_v, wl_v, wu_v, t1, t2, wq, raw, tc, wide, first, skip_p, send, recv, flat, cols, own_sums, sums, parts, shares,
    load_sem, twin_sem, halo_s, halo_r, raw_s, raw_r, fwd_s, fwd_r, side_s, side_r, a2a_s, a2a_r, rs_s, rs_r,
):
    g = lax.axis_index("grp")
    d = lax.axis_index("dev")
    ring = devices // 4
    half = devices // 2
    lanes = wl.shape[1]
    width = lanes // 2
    part = width // 2
    tile = min(128, width)
    core = lax.rem(d, 2)
    zh = lax.rem(lax.div(d, 2), 2)
    ry = lax.div(d, 4)
    zl = lax.rem(g, 4)
    edge = (zl == 0) | (zl == 3)

    def member(dy, other_core):
        to_core = 1 - core if other_core else core
        return (lax.rem(ry + dy + ring, ring) * 2 + zh) * 2 + to_core

    def neighbour(dx, dy):
        return lax.rem(g + dx + groups, groups), lax.rem(d + dy + devices, devices)

    def across(to_core):
        return g + 3 - 2 * zl, (ry * 2 + 1 - zh) * 2 + to_core

    xp = lax.rem(lax.div(g, 4), 2)
    aside = (g + 4 - 8 * xp, d)

    steps = [ring // 2]
    for k in range(ring // 2 - 1, 0, -1):
        steps += [k, -k]
    members = [(k, b) for k in steps for b in (0, 1)] + [(0, 1)]
    beside = [(dx, dy) for dx in (-1, 1) for dy in (-1, 1, 0)]
    around = [(0, -1), (0, 1)] + beside

    def exists(dx, dy):
        there = (d + dy >= 0) & (d + dy < devices)
        return there & (g + dx >= 0) & (g + dx < groups)

    barrier = pltpu.get_barrier_semaphore()
    first_load = pltpu.make_async_copy(vol, block_v, load_sem.at[0])
    first_load.start()
    sibling = 1 - 2 * core
    greeted = 0
    for dx, dy in around:
        wanted = exists(dx, dy)
        if dx == 0:
            wanted = wanted & (sibling != dy)
        greeted += wanted.astype(jnp.int32)

        @pl.when(wanted)
        def _():
            pl.semaphore_signal(
                barrier, inc=1, device_id=neighbour(dx, dy), device_id_type=MESH
            )

    partners = [across(0), across(1), aside] + [(g, member(*m)) for m in members]
    for p in partners:
        pl.semaphore_signal(barrier, inc=1, device_id=p, device_id_type=MESH)

    mine = 2 * zh + core
    loads = [
        pltpu.make_async_copy(src, dst, load_sem.at[i + 1])
        for i, (src, dst) in enumerate(
            [
                (w1, w1_v),
                (w2, w2_v),
                (wl, wl_v),
                (wu, wu_v),
            ]
        )
    ]
    quarters = [
        pltpu.make_async_copy(
            wc.at[:, :, :, q * part : q * part + part], wq.at[q], load_sem.at[5 + q]
        )
        for q in range(4)
    ]
    for c in quarters + loads:
        c.start()
    first_load.wait()
    blocks[4] = block_v[...].astype(F32).reshape(16, 256).astype(BF16)
    pl.semaphore_wait(barrier, greeted + len(partners))

    def cross(i, to_core):
        lo, hi = CHUNKS[i]
        return pltpu.make_async_remote_copy(
            src_ref=wq.at[2 * to_core + xp, lo:hi],
            dst_ref=raw.at[mine, xp, lo:hi],
            send_sem=raw_s.at[2 * i + to_core],
            recv_sem=raw_r.at[2 * i + core],
            device_id=across(to_core),
            device_id_type=MESH,
        )

    def block_copy(dx, dy, slot):
        return pltpu.make_async_remote_copy(
            src_ref=blocks.at[4],
            dst_ref=blocks.at[slot],
            send_sem=halo_s.at[slot],
            recv_sem=halo_r.at[slot],
            device_id=neighbour(dx, dy),
            device_id_type=MESH,
        )

    for dx, dy in around:

        @pl.when(exists(dx, dy))
        def _():
            block_copy(dx, dy, (1 - dx) * 3 + 1 - dy).start()

    for c in quarters:
        c.wait()

    @pl.when(edge)
    def _():
        for i in range(len(CHUNKS)):
            for to_core in range(2):
                cross(i, to_core).start()

    twin = pltpu.make_async_remote_copy(
        src_ref=wq.at[pl.ds(2 - 2 * core, 2)],
        dst_ref=raw.at[mine],
        send_sem=twin_sem.at[0],
        recv_sem=twin_sem.at[1],
        device_id=(g, member(0, 1)),
        device_id_type=MESH,
    )
    twin.start()

    foreign = 2 * (1 - zh)

    def onward(i, sideways):
        lo, hi = CHUNKS[i]
        here = raw.at[pl.ds(foreign, 2), xp, lo:hi]
        return pltpu.make_async_remote_copy(
            src_ref=here,
            dst_ref=here,
            send_sem=(side_s if sideways else fwd_s).at[i],
            recv_sem=(side_r if sideways else fwd_r).at[i],
            device_id=aside if sideways else (jnp.where(zl == 0, g + 1, g - 1), d),
            device_id_type=MESH,
        )

    def crossed(i, block):
        lo, hi = CHUNKS[i]
        there = raw.at[foreign + block, xp, lo:hi]
        return pltpu.make_async_remote_copy(
            src_ref=there,
            dst_ref=there,
            send_sem=raw_s.at[2 * i + block],
            recv_sem=raw_r.at[2 * i + block],
            device_id=across(block),
            device_id_type=MESH,
        )

    def pass_on(where):
        @pl.when(edge if where else jnp.logical_not(edge))
        def _():
            for i in range(len(CHUNKS)):
                if where:
                    crossed(i, 0).wait_recv()
                    crossed(i, 1).wait_recv()
                    onward(i, False).start()
                else:
                    onward(i, False).wait_recv()
                onward(i, True).start()

    def banded(z_half, block, h, source):
        for zi, zo in BANDS:
            at = pl.multiple_of(zo * width + h * part, part)
            tc[z_half, :, zi, block, :, pl.ds(at, part)] = source[:, zi - zo + 1]

    for zi, zo in GAPS:
        tc[:, :, zi, :, :, zo * width : zo * width + width] = jnp.zeros((2, 9, 2, 16, width), BF16)
    wide[144:152] = jnp.zeros((8, 256), F32)
    first[120:128] = jnp.zeros((8, 256), F32)
    loads[0].wait()
    band_weights(w1_v, t1)
    loads[1].wait()
    band_weights(w2_v, t2)
    for c in loads[2:]:
        c.wait()
    for h in range(2):
        banded(zh, core, h, wq.at[2 * core + h])

    row, col = iota((144, 144), 0), iota((144, 144), 1)
    slot = col >> 4
    sx = (slot >= 3).astype(jnp.int32) + (slot >= 6).astype(jnp.int32)
    sy = slot - 3 * sx
    fits = (sx * 4 + ((col >> 2) & 3)) * 12 + sy * 4 + (col & 3) == row
    gx, gy = g - 1 + sx, d - 1 + sy
    fits = fits & (gx >= 0) & (gx < groups) & (gy >= 0) & (gy < devices)
    place = one_hot(fits)

    for dx, dy in around:
        slot = (1 + dx) * 3 + 1 + dy

        @pl.when(exists(dx, dy))
        def _():
            block_copy(dx, dy, slot).wait_recv()

        @pl.when(jnp.logical_not(exists(dx, dy)))
        def _():
            blocks[slot] = jnp.zeros((16, 256), BF16)

    wide[0:144] = dot(place, blocks[...].reshape(144, 256))

    total = jnp.zeros((120, 256), F32)
    for tap in range(9):
        off = (tap // 3) * 12 + tap % 3
        total += dot(wide[off : off + 120].astype(BF16), t1[tap])
    rows = iota((120, 256), 0)
    rx = (rows * 171) >> 11
    fx, fy = 4 * g - 3 + rx, 4 * d - 3 + rows - 12 * rx
    inside = (fx >= 0) & (fx < 4 * groups) & (fy >= 0) & (fy < 4 * devices)
    act = gelu(total).astype(BF16).astype(F32)
    first[0:120] = jnp.where(inside, act, 0.0)

    total = jnp.zeros((96, 256), F32)
    for tap in range(9):
        off = (tap // 3) * 12 + tap % 3
        total += dot(first[off : off + 96].astype(BF16), t2[tap])
    skip = gelu(total).astype(BF16)

    row, col = iota((64, 96), 0), iota((64, 96), 1)
    ci, cj = (row >> 2) & 3, row & 3
    fits = (2 * ci + (row >> 5)) * 12 + 2 * cj + ((row >> 4) & 1) == col
    cx, cy = 2 * g - 1 + ci, 2 * d - 1 + cj
    fits = fits & (cx >= 0) & (cx < 2 * groups) & (cy >= 0) & (cy < 2 * devices)
    moved = dot(one_hot(fits), skip)
    skip_p[...] = moved
    stacked = jnp.concatenate(
        [
            jnp.concatenate(
                [moved[ab * 16 : ab * 16 + 16, k * 64 : k * 64 + 64] for ab in range(4)], axis=1
            )
            for k in range(4)
        ],
        axis=0,
    )
    lifted = gelu(dot(stacked.astype(BF16), wl_v[...]))
    for t in range(ring):
        send[t] = jnp.concatenate(
            [
                lifted[k * 16 : k * 16 + 16, t * 64 + h * 32 : t * 64 + h * 32 + 32]
                for h in range(2)
                for k in range(4)
            ],
            axis=1,
        ).astype(BF16)

    me = 2 * ry + core

    def spread(m):
        to_y = lax.rem(ry + m[0] + ring, ring)
        to = 2 * to_y + (1 - core if m[1] else core)
        return pltpu.make_async_remote_copy(
            src_ref=send.at[to_y],
            dst_ref=recv.at[me],
            send_sem=a2a_s.at[to],
            recv_sem=a2a_r.at[me],
            device_id=(g, member(*m)),
            device_id_type=MESH,
        )

    for m in members:
        spread(m).start()
    recv[me] = send[ry]
    pass_on(True)
    pass_on(False)
    twin.wait_recv()
    for h in range(2):
        banded(zh, 1 - core, h, raw.at[2 * zh + 1 - core, h])

    def arrive(off, carry):
        frm = lax.rem(me + off, half)
        pltpu.make_async_remote_copy(
            src_ref=send.at[0],
            dst_ref=recv.at[frm],
            send_sem=a2a_s.at[frm],
            recv_sem=a2a_r.at[frm],
            device_id=(g, d),
            device_id_type=MESH,
        ).wait_recv()
        return carry

    lax.fori_loop(1, half, arrive, 0)

    for lt in range(2):
        flat[lt] = recv[:, :, lt * 128 : lt * 128 + 128].astype(F32).reshape(16 * half, 128)
    for xx in range(4):
        for yb in range(4):
            for lt in range(2):
                piece = flat[lt, pl.ds(4 * xx + yb, half, stride=16), :].astype(BF16)
                for a in range(3):
                    for b in range(3):
                        ox, oy = xx - a, yb - b
                        if 0 <= ox < 2 and 0 <= oy < 2:
                            at, to = (2 * ox + oy) * half, (3 * a + b) * 128
                            cols[lt, at : at + half, to : to + 128] = piece

    def product(z_half, z):
        return dot(
            cols[z_half],
            tc[z_half, :, :, :, :, z * width : z * width + width].reshape(1152, width),
        )

    for z in range(4):
        own_sums[z] = product(zh, z)
    for block in range(2):
        banded(1 - zh, block, xp, raw.at[foreign + block, xp])

    for i in range(len(CHUNKS)):
        lo, hi = CHUNKS[i]
        there = raw.at[pl.ds(foreign, 2), 1 - xp, lo:hi]
        pltpu.make_async_remote_copy(
            src_ref=there,
            dst_ref=there,
            send_sem=side_s.at[i],
            recv_sem=side_r.at[i],
            device_id=aside,
            device_id_type=MESH,
        ).wait_recv()
    for block in range(2):
        banded(1 - zh, block, 1 - xp, raw.at[foreign + block, 1 - xp])

    for z in range(4):
        got = own_sums[z] + product(1 - zh, z)
        for q in range(4):
            for lt in range(width // tile):
                sums[lt, pl.ds(4 * z + q, half, stride=16), :] = got[
                    q * half : q * half + half, lt * tile : lt * tile + tile
                ]
    for lt in range(width // tile):
        parts[:, :, lt * tile : lt * tile + tile] = sums[lt].reshape(half, 16, tile).astype(BF16)

    def share(m):
        to = 2 * lax.rem(ry + m[0] + ring, ring) + (1 - core if m[1] else core)
        return pltpu.make_async_remote_copy(
            src_ref=parts.at[to],
            dst_ref=shares.at[me],
            send_sem=rs_s.at[to],
            recv_sem=rs_r.at[me],
            device_id=(g, member(*m)),
            device_id_type=MESH,
        )

    for m in members:
        share(m).start()
    shares[me] = parts[me]

    def share_arrive(off, carry):
        frm = lax.rem(me + off, half)
        pltpu.make_async_remote_copy(
            src_ref=parts.at[0],
            dst_ref=shares.at[frm],
            send_sem=rs_s.at[frm],
            recv_sem=rs_r.at[frm],
            device_id=(g, d),
            device_id_type=MESH,
        ).wait_recv()
        return carry

    lax.fori_loop(1, half, share_arrive, 0)

    halves = []
    for h in range(2):
        total = shares[h].astype(F32)
        for t in range(1, ring):
            total += shares[2 * t + h].astype(F32)
        halves.append(total)
    coarse = gelu(jnp.concatenate(halves, axis=1)).astype(BF16)
    upper = dot(coarse, wu_v[...])

    def expand(base):
        return jnp.concatenate(
            [
                jnp.concatenate(
                    [
                        upper[4 * k : 4 * k + 4, base + ab * 64 : base + ab * 64 + 64]
                        for k in range(4)
                    ],
                    axis=1,
                )
                for ab in range(4)
            ],
            axis=0,
        )

    gate, value = expand(0), expand(256)
    own = jnp.concatenate(
        [skip_p[ab * 16 + 4 * i + 1 : ab * 16 + 4 * i + 3] for ab in range(4) for i in (1, 2)], axis=0
    )
    mixed = (own * jax.nn.sigmoid(gate) + value).astype(BF16)
    row, col = iota((16, 16), 0), iota((16, 16), 1)
    fits = ((row >> 2) == 2 * ((col >> 1) & 1) + (col >> 3)) & (
        (row & 3) == 2 * (col & 1) + ((col >> 2) & 1)
    )
    out[...] = dot(one_hot(fits), mixed).reshape(4, 4, 256).astype(BF16)

    for dx, dy in around:

        @pl.when(exists(dx, dy))
        def _():
            block_copy(dx, dy, (1 - dx) * 3 + 1 - dy).wait_send()

    twin.wait_send()

    @pl.when(edge)
    def _():
        for i in range(len(CHUNKS)):
            for k in range(2):
                cross(i, k).wait_send()
            onward(i, False).wait_send()

    for i in range(len(CHUNKS)):
        onward(i, True).wait_send()

    for m in members:
        spread(m).wait_send()
        share(m).wait_send()


def on_device(groups, devices, volume, w_first, w_second, w_lift, w_coarse, w_up):
    half = devices // 2
    wide = w_up.shape[0]
    tile = min(128, wide // 2)
    in_hbm = pl.BlockSpec(memory_space=pltpu.HBM)
    dma = pltpu.SemaphoreType.DMA
    result = pl.pallas_call(
        functools.partial(kernel, groups, devices),
        out_shape=jax.ShapeDtypeStruct((4, 4, 256), BF16),
        in_specs=[pl.BlockSpec(memory_space=pl.ANY)] + [in_hbm] * 5,
        out_specs=pl.BlockSpec(memory_space=pltpu.VMEM),
        scratch_shapes=[
            pltpu.VMEM((4, 4, 256), BF16),
            pltpu.VMEM((9, 16, 256), BF16),
            pltpu.VMEM((9, 3, 32, 32), BF16),
            pltpu.VMEM((9, 3, 32, 32), BF16),
            pltpu.VMEM((256, wide), BF16),
            pltpu.VMEM((wide, 512), BF16),
            pltpu.VMEM((9, 256, 256), BF16),
            pltpu.VMEM((9, 256, 256), BF16),
            pltpu.VMEM((4, 9, 3, 16, wide // 4), BF16),
            pltpu.VMEM((4, 2, 9, 3, 16, wide // 4), BF16),
            pltpu.VMEM((2, 9, 4, 2, 16, 2 * wide), BF16),
            pltpu.VMEM((152, 256), F32),
            pltpu.VMEM((128, 256), F32),
            pltpu.VMEM((64, 256), F32),
            pltpu.VMEM((devices // 4, 16, 256), BF16),
            pltpu.VMEM((half, 16, 256), BF16),
            pltpu.VMEM((2, 16 * half, 128), F32),
            pltpu.VMEM((2, 4 * half, 1152), BF16),
            pltpu.VMEM((4, 4 * half, wide // 2), F32),
            pltpu.VMEM((wide // 2 // tile, 16 * half, tile), F32),
            pltpu.VMEM((half, 16, wide // 2), BF16),
            pltpu.VMEM((half, 16, wide // 2), BF16),
            dma((9,)),
            dma((2,)),
            dma((9,)),
            dma((9,)),
            dma((2 * len(CHUNKS),)),
            dma((2 * len(CHUNKS),)),
            dma((len(CHUNKS),)),
            dma((len(CHUNKS),)),
            dma((len(CHUNKS),)),
            dma((len(CHUNKS),)),
            dma((half,)),
            dma((half,)),
            dma((half,)),
            dma((half,)),
        ],
        compiler_params=pltpu.CompilerParams(
            collective_id=0, has_side_effects=True, vmem_limit_bytes=56 * 1024 * 1024
        ),
    )(
        volume,
        w_first.reshape(9, 3, 32, 32),
        w_second.reshape(9, 3, 32, 32),
        w_lift,
        w_coarse.reshape(9, 3, 16, wide),
        w_up,
    )
    return result


def solution(mesh):
    return jax.shard_map(
        functools.partial(on_device, mesh.shape["grp"], mesh.shape["dev"]),
        mesh=mesh,
        in_specs=(P("grp", "dev", None), P(), P(), P(), P(None, None, None, "dev", None), P()),
        out_specs=P("grp", "dev", None),
        check_vma=False,
    )
```
